32 devices in a mesh: groups: 2 (over x), blk: 4 (over y, core), row: 4 (over z).
Axes of the slice: x: 2, y: 2, z: 4, core: 2. Of those that a mesh axis runs over, the one named last changes fastest.
Arguments:
- coords: float32 [3, 24576], P(None, ('groups', 'blk', 'row')), parts along dimension 1, may hold values from 0 to 1
- charges: float32 [24576], P(('groups', 'blk', 'row')), parts along dimension 0, may hold values from -1 to 1
- counts: int32 [32], P(('groups', 'blk', 'row')), parts along dimension 0, may hold values from 256 to 768, as said below
- send_slot: int32 [24576], P(('groups', 'blk', 'row')), parts along dimension 0, may hold values from 0 to 1023, as said below
- recv_index: int32 [16384], P(('groups', 'blk', 'row')), parts along dimension 0, may hold values from 0 to 1023, as said below
- wave_ints: int32 [3, 24576], P(None, 'blk'), may hold values from -36 to 36, as said below
Outputs:
- slot_forces: float32 [3, 24576], P(None, ('groups', 'blk', 'row')), parts along dimension 1
- atom_forces: float32 [3, 16384], P(None, ('groups', 'blk', 'row')), parts along dimension 1
The draws below stay inside these ranges and needn't reach their ends.
There are 2 independent parts, one for each index of `groups`. The reference program is written for one: setup_inputs(seed, part) draws one part's arguments, and reference() takes and returns one part's arrays. A program takes and returns all parts, laid end to end along the dimension named above; an argument that names none is the same for every part. Nothing has to cross between parts.
Inputs may be any that keep to these rules, and one draw needn't show every extreme that they name: The counts of one system sum to 8192; the largest is 768. `send_slot`: for a live slot the value is d * 64 + r: the ion goes to k-space device d as its r-th arrival from this owner. Live values of one owner are distinct, and the ranks r to one device are 0 up to the number sent there minus one. Every device receives exactly 512 ions; some owner sends exactly 64 to some device. Slots that are not live hold arbitrary values. `recv_index`: the 512 values of device d are distinct and are exactly the arrivals s * 64 + r sent to d. `wave_ints`: each column is (h, k, l) with |h|, |k| at most 12 and l nonzero.
All inputs are finite; a program needn't handle non-finite values.
Results may differ from the reference program's by a relative error of at most 0.00007.
Values sent between devices are 32-bit elements; how exact they have to be, the bound alone decides.
No kernel may reach another device: no remote copies, remote signals or barrier semaphores. Data moves between devices by JAX's collectives and lax.ppermute only.
A program may use at most 128 MiB of HBM per device.

```python
import math
import jax
import jax.numpy as jnp
from jax import lax

A_DEV = 512
K = 24576
HMAX = 12
LMAX = 36
PEERS = 16
SLOTS_DEV = 768
ION_SLOT_TOTAL = 12288
PAIR_CAP = 64


def balanced_loads(sub_key, half_load):
    pair_count = PEERS // 2
    key_swing, key_order = jax.random.split(sub_key)
    swing = jax.random.randint(key_swing, (pair_count,), -half_load, half_load + 1)
    swing = swing.at[0].set(half_load)
    loads = jnp.stack([half_load + swing, half_load - swing], axis=1).reshape(-1)
    order = jax.random.permutation(key_order, PEERS)
    return loads[order].astype(jnp.int32)


def routing_tables(key):
    base = jax.random.fold_in(key, 7)
    keys = jax.random.split(base, 5)
    half_load = A_DEV // (2 * PEERS)
    owner_load = balanced_loads(keys[0], half_load)
    shared_load = balanced_loads(keys[1], half_load)
    peer_ids = jnp.arange(PEERS, dtype=jnp.int32)
    shifted = (peer_ids[:, None] + peer_ids[None, :]) % PEERS
    sent = owner_load[:, None] + shared_load[shifted]
    counts = jnp.sum(sent, axis=1).astype(jnp.int32)
    flat_ids = jnp.arange(PEERS * PAIR_CAP, dtype=jnp.int32)
    ranks = flat_ids % PAIR_CAP
    partner = flat_ids // PAIR_CAP

    def owner_slots(sub_key, owner):
        usable = ranks < sent[owner, partner]
        scores = jnp.where(usable, jax.random.permutation(sub_key, PEERS * PAIR_CAP).astype(jnp.int32), PEERS * PAIR_CAP + flat_ids)
        return jnp.argsort(scores, stable=True)[:SLOTS_DEV].astype(jnp.int32)
    send_keys = jax.random.split(keys[2], PEERS)
    outbound_rows = jax.vmap(owner_slots)(send_keys, peer_ids)
    slot_ids = jnp.arange(SLOTS_DEV, dtype=jnp.int32)
    filler = jax.random.randint(keys[3], (PEERS, SLOTS_DEV), 0, PEERS * PAIR_CAP)
    send_slot = jnp.where(slot_ids[None, :] < counts[:, None], outbound_rows, filler).reshape(-1).astype(jnp.int32)

    def device_rows(sub_key, device):
        usable = ranks < sent[partner, device]
        scores = jnp.where(usable, jax.random.permutation(sub_key, PEERS * PAIR_CAP).astype(jnp.int32), PEERS * PAIR_CAP + flat_ids)
        return jnp.argsort(scores, stable=True)[:A_DEV].astype(jnp.int32)
    recv_keys = jax.random.split(keys[4], PEERS)
    recv_index = jax.vmap(device_rows)(recv_keys, peer_ids).reshape(-1).astype(jnp.int32)
    return (counts, send_slot, recv_index)


def draw_counts(key, part):
    return routing_tables(key)[0]


def draw_send_slot(key, part):
    return routing_tables(key)[1]


def draw_recv_index(key, part):
    return routing_tables(key)[2]


def draw_wave_ints(key, part):
    keys = jax.random.split(jax.random.fold_in(key, 11), 4)
    first = jax.random.randint(keys[0], (K,), -HMAX, HMAX + 1)
    second = jax.random.randint(keys[1], (K,), -HMAX, HMAX + 1)
    third = jax.random.randint(keys[2], (K,), 1, LMAX + 1)
    signs = 2 * jax.random.randint(keys[3], (K,), 0, 2) - 1
    triples = jnp.stack([first, second, third * signs]).astype(jnp.int32)
    triples = triples.at[:, 0].set(jnp.array([HMAX, -HMAX, LMAX], jnp.int32))
    triples = triples.at[:, 1].set(jnp.array([-HMAX, HMAX, -LMAX], jnp.int32))
    return triples


def block_levels(rng, shape, cuts, least, top_value):
    level, own = 1.0, jax.random.fold_in(rng, 6)
    for dim, blocks in cuts:
        steps = jnp.exp(jax.random.uniform(jax.random.fold_in(own, dim), (blocks,), jnp.float32, least / len(cuts), top_value / len(cuts)))
        level = level * jnp.repeat(steps, shape[dim] // blocks).reshape([-1 if axis == dim else 1 for axis in range(len(shape))])
    return level


def setup_inputs(seed: int = 0, part: int = 0) -> dict:
    key_list = jax.random.split(jax.random.key(seed), 7)
    own_keys = jax.random.split(jax.random.fold_in(key_list[6], part), 7)
    return {
        "coords": jnp.clip(1.0 * jax.random.uniform(own_keys[0], (3, ION_SLOT_TOTAL), jnp.float32) ** block_levels(own_keys[0], (3, ION_SLOT_TOTAL), ((1, 16),), -0.2, 0.2), 0.0, 1.0),
        "charges": jnp.clip(jax.random.uniform(own_keys[1], (ION_SLOT_TOTAL,), jnp.float32, -1.0, 1.0) * block_levels(own_keys[1], (ION_SLOT_TOTAL,), ((0, 16),), -0.4, 0.0), -1.0, 1.0),
        "counts": draw_counts(jax.random.fold_in(jax.random.fold_in(key_list[6], part), 71), part),
        "send_slot": draw_send_slot(jax.random.fold_in(jax.random.fold_in(key_list[6], part), 71), part),
        "recv_index": draw_recv_index(jax.random.fold_in(jax.random.fold_in(key_list[6], part), 71), part),
        "wave_ints": draw_wave_ints(jax.random.fold_in(key_list[6], 71), part),
    }


DOUBLE_PI = 2.0 * math.pi
EWALD_BETA = 30.0
BOX_Z = 3.0
FORCE_GAIN = 400.0

def phys_vectors(wave_float):
    return jnp.stack([DOUBLE_PI * wave_float[0], DOUBLE_PI * wave_float[1], DOUBLE_PI * wave_float[2] / BOX_Z])

def phase_angles(wave_float, frac):
    inner = wave_float[0][:, None] * frac[0][None, :] + wave_float[1][:, None] * frac[1][None, :]
    inner = inner + wave_float[2][:, None] * frac[2][None, :]
    return DOUBLE_PI * inner

def pull_sum(wave_float, cos_weighted, sin_weighted, frac):
    angles = phase_angles(wave_float, frac)
    coef = jnp.sin(angles) * cos_weighted[:, None] - jnp.cos(angles) * sin_weighted[:, None]
    wave_phys = phys_vectors(wave_float)
    return lax.optimization_barrier(jnp.sum(wave_phys[:, :, None] * coef[None, :, :], axis=1))

def reference(coords, charges, counts, send_slot, recv_index, wave_ints):
    devices = counts.shape[0]
    slots_dev = charges.shape[0] // devices
    atoms_dev = recv_index.shape[0] // devices
    pair_cap = 2 * atoms_dev // devices
    buf_width = devices * pair_cap
    slot_ids = jnp.arange(slots_dev, dtype=jnp.int32)
    is_live = slot_ids[None, :] < counts[:, None]
    source = jnp.arange(devices, dtype=jnp.int32)[:, None]
    target_slot = jnp.where(is_live, source * buf_width + send_slot.reshape(devices, slots_dev), devices * buf_width)
    target_slot = target_slot.reshape(-1).astype(jnp.int32)
    value_entries = jnp.concatenate([coords, charges[None, :]], axis=0)
    table = jnp.zeros((4, devices * buf_width), jnp.float32).at[:, target_slot].set(value_entries, mode='drop')
    dest = jnp.repeat(jnp.arange(devices, dtype=jnp.int32), atoms_dev)
    where_from = (recv_index // pair_cap * buf_width + dest * pair_cap + recv_index % pair_cap).astype(jnp.int32)
    atom_rows = table[:, where_from]
    n_total = atom_rows.shape[1]
    wave_float = wave_ints.astype(jnp.float32)
    k_block = 128
    k_blocks = wave_float.reshape(3, K // k_block, k_block).transpose(1, 0, 2)

    def block_sums(wave_part):
        angles = phase_angles(wave_part, atom_rows[:3])
        return (lax.optimization_barrier(jnp.sum(atom_rows[3][None, :] * jnp.cos(angles), axis=1)), lax.optimization_barrier(jnp.sum(atom_rows[3][None, :] * jnp.sin(angles), axis=1)))
    cos_sum, sin_sum = lax.map(block_sums, k_blocks)
    cos_sum = cos_sum.reshape(-1)
    sin_sum = sin_sum.reshape(-1)
    wave_phys = phys_vectors(wave_float)
    k_squared = lax.optimization_barrier(jnp.sum(wave_phys * wave_phys, axis=0))
    weight = jnp.exp(-k_squared / (4.0 * EWALD_BETA * EWALD_BETA)) / k_squared
    cos_weighted = weight * cos_sum
    sin_weighted = weight * sin_sum
    force_scale = FORCE_GAIN / math.sqrt(float(n_total * K))
    a_block = 1024
    atom_blocks = atom_rows.reshape(4, n_total // a_block, a_block).transpose(1, 0, 2)

    def force_of_block(block_rows):
        pull_total = pull_sum(wave_float, cos_weighted, sin_weighted, block_rows[:3])
        return force_scale * block_rows[3][None, :] * pull_total
    atom_forces = lax.map(force_of_block, atom_blocks).transpose(1, 0, 2).reshape(3, n_total)
    back = jnp.zeros((3, devices * buf_width), jnp.float32).at[:, where_from].set(atom_forces)
    picked = back[:, jnp.minimum(target_slot, devices * buf_width - 1)]
    slot_forces = jnp.where(is_live.reshape(-1)[None, :], picked, 0.0)
    return (slot_forces, atom_forces)
```

```python
import functools
import math

import jax
import jax.numpy as jnp
from jax import lax
from jax.experimental import pallas as pl
from jax.experimental.pallas import tpu as pltpu
from jax.sharding import PartitionSpec as P

DOUBLE_PI = 2.0 * math.pi
EWALD_BETA = 30.0
BOX_Z = 3.0
FORCE_GAIN = 400.0
SIN_POLY = (6.283185, -41.34159, 81.599945, -76.61447, 41.342884, -12.471244)
COS_POLY = (1.0, -19.739204, 64.93912, -85.45014, 60.16763, -25.9676, 6.5286584)

BASIS = 24
PAIR_ROWS = 600
GRID_ROWS = 640
HARM = 40
WEIGHT_LANE = 80
F32 = jnp.float32
BF16 = jnp.bfloat16
NT = (((1,), (1,)), ((), ()))
VMEM_BYTES = 40 * 1024 * 1024


def horner(coefs, v):
    total = jnp.full_like(v, coefs[-1])
    for coef in coefs[-2::-1]:
        total = total * v + coef
    return total


def first_harmonics(pos):
    harm = lax.broadcasted_iota(jnp.int32, (8, pos.shape[1]), 0).astype(F32) + 1.0
    turns = harm * pos
    turns = turns - jnp.floor(turns + 0.5)
    square = turns * turns
    return horner(COS_POLY, square), turns * horner(SIN_POLY, square)


def advance(first, by):
    cos_a, sin_a = first
    cos_b, sin_b = by[0][7:8], by[1][7:8]
    return cos_a * cos_b - sin_a * sin_b, sin_a * cos_b + cos_a * sin_b


def merge_last(cos_part, sin_part):
    low = lax.broadcasted_iota(jnp.int32, cos_part.shape, 0) < 4
    return jnp.where(low, cos_part, pltpu.roll(sin_part, 4, 0))


def short_basis(pos):
    first = first_harmonics(pos)
    second = advance(first, first)
    return [first[0], first[1], merge_last(*second)]


def short_slopes(basis):
    row = lax.broadcasted_iota(jnp.int32, basis[0].shape, 0)
    harm = row.astype(F32) + 1.0
    low = row < 4
    factor = jnp.where(low, -(harm + 8.0), harm + 4.0)
    return [-harm * basis[1], harm * basis[0], factor * pltpu.roll(basis[2], 4, 0)]


def long_basis(pos):
    first = first_harmonics(pos)
    second = advance(first, first)
    third = advance(first, second)
    fourth = advance(second, second)
    fifth = advance(first, fourth)
    parts = (first, second, third, fourth, fifth)
    return [p[0] for p in parts], [p[1] for p in parts]


def split_two(value):
    high = value.astype(BF16)
    return high, (value - high.astype(F32)).astype(BF16)


def prep_kernel(cap, coords_ref, charges_ref, counts_ref, send_ref, waves_ref, out_ref):
    slots = charges_ref.shape[1]
    half = slots // 2
    live = lax.broadcasted_iota(jnp.int32, (1, slots), 1) < counts_ref[0]
    charge = jnp.where(live, charges_ref[...], 0.0)
    send = jnp.where(live, send_ref[...], -1).astype(F32)
    out_ref[...] = jnp.zeros_like(out_ref)
    for part in range(2):
        lanes = slice(part * half, (part + 1) * half)
        out_ref[4 * part : 4 * part + 3, 0:half] = coords_ref[:, lanes]
        out_ref[4 * part + 3 : 4 * part + 4, 0:half] = charge[:, lanes]
    for piece in range(slots // 128):
        out_ref[piece : piece + 1, half : half + 128] = send[:, piece * 128 : (piece + 1) * 128]
    block = half + 128
    rows, width = wave_shape(waves_ref.shape[1])
    for row in range(rows):
        for comp in range(3):
            out_ref[row : row + 1, block + comp * width : block + (comp + 1) * width] = waves_ref[
                comp : comp + 1, row * width : (row + 1) * width
            ].astype(F32)


def wave_shape(k_local):
    rows = 8
    while k_local % (rows * 128):
        rows //= 2
    return rows, k_local // rows


def basis_row(index):
    size = jnp.abs(index)
    sign = jnp.where(index < 0.0, 1.0, 0.0)
    row = jnp.where(size <= 8.0, size - 1.0 + 8.0 * sign, size + 7.0 + 4.0 * sign)
    return jnp.where(size == 0.0, float(BASIS), row)


def basis_size(row):
    low = jnp.where(row < 8, row, row - 8) + 1
    high = jnp.where(row < 20, row - 16, row - 20) + 9
    return jnp.where(row < 16, low, jnp.where(row < BASIS, high, 0))


def weight_table():
    row = lax.broadcasted_iota(jnp.int32, (GRID_ROWS, 128), 0)
    lane = lax.broadcasted_iota(jnp.int32, (GRID_ROWS, 128), 1)
    paired = row < PAIR_ROWS
    row_x = jnp.where(paired, row // BASIS, jnp.minimum(row - PAIR_ROWS, BASIS))
    row_y = jnp.where(paired, row % BASIS, BASIS)
    phys_x = DOUBLE_PI * basis_size(row_x).astype(F32)
    phys_y = DOUBLE_PI * basis_size(row_y).astype(F32)
    phys_z = DOUBLE_PI * jnp.maximum(lane - (WEIGHT_LANE - 1), 1).astype(F32) / BOX_Z
    k_squared = phys_x * phys_x + phys_y * phys_y + phys_z * phys_z
    weight = jnp.exp(-k_squared / (4.0 * EWALD_BETA * EWALD_BETA)) / k_squared
    return jnp.where(lane >= WEIGHT_LANE, weight, 0.0)


def weights_kernel(rows, width, has_base, *refs):
    if has_base:
        base_ref, waves_ref, out_ref, ids_ref = refs
    else:
        waves_ref, out_ref, ids_ref = refs
    start = waves_ref.shape[1] - 3 * width
    wave_h = waves_ref[0:rows, start : start + width]
    wave_k = waves_ref[0:rows, start + width : start + 2 * width]
    wave_l = waves_ref[0:rows, start + 2 * width : start + 3 * width]
    flip = jnp.where(wave_l < 0.0, -1.0, 1.0)
    row_x = basis_row(wave_h * flip)
    row_y = basis_row(wave_k * flip)
    ids_ref[0] = jnp.where(row_y == float(BASIS), PAIR_ROWS + row_x, BASIS * row_x + row_y)
    ids_ref[1] = wave_l * flip + float(WEIGHT_LANE - 1)
    out_ref[...] = jnp.zeros_like(out_ref)
    row_iota = lax.broadcasted_iota(jnp.int32, (GRID_ROWS, width), 0).astype(F32)
    lane_iota = lax.broadcasted_iota(jnp.int32, (128, width), 0).astype(F32)

    def step(piece, carry):
        row_id = ids_ref[0, pl.ds(piece, 1), :]
        lane_id = ids_ref[1, pl.ds(piece, 1), :]
        row_hot = jnp.where(row_iota == row_id, 1.0, 0.0).astype(BF16)
        lane_hot = jnp.where(lane_iota == lane_id, 1.0, 0.0).astype(BF16)
        out_ref[...] += lax.dot_general(row_hot, lane_hot, NT, preferred_element_type=F32)
        return carry

    lax.fori_loop(0, rows, step, 0)
    total = out_ref[...] * weight_table()
    if has_base:
        total = total + base_ref[...]
    out_ref[...] = total


def sums_kernel(owners, first_owner, half, cap, row_count, base_ref, ions_ref, out_ref, arrive_ref, v_ref):
    block = half + 128
    slots = 2 * half
    per_pack = 64 // cap
    out_ref[...] = base_ref[...]
    device = lax.axis_index("blk") * row_count + lax.axis_index("row")
    hot_iota = lax.broadcasted_iota(jnp.int32, (64, slots), 0).astype(F32)

    def step(owner, carry):
        begin = pl.multiple_of(owner * block, 128)
        block_rows = ions_ref[:, pl.ds(begin, block)]

        def comp(index):
            return jnp.concatenate(
                [block_rows[index : index + 1, 0:half], block_rows[index + 4 : index + 5, 0:half]], axis=1
            )

        charge = comp(3)
        basis_x = [charge * rows for rows in short_basis(comp(0))]
        basis_y = jnp.concatenate(short_basis(comp(1)), axis=0)
        cos_z, sin_z = long_basis(comp(2))
        for row in range(0, BASIS, 2):
            pair = [basis_x[r // 8][r % 8 : r % 8 + 1] * basis_y for r in (row, row + 1)]
            high, low = split_two(jnp.concatenate(pair, axis=0))
            v_ref[row * BASIS : (row + 2) * BASIS] = high
            v_ref[GRID_ROWS + row * BASIS : GRID_ROWS + (row + 2) * BASIS] = low
        const_x = jnp.where(
            lax.broadcasted_iota(jnp.int32, (8, slots), 0) == 0, jnp.broadcast_to(charge, (8, slots)), 0.0
        )
        none = jnp.zeros((8, slots), F32)
        tail = jnp.concatenate([charge * basis_y] + basis_x + [const_x, none], axis=0)
        high, low = split_two(tail)
        v_ref[BASIS * BASIS : GRID_ROWS] = high
        v_ref[GRID_ROWS + BASIS * BASIS : 2 * GRID_ROWS] = low
        high, low = split_two(jnp.concatenate(cos_z + sin_z, axis=0))
        gap = jnp.zeros((128 - 2 * HARM, slots), BF16)
        table_z = jnp.concatenate([high, gap, low, gap], axis=0)
        part = lax.dot_general(v_ref[...], table_z, NT, preferred_element_type=F32)
        out_ref[...] += part[:GRID_ROWS, :128] + (part[:GRID_ROWS, 128:] + part[GRID_ROWS:, :128])

        send = jnp.concatenate([block_rows[p : p + 1, half:block] for p in range(slots // 128)], axis=1)
        place = lax.rem(first_owner + owner, per_pack) * cap
        hots = []
        for target in (device, device ^ row_count):
            rank = send - (target * cap).astype(F32)
            valid = jnp.logical_and(rank >= 0.0, rank < float(cap))
            key = jnp.where(valid, rank + place.astype(F32), -1.0)
            hots.append(jnp.where(hot_iota == key, 1.0, 0.0).astype(BF16))
        values = jnp.concatenate([comp(0), comp(1), comp(2), charge], axis=0)
        high = values.astype(BF16)
        rest = values - high.astype(F32)
        mid = rest.astype(BF16)
        low = (rest - mid.astype(F32)).astype(BF16)
        hot = jnp.concatenate(hots, axis=0)
        found = [lax.dot_general(v, hot, NT, preferred_element_type=F32) for v in (high, mid, low)]
        row = (found[0] + found[1]) + found[2]
        pack = owner // per_pack
        if per_pack == 1:
            arrive_ref[pack] = row
        else:
            arrive_ref[pack] = jnp.where(place == 0, row, arrive_ref[pack] + row)
        return carry

    lax.fori_loop(0, owners, step, 0)


def force_kernel(
    force_scale, half, mine_ref, other_ref, arrive_ref, arrived_ref, block_ref, key_ref, slot_ref, atom_ref, w_ref, z_ref
):
    slots = 2 * half
    atoms_dev = key_ref.shape[1]
    packs = arrive_ref.shape[0]
    lane = lax.broadcasted_iota(jnp.int32, (4, 128), 1)
    pieces = [jnp.where(lane < 64, arrive_ref[p], arrived_ref[p]) for p in range(packs)]
    pool = jnp.concatenate(pieces, axis=1)
    high = pool.astype(BF16)
    rest = pool - high.astype(F32)
    mid = rest.astype(BF16)
    low = (rest - mid.astype(F32)).astype(BF16)
    spot = lax.broadcasted_iota(jnp.int32, (packs * 128, atoms_dev), 0)
    hot = jnp.where(spot == key_ref[...], 1.0, 0.0).astype(BF16)
    found = [jnp.dot(v, hot, preferred_element_type=F32) for v in (high, mid, low)]
    routed = (found[0] + found[1]) + found[2]
    ions = jnp.concatenate([block_ref[0:4, 0:half], block_ref[4:8, 0:half], routed], axis=1)
    count = slots + atoms_dev
    basis_x = short_basis(ions[0:1])
    basis_y = short_basis(ions[1:2])
    cos_z, sin_z = long_basis(ions[2:3])
    table_z = jnp.concatenate(cos_z + sin_z, axis=0)
    harm = lax.broadcasted_iota(jnp.int32, (HARM, count), 0).astype(F32) + 1.0
    slope_z = jnp.concatenate(
        [-harm * jnp.concatenate(sin_z, axis=0), harm * jnp.concatenate(cos_z, axis=0)], axis=0
    )
    for spot_z, table in ((0, table_z), (count, slope_z)):
        high, low = split_two(table)
        z_ref[:, spot_z : spot_z + count] = jnp.concatenate(
            [high, low, high, jnp.zeros((256 - 6 * HARM, count), BF16)], axis=0
        )
    slope_x = short_slopes(basis_x)
    slope_y = short_slopes(basis_y)
    lane = lax.broadcasted_iota(jnp.int32, (8, 128), 1)
    is_cos = lane < HARM
    is_wave = lane < 2 * HARM
    low_rows = lax.broadcasted_iota(jnp.int32, (8, 128), 0) < 4

    def fields(row):
        tile = mine_ref[row : row + 8] + other_ref[row : row + 8]
        sums = jnp.where(is_wave, tile, 0.0)
        gain = jnp.where(is_cos, pltpu.roll(tile, 48, 1), jnp.where(is_wave, pltpu.roll(tile, 88, 1), 0.0))
        turned = jnp.where(
            is_cos, pltpu.roll(sums, 88, 1), jnp.where(is_wave, -pltpu.roll(sums, HARM, 1), 0.0)
        )
        return gain, sums, turned

    def swap(parts):
        return [parts[1], parts[0], pltpu.roll(parts[2], 4, 0)]

    def store(row, value):
        high, low = split_two(value)
        high = high.astype(F32)
        low = low.astype(F32)
        turned = pltpu.roll(high, 2 * HARM, 1)
        w_ref[row : row + 8, 0:128] = jnp.where(is_wave, high, turned)
        w_ref[row : row + 8, 128:256] = jnp.where(lane < 32, turned, pltpu.roll(low, 32, 1))

    def combine(x_rows, x_other):
        gain, sums, turned = x_rows
        swapped_gain, swapped_sums, swapped_turned = swap(gain), swap(sums), swap(turned)
        both = [a + b for a, b in zip(gain, swapped_gain)]
        odd = [a - b for a, b in zip(gain, swapped_gain)]
        if x_other is None:
            return [both[i] * sums[i] - odd[i] * swapped_turned[i] for i in range(3)]
        gain_o, sums_o, turned_o = x_other
        swapped_gain_o, swapped_sums_o = swap(gain_o), swap(sums_o)
        both_o = [a + b for a, b in zip(gain_o, swapped_gain_o)]
        odd_o = [a - b for a, b in zip(gain_o, swapped_gain_o)]
        return [
            (both[i] + both_o[i]) * sums[i]
            - (odd[i] + odd_o[i]) * swapped_turned[i]
            - (both[i] - both_o[i]) * turned_o[i]
            - (odd[i] - odd_o[i]) * swapped_sums_o[i]
            for i in range(3)
        ]

    def group(x):
        parts = [fields(BASIS * x + 8 * i) for i in range(3)]
        return [[p[j] for p in parts] for j in range(3)]

    pairs = [(x, x + 8) for x in range(8)] + [(x, x + 4) for x in range(16, 20)]
    for x, other in pairs:
        group_x, group_o = group(x), group(other)
        for i, value in enumerate(combine(group_x, group_o)):
            store(BASIS * x + 8 * i, value)
        for i, value in enumerate(combine(group_o, group_x)):
            store(BASIS * other + 8 * i, value)
    for i, value in enumerate(combine(group(BASIS), None)):
        store(BASIS * BASIS + 8 * i, value)
    last = [fields(PAIR_ROWS + 8 * i) for i in range(4)]
    gain, sums, turned = [[p[j] for p in last] for j in range(3)]
    gain_s, turned_s = swap(gain), swap(turned)
    for i in range(3):
        store(
            PAIR_ROWS + 8 * i,
            (gain[i] + gain_s[i]) * sums[i] - (gain[i] - gain_s[i]) * turned_s[i],
        )
    store(PAIR_ROWS + 24, gain[3] * sums[3])
    w_ref[PAIR_ROWS + 32 :] = jnp.zeros((GRID_ROWS - PAIR_ROWS - 32, 256), F32)
    weights = w_ref[...].astype(BF16)
    tile = 256
    for begin in range(0, count, tile):
        lanes = slice(begin, begin + tile)
        plain = jnp.dot(weights, z_ref[:, begin : begin + tile], preferred_element_type=F32)
        sloped = jnp.dot(weights, z_ref[:, count + begin : count + begin + tile], preferred_element_type=F32)
        sum_x = jnp.zeros((8, tile), F32)
        sum_y = jnp.zeros((8, tile), F32)
        sum_z = jnp.zeros((8, tile), F32)
        rows_y = [rows[:, lanes] for rows in basis_y]
        rows_dy = [rows[:, lanes] for rows in slope_y]
        for x in range(BASIS + 1):
            part_x = part_y = part_z = 0.0
            for i in range(3):
                row = BASIS * x + 8 * i
                part_x = part_x + rows_y[i] * plain[row : row + 8]
                part_y = part_y + rows_dy[i] * plain[row : row + 8]
                part_z = part_z + rows_y[i] * sloped[row : row + 8]
            if x < BASIS:
                basis = basis_x[x // 8][x % 8 : x % 8 + 1, lanes]
                sum_x = sum_x + slope_x[x // 8][x % 8 : x % 8 + 1, lanes] * part_x
                sum_y = sum_y + basis * part_y
                sum_z = sum_z + basis * part_z
            else:
                sum_y = sum_y + part_y
                sum_z = sum_z + part_z
        for i in range(3):
            row = PAIR_ROWS + 8 * i
            sum_x = sum_x + slope_x[i][:, lanes] * plain[row : row + 8]
            sum_z = sum_z + basis_x[i][:, lanes] * sloped[row : row + 8]
        sum_z = sum_z + sloped[PAIR_ROWS + 24 : PAIR_ROWS + 32]
        gain = (-DOUBLE_PI * force_scale) * ions[3:4, lanes]
        force = jnp.concatenate(
            [
                gain * jnp.sum(sum_x, axis=0, keepdims=True),
                gain * jnp.sum(sum_y, axis=0, keepdims=True),
                (gain / BOX_Z) * jnp.sum(sum_z, axis=0, keepdims=True),
            ],
            axis=0,
        )
        if begin < slots:
            slot_ref[:, begin : begin + tile] = force
        else:
            atom_ref[:, begin - slots : begin - slots + tile] = force


def params():
    return pltpu.CompilerParams(vmem_limit_bytes=VMEM_BYTES)


def whole(count):
    return [pl.BlockSpec(memory_space=pltpu.VMEM)] * count


def body(coords, charges, counts, send_slot, recv_index, wave_ints):
    slots = charges.shape[0]
    half = slots // 2
    block = half + 128
    atoms_dev = recv_index.shape[0]
    devices = lax.axis_size(("blk", "row"))
    blk_count = lax.axis_size("blk")
    row_count = lax.axis_size("row")
    k_local = wave_ints.shape[1]
    cap = 2 * atoms_dev // devices
    per_pack = 64 // cap
    wave_rows, wave_width = wave_shape(k_local)
    device = lax.axis_index(("blk", "row")).astype(jnp.int32)
    force_scale = FORCE_GAIN / math.sqrt(float(atoms_dev * devices * blk_count * k_local))

    with jax.named_scope("payload"):
        payload = pl.pallas_call(
            functools.partial(prep_kernel, cap),
            out_shape=jax.ShapeDtypeStruct((8, block + 3 * wave_width), F32),
            in_specs=whole(2) + [pl.BlockSpec(memory_space=pltpu.SMEM)] + whole(2),
            out_specs=pl.BlockSpec(memory_space=pltpu.VMEM),
            compiler_params=params(),
        )(coords, charges.reshape(1, slots), counts, send_slot.reshape(1, slots), wave_ints)

    def flip(value, axis, bit):
        size = lax.axis_size(axis)
        return lax.ppermute(value, axis, [(i, i ^ bit) for i in range(size)])

    def wave_weights(base, value, pieces):
        shape = jax.ShapeDtypeStruct((GRID_ROWS, 128), F32)
        args = (value,) if base is None else (base, value)
        return pl.pallas_call(
            functools.partial(weights_kernel, wave_rows, wave_width, base is not None),
            out_shape=shape,
            in_specs=whole(len(args)),
            out_specs=pl.BlockSpec(memory_space=pltpu.VMEM),
            scratch_shapes=[pltpu.VMEM((2, wave_rows, wave_width), F32)],
            compiler_params=params(),
            cost_estimate=pl.CostEstimate(flops=2 * GRID_ROWS * 128 * k_local, bytes_accessed=1 << 20, transcendentals=0),
        )(*args)

    bits = []
    table = wave_weights(None, payload, 1)
    waves = [payload[:, block:]]
    ions = payload[:, :block]
    bit = 2
    while bit < blk_count:
        with jax.named_scope("exchange_blk"):
            sent = jnp.concatenate([ions] + waves, axis=1)
            got = flip(sent, "blk", bit)
        width = ions.shape[1]
        ions = jnp.concatenate([ions, got[:, :width]], axis=1)
        fresh = [got[:, at : at + 3 * wave_width] for at in range(width, got.shape[1], 3 * wave_width)]
        for piece in fresh:
            table = wave_weights(table, piece, 1)
        waves = waves + fresh
        bits.append(row_count * bit)
        bit *= 2
    groups = [ions]
    bit = row_count // 2
    while bit >= 1:
        held = groups[0] if len(groups) == 1 else jnp.concatenate(groups, axis=1)
        with jax.named_scope("exchange_row"):
            groups = [held, flip(held, "row", bit)]
        bits.append(bit)
        bit //= 2

    source = (recv_index // cap) ^ device
    order = jnp.zeros_like(source)
    for place, distance in enumerate(bits):
        order = order | jnp.where((source & distance) != 0, 1 << place, 0)
    far = jnp.where((source & row_count) != 0, 64, 0)
    key = (order // per_pack) * 128 + far + (order % per_pack) * cap + recv_index % cap

    owners_half = devices // 2
    arrive_parts = []
    owner = 0
    for held in groups:
        count = held.shape[1] // block
        packs = max(1, count // per_pack)
        with jax.named_scope("structure_sums"):
            table, arrive = pl.pallas_call(
                functools.partial(sums_kernel, count, owner, half, cap, row_count),
                out_shape=(
                    jax.ShapeDtypeStruct((GRID_ROWS, 128), F32),
                    jax.ShapeDtypeStruct((packs, 4, 128), F32),
                ),
                in_specs=whole(2),
                out_specs=whole(2),
                scratch_shapes=[pltpu.VMEM((2 * GRID_ROWS, slots), BF16)],
                compiler_params=params(),
                cost_estimate=pl.CostEstimate(
                    flops=2 * count * slots * 256 * 2 * GRID_ROWS, bytes_accessed=1 << 20, transcendentals=0
                ),
            )(table, held)
        arrive_parts.append(arrive)
        owner += count
    arrive = jnp.concatenate(arrive_parts, axis=0)
    packs = arrive.shape[0]
    mine = jnp.concatenate([table, arrive.reshape(4 * packs, 128)], axis=0)
    with jax.named_scope("exchange_core"):
        other = flip(mine, "blk", 1)
    with jax.named_scope("forces"):
        return pl.pallas_call(
            functools.partial(force_kernel, force_scale, half),
            out_shape=(
                jax.ShapeDtypeStruct((3, slots), F32),
                jax.ShapeDtypeStruct((3, atoms_dev), F32),
            ),
            in_specs=whole(6),
            out_specs=tuple(whole(2)),
            scratch_shapes=[
                pltpu.VMEM((GRID_ROWS, 256), F32),
                pltpu.VMEM((256, 2 * (slots + atoms_dev)), BF16),
            ],
            compiler_params=params(),
        )(
            table,
            other[:GRID_ROWS],
            arrive,
            other[GRID_ROWS:].reshape(packs, 4, 128),
            payload[:, :block],
            key.reshape(1, atoms_dev),
        )


def solution(mesh):
    placed = (
        P(None, ("groups", "blk", "row")),
        P(("groups", "blk", "row")),
        P(("groups", "blk", "row")),
        P(("groups", "blk", "row")),
        P(("groups", "blk", "row")),
        P(None, "blk"),
    )
    return jax.shard_map(
        body,
        mesh=mesh,
        in_specs=placed,
        out_specs=(P(None, ("groups", "blk", "row")), P(None, ("groups", "blk", "row"))),
        check_vma=False,
    )
```

```python
import functools
import math

import jax
import jax.numpy as jnp
from jax import lax
from jax.experimental import pallas as pl
from jax.experimental.pallas import tpu as pltpu
from jax.sharding import PartitionSpec as P

DOUBLE_PI = 2.0 * math.pi
EWALD_BETA = 30.0
BOX_Z = 3.0
FORCE_GAIN = 400.0
SIN_POLY = (6.283185, -41.34159, 81.599945, -76.61447, 41.342884, -12.471244)
COS_POLY = (1.0, -19.739204, 64.93912, -85.45014, 60.16763, -25.9676, 6.5286584)

BASIS = 24
PAIR_ROWS = 600
GRID_ROWS = 640
HARM = 40
WEIGHT_LANE = 80
COUNT_PAIRS = 200
COUNT_ROWS = 240
F32 = jnp.float32
BF16 = jnp.bfloat16
NT = (((1,), (1,)), ((), ()))
VMEM_BYTES = 40 * 1024 * 1024


def horner(coefs, v):
    total = jnp.full_like(v, coefs[-1])
    for coef in coefs[-2::-1]:
        total = total * v + coef
    return total


def first_harmonics(pos):
    harm = lax.broadcasted_iota(jnp.int32, (8, pos.shape[1]), 0).astype(F32) + 1.0
    turns = harm * pos
    turns = turns - jnp.floor(turns + 0.5)
    square = turns * turns
    return horner(COS_POLY, square), turns * horner(SIN_POLY, square)


def advance(first, by):
    cos_a, sin_a = first
    cos_b, sin_b = by[0][7:8], by[1][7:8]
    return cos_a * cos_b - sin_a * sin_b, sin_a * cos_b + cos_a * sin_b


def merge_last(cos_part, sin_part):
    low = lax.broadcasted_iota(jnp.int32, cos_part.shape, 0) < 4
    return jnp.where(low, cos_part, pltpu.roll(sin_part, 4, 0))


def short_basis(pos):
    first = first_harmonics(pos)
    second = advance(first, first)
    return [first[0], first[1], merge_last(*second)]


def short_slopes(basis):
    row = lax.broadcasted_iota(jnp.int32, basis[0].shape, 0)
    harm = row.astype(F32) + 1.0
    low = row < 4
    factor = jnp.where(low, -(harm + 8.0), harm + 4.0)
    return [-harm * basis[1], harm * basis[0], factor * pltpu.roll(basis[2], 4, 0)]


def long_basis(pos):
    first = first_harmonics(pos)
    second = advance(first, first)
    third = advance(first, second)
    fourth = advance(second, second)
    fifth = advance(first, fourth)
    parts = (first, second, third, fourth, fifth)
    return [p[0] for p in parts], [p[1] for p in parts]


def split_two(value):
    high = value.astype(BF16)
    return high, (value - high.astype(F32)).astype(BF16)


def key_of_rows(recv, device, cap, row_count, bits):
    per_pack = 64 // cap
    source = (recv // cap) ^ device
    order = jnp.zeros_like(source)
    for place, distance in enumerate(bits):
        order = order | jnp.where((source & distance) != 0, 1 << place, 0)
    far = jnp.where((source & row_count) != 0, 64, 0)
    return (order // per_pack) * 128 + far + (order % per_pack) * cap + recv % cap


def prep_kernel(
    coords_hbm, charges_hbm, counts_hbm, send_hbm, waves_hbm, out_ref, waves_out_ref,
    coords_ref, charges_ref, counts_ref, send_ref, waves_ref, sems,
):
    copies = [
        pltpu.make_async_copy(source, target, sems.at[i])
        for i, (source, target) in enumerate(
            (
                (waves_hbm, waves_ref),
                (counts_hbm, counts_ref),
                (send_hbm, send_ref),
                (charges_hbm, charges_ref),
                (coords_hbm, coords_ref),
            )
        )
    ]
    for copy in copies:
        copy.start()
    slots = charges_ref.shape[0]
    half = slots // 2
    out_ref[:, 0 : half + 128] = jnp.zeros((8, half + 128), F32)
    for copy in copies:
        copy.wait()
    live = lax.broadcasted_iota(jnp.int32, (1, slots), 1) < counts_ref[0]
    charge = jnp.where(live, charges_ref[...].reshape(1, slots), 0.0)
    send = jnp.where(live, send_ref[...].reshape(1, slots), -1).astype(F32)
    for part in range(2):
        lanes = slice(part * half, (part + 1) * half)
        out_ref[4 * part : 4 * part + 3, 0:half] = coords_ref[:, lanes]
        out_ref[4 * part + 3 : 4 * part + 4, 0:half] = charge[:, lanes]
    for piece in range(slots // 128):
        out_ref[piece : piece + 1, half : half + 128] = send[:, piece * 128 : (piece + 1) * 128]
    rows, width = wave_shape(waves_ref.shape[1])
    for row in range(rows):
        for comp in range(3):
            waves_out_ref[row : row + 1, comp * width : (comp + 1) * width] = waves_ref[
                comp : comp + 1, row * width : (row + 1) * width
            ].astype(F32)


def wave_shape(k_local):
    rows = 8
    while k_local % (rows * 128):
        rows //= 2
    return rows, k_local // rows


def basis_row(index):
    size = jnp.abs(index)
    sign = jnp.where(index < 0.0, 1.0, 0.0)
    row = jnp.where(size <= 8.0, size - 1.0 + 8.0 * sign, size + 7.0 + 4.0 * sign)
    return jnp.where(size == 0.0, float(BASIS), row)


def compact_weights():
    row = lax.broadcasted_iota(jnp.int32, (COUNT_ROWS, 128), 0)
    lane = lax.broadcasted_iota(jnp.int32, (COUNT_ROWS, 128), 1)
    paired = row < COUNT_PAIRS
    row_x = jnp.where(paired, row // 8, jnp.minimum(row - COUNT_PAIRS, BASIS))
    part = jnp.where(lane < HARM, 0, jnp.where(lane < 2 * HARM, 1, 2))
    row_y = jnp.where(paired, row % 8 + 8 * part, BASIS)
    phys_x = DOUBLE_PI * basis_size(row_x).astype(F32)
    phys_y = DOUBLE_PI * basis_size(row_y).astype(F32)
    phys_z = DOUBLE_PI * (lane - HARM * part + 1).astype(F32) / BOX_Z
    k_squared = phys_x * phys_x + phys_y * phys_y + phys_z * phys_z
    return jnp.exp(-k_squared / (4.0 * EWALD_BETA * EWALD_BETA)) / k_squared


def basis_size(row):
    low = jnp.where(row < 8, row, row - 8) + 1
    high = jnp.where(row < 20, row - 16, row - 20) + 9
    return jnp.where(row < 16, low, jnp.where(row < BASIS, high, 0))


def count_waves(waves, rows, width):
    wave_h = waves[0:rows, 0:width]
    wave_k = waves[0:rows, width : 2 * width]
    wave_l = waves[0:rows, 2 * width : 3 * width]
    flip = jnp.where(wave_l < 0.0, -1.0, 1.0)
    row_x = basis_row(wave_h * flip)
    row_y = basis_row(wave_k * flip)
    part = jnp.where(row_y >= 16.0, 2.0, jnp.where(row_y >= 8.0, 1.0, 0.0))
    const = row_y == float(BASIS)
    part = jnp.where(const, 0.0, part)
    row_id = jnp.where(const, COUNT_PAIRS + row_x, 8.0 * (row_x - part) + row_y)
    lane_id = wave_l * flip + (HARM * part - 1.0)
    step = lax.broadcasted_iota(jnp.int32, (16, width), 0).astype(F32)
    steps = [(step + 16.0 * i).astype(BF16) for i in range(COUNT_ROWS // 16)]
    one = jnp.ones((16, width), BF16)
    none = jnp.zeros((16, width), BF16)
    total = None
    for piece in range(rows):
        rows_at = jnp.broadcast_to(row_id[piece : piece + 1], (16, width)).astype(BF16)
        lanes_at = jnp.broadcast_to(lane_id[piece : piece + 1], (16, width)).astype(BF16)
        row_hot = jnp.concatenate([jnp.where(rows_at == at, one, none) for at in steps], axis=0)
        lane_hot = jnp.concatenate([jnp.where(lanes_at == at, one, none) for at in steps[:8]], axis=0)
        part = lax.dot_general(row_hot, lane_hot, NT, preferred_element_type=F32)
        total = part if total is None else total + part
    return total


def spread_weights(counts, table_ref):
    weights = counts * compact_weights()
    lane = lax.broadcasted_iota(jnp.int32, (8, 128), 1)
    inside = jnp.logical_and(lane >= WEIGHT_LANE, lane < WEIGHT_LANE + HARM)
    for x in range(BASIS + 1):
        tile = weights[8 * x : 8 * x + 8]
        for part in range(3):
            row = BASIS * x + 8 * part
            moved = tile if part == 2 else pltpu.roll(tile, WEIGHT_LANE - HARM * part, 1)
            table_ref[row : row + 8] += jnp.where(inside, moved, 0.0)
    for block in range(4):
        moved = pltpu.roll(weights[COUNT_PAIRS + 8 * block : COUNT_PAIRS + 8 * block + 8], WEIGHT_LANE, 1)
        table_ref[PAIR_ROWS + 8 * block : PAIR_ROWS + 8 * block + 8] += jnp.where(inside, moved, 0.0)


def add_owner(block_rows, half, cap, place, pack, targets, table_ref, v_ref):
    block = half + 128
    slots = 2 * half

    def comp(index):
        return jnp.concatenate(
            [block_rows[index : index + 1, 0:half], block_rows[index + 4 : index + 5, 0:half]], axis=1
        )

    charge = comp(3)
    basis_x = [charge * rows for rows in short_basis(comp(0))]
    basis_y = jnp.concatenate(short_basis(comp(1)), axis=0)
    cos_z, sin_z = long_basis(comp(2))
    for row in range(0, BASIS, 2):
        pair = [basis_x[r // 8][r % 8 : r % 8 + 1] * basis_y for r in (row, row + 1)]
        high, low = split_two(jnp.concatenate(pair, axis=0))
        v_ref[row * BASIS : (row + 2) * BASIS] = high
        v_ref[GRID_ROWS + row * BASIS : GRID_ROWS + (row + 2) * BASIS] = low
    first_row = lax.broadcasted_iota(jnp.int32, (8, slots), 0) == 0
    const_x = jnp.where(first_row, jnp.broadcast_to(charge, (8, slots)), 0.0)
    none = jnp.zeros((8, slots), F32)
    tail = jnp.concatenate([charge * basis_y] + basis_x + [const_x, none], axis=0)
    high, low = split_two(tail)
    v_ref[BASIS * BASIS : GRID_ROWS] = high
    v_ref[GRID_ROWS + BASIS * BASIS : 2 * GRID_ROWS] = low
    high, low = split_two(jnp.concatenate(cos_z + sin_z, axis=0))
    gap = jnp.zeros((128 - 2 * HARM, slots), BF16)
    table_z = jnp.concatenate([high, gap, low, gap], axis=0)
    part = lax.dot_general(v_ref[...], table_z, NT, preferred_element_type=F32)
    table_ref[:GRID_ROWS] += part[:GRID_ROWS, :128] + (part[:GRID_ROWS, 128:] + part[GRID_ROWS:, :128])

    send = jnp.concatenate([block_rows[p : p + 1, half:block] for p in range(slots // 128)], axis=1)
    hot_iota = lax.broadcasted_iota(jnp.int32, (64, slots), 0).astype(F32)
    hots = []
    for target in targets:
        rank = send - (target * cap).astype(F32)
        valid = jnp.logical_and(rank >= 0.0, rank < float(cap))
        key = jnp.where(valid, rank + place, -1.0)
        hots.append(jnp.where(hot_iota == key, 1.0, 0.0).astype(BF16))
    values = jnp.concatenate([comp(0), comp(1), comp(2), charge, jnp.zeros((4, slots), F32)], axis=0)
    found = lax.dot_general(split_three(values), jnp.concatenate(hots, axis=0), NT, preferred_element_type=F32)
    row = GRID_ROWS + 8 * pack
    if not isinstance(row, int):
        row = pl.multiple_of(row, 8)
    table_ref[pl.ds(row, 8)] += (found[0:8] + found[8:16]) + found[16:24]


def split_three(value):
    high = value.astype(BF16).astype(F32)
    rest = value - high
    mid = rest.astype(BF16).astype(F32)
    return jnp.concatenate([high, mid, rest - mid], axis=0).astype(BF16)


def sums_kernel(plan, *refs):
    refs = list(refs)
    base_ref = refs.pop(0) if plan["has_base"] else None
    counts_ref = refs.pop(0) if plan["has_counts"] else None
    wave_refs = [refs.pop(0) for _ in plan["pieces"]]
    ion_refs = [refs.pop(0) for _ in plan["chunks"]]
    table_ref = refs.pop(0) if plan["table"] else None
    counts_out_ref = refs.pop(0) if plan["pieces"] else None
    v_ref = refs.pop(0)
    half, cap, row_count = plan["half"], plan["cap"], plan["row_count"]
    rows, width = plan["wave_shape"]
    block = half + 128
    per_pack = 64 // cap
    counts = None if counts_ref is None else counts_ref[...]
    for ref, pieces in zip(wave_refs, plan["pieces"]):
        for piece in range(pieces):
            part = count_waves(ref[:, 3 * width * piece : 3 * width * (piece + 1)], rows, width)
            counts = part if counts is None else counts + part
    if counts_out_ref is not None:
        counts_out_ref[...] = counts
    if table_ref is None:
        return
    device = lax.axis_index("blk") * row_count + lax.axis_index("row")
    targets = (device, device ^ row_count)
    table_ref[...] = jnp.zeros_like(table_ref) if base_ref is None else base_ref[...]
    if plan["spread"]:
        spread_weights(counts, table_ref)
    turn = 0
    for ref, (owners, first_owner) in zip(ion_refs, plan["chunks"]):
        if owners <= 4 and per_pack == 1:
            for owner in range(owners):
                add_owner(
                    ref[:, owner * block : (owner + 1) * block], half, cap, 0.0, first_owner + owner, targets,
                    table_ref, v_ref.at[turn % 2],
                )
                turn += 1
        else:

            def step(owner, carry, ref=ref, first_owner=first_owner):
                begin = pl.multiple_of(owner * block, 128)
                index = first_owner + owner
                add_owner(
                    ref[:, pl.ds(begin, block)], half, cap, (lax.rem(index, per_pack) * cap).astype(F32),
                    index // per_pack, targets, table_ref, v_ref.at[0],
                )
                return carry

            lax.fori_loop(0, owners, step, 0)


def store_bases(ions, basis_ref, z_ref):
    count = ions.shape[1]
    basis_x = short_basis(ions[0:1])
    basis_y = short_basis(ions[1:2])
    parts = basis_x + basis_y + short_slopes(basis_x) + short_slopes(basis_y)
    for i, part in enumerate(parts):
        basis_ref[8 * i : 8 * i + 8] = part
    cos_z, sin_z = (jnp.concatenate(rows, axis=0) for rows in long_basis(ions[2:3]))
    harm = lax.broadcasted_iota(jnp.int32, (HARM, count), 0).astype(F32) + 1.0
    plain = jnp.concatenate([cos_z, sin_z], axis=0)
    slope = jnp.concatenate([-harm * sin_z, harm * cos_z], axis=0)
    for i, table in enumerate((plain, slope)):
        high, low = split_two(table)
        z_ref[:, i * count : (i + 1) * count] = jnp.concatenate(
            [high, low, high, jnp.zeros((256 - 6 * HARM, count), BF16)], axis=0
        )


def own_kernel(half, cap, row_count, bits, data_ref, recv_ref, basis_ref, z_ref, hot_ref):
    store_bases(jnp.concatenate([data_ref[0:4, 0:half], data_ref[4:8, 0:half]], axis=1), basis_ref, z_ref)
    atoms_dev = recv_ref.shape[0]
    device = lax.axis_index("blk") * row_count + lax.axis_index("row")
    key = key_of_rows(recv_ref[...].reshape(1, atoms_dev), device, cap, row_count, bits)
    spot = lax.broadcasted_iota(jnp.int32, hot_ref.shape, 0)
    hot_ref[...] = jnp.where(spot == key, 1.0, 0.0).astype(BF16)


def force_kernel(
    force_scale, half, mine_ref, other_ref, data_ref, basis_ref, z_ref, hot_ref, slot_ref, atom_ref,
    w_ref, atom_basis_ref, atom_z_ref,
):
    slots = 2 * half
    atoms_dev = hot_ref.shape[1]
    packs = (mine_ref.shape[0] - GRID_ROWS) // 8
    lane = lax.broadcasted_iota(jnp.int32, (8, 128), 1)
    starts = [GRID_ROWS + 8 * p for p in range(packs)]
    pool = jnp.concatenate([jnp.where(lane < 64, mine_ref[r : r + 8], other_ref[r : r + 8]) for r in starts], axis=1)
    found = jnp.dot(split_three(pool), hot_ref[...], preferred_element_type=F32)
    routed = ((found[0:8] + found[8:16]) + found[16:24])[0:4]
    store_bases(routed, atom_basis_ref, atom_z_ref)
    lane = lax.broadcasted_iota(jnp.int32, (8, 128), 1)
    is_cos = lane < HARM
    is_wave = lane < 2 * HARM
    low_rows = lax.broadcasted_iota(jnp.int32, (8, 128), 0) < 4

    def fields(row):
        tile = mine_ref[row : row + 8] + other_ref[row : row + 8]
        sums = jnp.where(is_wave, tile, 0.0)
        gain = jnp.where(is_cos, pltpu.roll(tile, 48, 1), jnp.where(is_wave, pltpu.roll(tile, 88, 1), 0.0))
        turned = jnp.where(
            is_cos, pltpu.roll(sums, 88, 1), jnp.where(is_wave, -pltpu.roll(sums, HARM, 1), 0.0)
        )
        return gain, sums, turned

    def swap(parts):
        return [parts[1], parts[0], pltpu.roll(parts[2], 4, 0)]

    def store(row, value):
        high, low = split_two(value)
        high = high.astype(F32)
        low = low.astype(F32)
        turned = pltpu.roll(high, 2 * HARM, 1)
        w_ref[row : row + 8, 0:128] = jnp.where(is_wave, high, turned)
        w_ref[row : row + 8, 128:256] = jnp.where(lane < 32, turned, pltpu.roll(low, 32, 1))

    def combine(x_rows, x_other):
        gain, sums, turned = x_rows
        swapped_gain, swapped_sums, swapped_turned = swap(gain), swap(sums), swap(turned)
        both = [a + b for a, b in zip(gain, swapped_gain)]
        odd = [a - b for a, b in zip(gain, swapped_gain)]
        if x_other is None:
            return [both[i] * sums[i] - odd[i] * swapped_turned[i] for i in range(3)]
        gain_o, sums_o, turned_o = x_other
        swapped_gain_o, swapped_sums_o = swap(gain_o), swap(sums_o)
        both_o = [a + b for a, b in zip(gain_o, swapped_gain_o)]
        odd_o = [a - b for a, b in zip(gain_o, swapped_gain_o)]
        return [
            (both[i] + both_o[i]) * sums[i]
            - (odd[i] + odd_o[i]) * swapped_turned[i]
            - (both[i] - both_o[i]) * turned_o[i]
            - (odd[i] - odd_o[i]) * swapped_sums_o[i]
            for i in range(3)
        ]

    def group(x):
        parts = [fields(BASIS * x + 8 * i) for i in range(3)]
        return [[p[j] for p in parts] for j in range(3)]

    pairs = [(x, x + 8) for x in range(8)] + [(x, x + 4) for x in range(16, 20)]
    for x, other in pairs:
        group_x, group_o = group(x), group(other)
        for i, value in enumerate(combine(group_x, group_o)):
            store(BASIS * x + 8 * i, value)
        for i, value in enumerate(combine(group_o, group_x)):
            store(BASIS * other + 8 * i, value)
    for i, value in enumerate(combine(group(BASIS), None)):
        store(BASIS * BASIS + 8 * i, value)
    last = [fields(PAIR_ROWS + 8 * i) for i in range(4)]
    gain, sums, turned = [[p[j] for p in last] for j in range(3)]
    gain_s, turned_s = swap(gain), swap(turned)
    for i in range(3):
        store(
            PAIR_ROWS + 8 * i,
            (gain[i] + gain_s[i]) * sums[i] - (gain[i] - gain_s[i]) * turned_s[i],
        )
    store(PAIR_ROWS + 24, gain[3] * sums[3])
    w_ref[PAIR_ROWS + 32 :] = jnp.zeros((GRID_ROWS - PAIR_ROWS - 32, 256), F32)
    weights = w_ref[...].astype(BF16)
    tile = 256
    charge = jnp.concatenate([data_ref[3:4, 0:half], data_ref[7:8, 0:half]], axis=1)
    jobs = [(basis_ref, z_ref, charge, slot_ref, slots, begin) for begin in range(0, slots, tile)]
    jobs += [(atom_basis_ref, atom_z_ref, routed[3:4], atom_ref, atoms_dev, begin) for begin in range(0, atoms_dev, tile)]
    for rows_ref, table_ref, charges, out_ref, count, begin in jobs:
        lanes = slice(begin, begin + tile)
        plain = jnp.dot(weights, table_ref[:, begin : begin + tile], preferred_element_type=F32)
        sloped = jnp.dot(weights, table_ref[:, count + begin : count + begin + tile], preferred_element_type=F32)
        sum_x = jnp.zeros((8, tile), F32)
        sum_y = jnp.zeros((8, tile), F32)
        sum_z = jnp.zeros((8, tile), F32)
        rows_y = [rows_ref[24 + 8 * i : 32 + 8 * i, lanes] for i in range(3)]
        rows_dy = [rows_ref[72 + 8 * i : 80 + 8 * i, lanes] for i in range(3)]
        for x in range(BASIS + 1):
            part_x = part_y = part_z = 0.0
            for i in range(3):
                row = BASIS * x + 8 * i
                part_x = part_x + rows_y[i] * plain[row : row + 8]
                part_y = part_y + rows_dy[i] * plain[row : row + 8]
                part_z = part_z + rows_y[i] * sloped[row : row + 8]
            if x < BASIS:
                basis = rows_ref[x : x + 1, lanes]
                sum_x = sum_x + rows_ref[48 + x : 49 + x, lanes] * part_x
                sum_y = sum_y + basis * part_y
                sum_z = sum_z + basis * part_z
            else:
                sum_y = sum_y + part_y
                sum_z = sum_z + part_z
        for i in range(3):
            row = PAIR_ROWS + 8 * i
            sum_x = sum_x + rows_ref[48 + 8 * i : 56 + 8 * i, lanes] * plain[row : row + 8]
            sum_z = sum_z + rows_ref[8 * i : 8 * i + 8, lanes] * sloped[row : row + 8]
        sum_z = sum_z + sloped[PAIR_ROWS + 24 : PAIR_ROWS + 32]
        gain = (-DOUBLE_PI * force_scale) * charges[:, lanes]
        out_ref[:, lanes] = jnp.concatenate(
            [
                gain * jnp.sum(sum_x, axis=0, keepdims=True),
                gain * jnp.sum(sum_y, axis=0, keepdims=True),
                (gain / BOX_Z) * jnp.sum(sum_z, axis=0, keepdims=True),
            ],
            axis=0,
        )


def params():
    return pltpu.CompilerParams(vmem_limit_bytes=VMEM_BYTES)


def stay(value):
    return pltpu.with_memory_space_constraint(value, pltpu.HBM)


def whole(count):
    return [pl.BlockSpec(memory_space=pltpu.VMEM)] * count


def body(coords, charges, counts, send_slot, recv_index, wave_ints):
    slots = charges.shape[0]
    half = slots // 2
    block = half + 128
    atoms_dev = recv_index.shape[0]
    devices = lax.axis_size(("blk", "row"))
    blk_count = lax.axis_size("blk")
    row_count = lax.axis_size("row")
    k_local = wave_ints.shape[1]
    cap = 2 * atoms_dev // devices
    packs = max(1, devices // 2 * cap // 64)
    wave_rows, wave_width = wave_shape(k_local)
    force_scale = FORCE_GAIN / math.sqrt(float(atoms_dev * devices * blk_count * k_local))
    table_shape = jax.ShapeDtypeStruct((GRID_ROWS + 8 * packs, 128), F32)
    count_shape = jax.ShapeDtypeStruct((COUNT_ROWS, 128), F32)

    with jax.named_scope("payload"):
        own_ions, own_waves = pl.pallas_call(
            prep_kernel,
            out_shape=(
                jax.ShapeDtypeStruct((8, block), F32),
                jax.ShapeDtypeStruct((wave_rows, 3 * wave_width), F32),
            ),
            in_specs=[pl.BlockSpec(memory_space=pltpu.HBM)] * 5,
            out_specs=tuple(whole(2)),
            scratch_shapes=[
                pltpu.VMEM(coords.shape, F32),
                pltpu.VMEM(charges.shape, F32),
                pltpu.SMEM(counts.shape, jnp.int32),
                pltpu.VMEM(send_slot.shape, jnp.int32),
                pltpu.VMEM(wave_ints.shape, jnp.int32),
                pltpu.SemaphoreType.DMA((5,)),
            ],
            compiler_params=params(),
        )(stay(coords), stay(charges), counts, stay(send_slot), stay(wave_ints))

    def flip(value, axis, bit):
        size = lax.axis_size(axis)
        return lax.ppermute(value, axis, [(i, i ^ bit) for i in range(size)])

    def accumulate(table, counted, pieces, chunks, spread):
        plan = {
            "has_base": table is not None and bool(chunks),
            "has_counts": counted is not None and (bool(pieces) or spread),
            "pieces": [count for _, count in pieces],
            "chunks": [tuple(chunk[1:]) for chunk in chunks],
            "table": bool(chunks),
            "spread": spread,
            "half": half,
            "cap": cap,
            "row_count": row_count,
            "wave_shape": (wave_rows, wave_width),
        }
        args = [table] * plan["has_base"] + [counted] * plan["has_counts"]
        args += [piece[0] for piece in pieces] + [chunk[0] for chunk in chunks]
        shapes = (table_shape,) * plan["table"] + (count_shape,) * bool(pieces)
        flops = sum(2 * chunk[1] * slots * 256 * 2 * GRID_ROWS for chunk in chunks)
        flops += sum(2 * piece[1] * k_local * COUNT_ROWS * 256 for piece in pieces)
        with jax.named_scope("structure_sums"):
            out = pl.pallas_call(
                functools.partial(sums_kernel, plan),
                out_shape=shapes,
                in_specs=whole(len(args)),
                out_specs=tuple(whole(len(shapes))),
                scratch_shapes=[pltpu.VMEM((2, 2 * GRID_ROWS, slots), BF16)],
                compiler_params=params(),
                cost_estimate=pl.CostEstimate(flops=flops, bytes_accessed=1 << 20, transcendentals=0),
            )(*args)
        return (out[0] if chunks else table), (out[-1] if pieces else counted)

    steps = []
    bit = 2
    while bit < blk_count:
        steps.append(("blk", bit, row_count * bit))
        bit *= 2
    bit = row_count // 2
    while bit >= 1:
        steps.append(("row", bit, bit))
        bit //= 2
    bits = [distance for _, _, distance in steps]
    with jax.named_scope("own_ions"):
        basis, table_z, hot = pl.pallas_call(
            functools.partial(own_kernel, half, cap, row_count, bits),
            out_shape=(
                jax.ShapeDtypeStruct((96, slots), F32),
                jax.ShapeDtypeStruct((256, 2 * slots), BF16),
                jax.ShapeDtypeStruct((128 * packs, atoms_dev), BF16),
            ),
            in_specs=whole(2),
            out_specs=tuple(whole(3)),
            compiler_params=params(),
            cost_estimate=pl.CostEstimate(flops=1 << 30, bytes_accessed=1 << 20, transcendentals=0),
        )(own_ions, recv_index)
    table, counted = None, None
    ions, waves = [own_ions], [own_waves]
    pieces, chunks = [(own_waves, 1)], [(own_ions, 1, 0)]
    held, counted_sets, spread_done = 1, 0, False
    for axis, bit, _ in steps:
        with jax.named_scope("exchange_" + axis):
            got = flip(ions[0] if len(ions) == 1 else jnp.concatenate(ions, axis=1), axis, bit)
            if axis == "blk":
                got_waves = flip(waves[0] if len(waves) == 1 else jnp.concatenate(waves, axis=1), axis, bit)
        spread = not spread_done and counted_sets == max(1, blk_count // 2)
        table, counted = accumulate(table, counted, pieces, chunks, spread)
        got, table, counted = lax.optimization_barrier((got, table, counted))
        spread_done = spread_done or spread
        counted_sets += sum(piece[1] for piece in pieces)
        chunks = [(got, held, held)]
        pieces = []
        if axis == "blk":
            pieces = [(got_waves, held)]
            waves = waves + [got_waves]
        ions = ions + [got]
        held *= 2
    table, counted = accumulate(table, counted, pieces, chunks, not spread_done)
    with jax.named_scope("exchange_core"):
        other = flip(table, "blk", 1)
    with jax.named_scope("forces"):
        return pl.pallas_call(
            functools.partial(force_kernel, force_scale, half),
            out_shape=(
                jax.ShapeDtypeStruct((3, slots), F32),
                jax.ShapeDtypeStruct((3, atoms_dev), F32),
            ),
            in_specs=whole(6),
            out_specs=tuple(whole(2)),
            scratch_shapes=[
                pltpu.VMEM((GRID_ROWS, 256), F32),
                pltpu.VMEM((96, atoms_dev), F32),
                pltpu.VMEM((256, 2 * atoms_dev), BF16),
            ],
            compiler_params=params(),
        )(table, other, own_ions, basis, table_z, hot)


def solution(mesh):
    placed = (
        P(None, ("groups", "blk", "row")),
        P(("groups", "blk", "row")),
        P(("groups", "blk", "row")),
        P(("groups", "blk", "row")),
        P(("groups", "blk", "row")),
        P(None, "blk"),
    )
    return jax.shard_map(
        body,
        mesh=mesh,
        in_specs=placed,
        out_specs=(P(None, ("groups", "blk", "row")), P(None, ("groups", "blk", "row"))),
        check_vma=False,
    )
```

```python
import functools
import math

import jax
import jax.numpy as jnp
from jax import lax
from jax.experimental import pallas as pl
from jax.experimental.pallas import tpu as pltpu
from jax.sharding import PartitionSpec as P

DOUBLE_PI = 2.0 * math.pi
EWALD_BETA = 30.0
BOX_Z = 3.0
FORCE_GAIN = 400.0
SIN_POLY = (6.283185, -41.34159, 81.599945, -76.61447, 41.342884, -12.471244)
COS_POLY = (1.0, -19.739204, 64.93912, -85.45014, 60.16763, -25.9676, 6.5286584)

BASIS = 24
HARM = 40
STEMS = (((0, 0), (3, 0), (3, 1), (6, 0), (6, 1)), ((9, 0), (9, 1), (12, 0), (12, 1)))
SUM_ROWS = (144, 112)
ORDERS = (
    tuple((k, 0) for k in range(8)) + tuple((k, 1) for k in range(1, 8)),
    tuple((k, 0) for k in range(8, 13)) + tuple((k, 1) for k in range(8, 13)),
)
COUNT_ROWS = 240
COUNT_AT = (0, 136)
COUNT_LEN = (136, 96)
FORCE_ROWS = (384, 256)
FORCE_AT = (0, 384)
PART_AT = (0, 2 * SUM_ROWS[0])
ARRIVE_AT = PART_AT[1] + 2 * SUM_ROWS[1]
F32 = jnp.float32
BF16 = jnp.bfloat16
NT = (((1,), (1,)), ((), ()))
VMEM_BYTES = 40 * 1024 * 1024


def horner(coefs, v):
    total = jnp.full_like(v, coefs[-1])
    for coef in coefs[-2::-1]:
        total = total * v + coef
    return total


def harmonics(pos, first):
    harm = lax.broadcasted_iota(jnp.int32, (8, pos.shape[1]), 0).astype(F32) + float(first)
    turns = harm * pos
    turns = turns - jnp.floor(turns + 0.5)
    square = turns * turns
    return horner(COS_POLY, square), turns * horner(SIN_POLY, square)


def advance(first, by):
    cos_a, sin_a = first
    cos_b, sin_b = by
    return cos_a * cos_b - sin_a * sin_b, sin_a * cos_b + cos_a * sin_b


def row_of(pair, row):
    return pair[0][row : row + 1], pair[1][row : row + 1]


def merge_last(cos_part, sin_part):
    low = lax.broadcasted_iota(jnp.int32, cos_part.shape, 0) < 4
    return jnp.where(low, cos_part, pltpu.roll(sin_part, 4, 0))


def first_basis(pos):
    first = harmonics(pos, 1)
    second = advance(first, row_of(first, 7))
    return [first[0], first[1], merge_last(*second)]


def first_slopes(basis):
    row = lax.broadcasted_iota(jnp.int32, basis[0].shape, 0)
    harm = row.astype(F32) + 1.0
    low = row < 4
    factor = jnp.where(low, -(harm + 8.0), harm + 4.0)
    return [-harm * basis[1], harm * basis[0], factor * pltpu.roll(basis[2], 4, 0)]


def second_basis(pos):
    first = harmonics(pos, 0)
    fourth = row_of(first, 4)
    second = advance(first, advance(fourth, fourth))
    return [first[0], first[1], second[0], second[1]]


def second_slopes(basis):
    harm = lax.broadcasted_iota(jnp.int32, basis[0].shape, 0).astype(F32)
    high = harm + 8.0
    return [-harm * basis[1], harm * basis[0], -high * basis[3], high * basis[2]]


def second_row(basis, harmonic, sine):
    return basis[2 * (harmonic // 8) + sine][harmonic % 8 : harmonic % 8 + 1]


def third_basis(pos):
    first = harmonics(pos, 1)
    second = advance(first, row_of(first, 7))
    third = advance(first, row_of(second, 7))
    fourth = advance(second, row_of(second, 7))
    fifth = advance(first, row_of(fourth, 7))
    parts = (first, second, third, fourth, fifth)
    return jnp.concatenate([p[0] for p in parts] + [p[1] for p in parts], axis=0)


def split_two(value):
    high = value.astype(BF16)
    return high, (value - high.astype(F32)).astype(BF16)


def key_of_rows(recv, device, cap, row_count, bits):
    per_pack = 64 // cap
    source = (recv // cap) ^ device
    order = jnp.zeros_like(source)
    for place, distance in enumerate(bits):
        order = order | jnp.where((source & distance) != 0, 1 << place, 0)
    far = jnp.where((source & row_count) != 0, 64, 0)
    return (order // per_pack) * 128 + far + (order % per_pack) * cap + recv % cap


def prep_kernel(
    coords_hbm, charges_hbm, counts_hbm, send_hbm, waves_hbm, out_ref, waves_out_ref,
    coords_ref, charges_ref, counts_ref, send_ref, waves_ref, sems,
):
    copies = [
        pltpu.make_async_copy(source, target, sems.at[i])
        for i, (source, target) in enumerate(
            (
                (waves_hbm, waves_ref),
                (counts_hbm, counts_ref),
                (send_hbm, send_ref),
                (charges_hbm, charges_ref),
                (coords_hbm, coords_ref),
            )
        )
    ]
    for copy in copies:
        copy.start()
    slots = charges_ref.shape[0]
    half = slots // 2
    out_ref[:, 0 : half + 128] = jnp.zeros((8, half + 128), F32)
    for copy in copies:
        copy.wait()
    live = lax.broadcasted_iota(jnp.int32, (1, slots), 1) < counts_ref[0]
    charge = jnp.where(live, charges_ref[...].reshape(1, slots), 0.0)
    send = jnp.where(live, send_ref[...].reshape(1, slots), -1).astype(F32)
    for part in range(2):
        lanes = slice(part * half, (part + 1) * half)
        out_ref[4 * part : 4 * part + 3, 0:half] = coords_ref[:, lanes]
        out_ref[4 * part + 3 : 4 * part + 4, 0:half] = charge[:, lanes]
    for piece in range(slots // 128):
        out_ref[piece : piece + 1, half : half + 128] = send[:, piece * 128 : (piece + 1) * 128]
    rows, width = wave_shape(waves_ref.shape[1])
    for row in range(rows):
        for comp in range(3):
            waves_out_ref[row : row + 1, comp * width : (comp + 1) * width] = waves_ref[
                comp : comp + 1, row * width : (row + 1) * width
            ].astype(F32)


def wave_shape(k_local):
    rows = 8
    while k_local % (rows * 128):
        rows //= 2
    return rows, k_local // rows


def basis_row(index):
    size = jnp.abs(index)
    sign = jnp.where(index < 0.0, 1.0, 0.0)
    row = jnp.where(size <= 8.0, size - 1.0 + 8.0 * sign, size + 7.0 + 4.0 * sign)
    return jnp.where(size == 0.0, float(BASIS), row)


def basis_size(row):
    low = jnp.where(row < 8, row, row - 8) + 1
    high = jnp.where(row < 20, row - 16, row - 20) + 9
    return jnp.where(row < 16, low, jnp.where(row < BASIS, high, 0))


def dense_weights():
    row = lax.broadcasted_iota(jnp.int32, (COUNT_ROWS, 128), 0)
    lane = lax.broadcasted_iota(jnp.int32, (COUNT_ROWS, 128), 1)
    early = row < COUNT_AT[1]
    own = jnp.where(early, row, row - COUNT_AT[1])
    paired = own < jnp.where(early, COUNT_LEN[0] - 16, COUNT_LEN[1] - 16)
    group = own // 8
    size_y = jnp.where(early, jnp.where(group < 8, group, group - 7), 8 + jnp.where(group < 5, group, group - 5))
    size_y = jnp.where(paired, size_y, jnp.where(early, own % 8, 8 + own % 8))
    part = jnp.where(lane < HARM, 0, jnp.where(lane < 2 * HARM, 1, 2))
    size_x = jnp.where(paired, basis_size(own % 8 + 8 * part), 0)
    phys_x = DOUBLE_PI * size_x.astype(F32)
    phys_y = DOUBLE_PI * size_y.astype(F32)
    phys_z = DOUBLE_PI * (lane - HARM * part + 1).astype(F32) / BOX_Z
    k_squared = phys_x * phys_x + phys_y * phys_y + phys_z * phys_z
    return jnp.exp(-k_squared / (4.0 * EWALD_BETA * EWALD_BETA)) / k_squared


def count_waves(waves, rows, width):
    wave_h = waves[0:rows, 0:width]
    wave_k = waves[0:rows, width : 2 * width]
    wave_l = waves[0:rows, 2 * width : 3 * width]
    flip = jnp.where(wave_l < 0.0, -1.0, 1.0)
    row_x = basis_row(wave_h * flip)
    wave_k = wave_k * flip
    size_y = jnp.abs(wave_k)
    sine = jnp.where(wave_k < 0.0, 1.0, 0.0)
    const = row_x == float(BASIS)
    part = jnp.where(row_x >= 16.0, 2.0, jnp.where(row_x >= 8.0, 1.0, 0.0))
    part = jnp.where(const, 0.0, part)
    late = size_y >= 8.0
    group = jnp.where(late, size_y - 8.0 + 5.0 * sine, size_y + 7.0 * sine)
    paired_id = 8.0 * group + (row_x - 8.0 * part) + jnp.where(late, float(COUNT_AT[1]), 0.0)
    tail = jnp.where(late, size_y - 8.0 + float(COUNT_AT[1] + COUNT_LEN[1] - 16), size_y + float(COUNT_LEN[0] - 16))
    row_id = jnp.where(const, tail + 8.0 * sine, paired_id)
    lane_id = wave_l * flip + (HARM * part - 1.0)
    step = lax.broadcasted_iota(jnp.int32, (16, width), 0).astype(F32)
    steps = [(step + 16.0 * i).astype(BF16) for i in range(COUNT_ROWS // 16)]
    one = jnp.ones((16, width), BF16)
    none = jnp.zeros((16, width), BF16)
    total = None
    for piece in range(rows):
        rows_at = jnp.broadcast_to(row_id[piece : piece + 1], (16, width)).astype(BF16)
        lanes_at = jnp.broadcast_to(lane_id[piece : piece + 1], (16, width)).astype(BF16)
        row_hot = jnp.concatenate([jnp.where(rows_at == at, one, none) for at in steps], axis=0)
        lane_hot = jnp.concatenate([jnp.where(lanes_at == at, one, none) for at in steps[:8]], axis=0)
        found = lax.dot_general(row_hot, lane_hot, NT, preferred_element_type=F32)
        total = found if total is None else total + found
    return total


def owner_rows(block_rows, half):
    return [
        jnp.concatenate([block_rows[i : i + 1, 0:half], block_rows[i + 4 : i + 5, 0:half]], axis=1) for i in range(4)
    ]


def owner_tables(rows):
    pos_x, pos_y, pos_z, charge = rows
    basis_x = jnp.concatenate([charge * part for part in first_basis(pos_x)], axis=0)
    basis_y = second_basis(pos_y)
    third = third_basis(pos_z)
    lanes = jnp.concatenate([third, third * basis_y[0][1:2], third * basis_y[1][1:2]], axis=0)
    high, low = split_two(lanes)
    gap = jnp.zeros((256 - 6 * HARM, third.shape[1]), BF16)
    high = jnp.concatenate([high, gap], axis=0)
    low = jnp.concatenate([low, gap], axis=0)
    return basis_x, basis_y, high, low


def stem_rows(part, basis_y):
    return [second_row(basis_y, harmonic, sine) for harmonic, sine in STEMS[part]]


def add_sums(basis_x, basis_y, charge, high, low, table_ref, v_ref):
    slots = charge.shape[1]
    all_rows = sum(SUM_ROWS)
    at = 0
    for part in range(2):
        stems = stem_rows(part, basis_y)
        rows = [stem * basis_x for stem in stems] + [charge * rows for rows in basis_y[2 * part : 2 * part + 2]]
        fill = SUM_ROWS[part] - BASIS * len(stems) - 16
        if fill:
            rows.append(jnp.zeros((fill, slots), F32))
        rows = jnp.concatenate(rows, axis=0)
        for begin in range(0, SUM_ROWS[part], 16):
            v_high, v_low = split_two(rows[begin : begin + 16])
            v_ref[at : at + 16] = v_high
            v_ref[all_rows + at : all_rows + at + 16] = v_low
            at += 16
    both = lax.dot_general(v_ref[...], high, NT, preferred_element_type=F32)
    rest = lax.dot_general(v_ref[0:all_rows], low, NT, preferred_element_type=F32)
    total = (both[:all_rows] + both[all_rows:]) + rest
    at = 0
    for part in range(2):
        count, begin = SUM_ROWS[part], PART_AT[part]
        table_ref[begin : begin + count] += total[at : at + count, :128]
        table_ref[begin + count : begin + 2 * count] += total[at : at + count, 128:]
        at += count


def add_arrivals(block_rows, rows, half, cap, place, pack, targets, table_ref):
    block = half + 128
    slots = 2 * half
    send = jnp.concatenate([block_rows[p : p + 1, half:block] for p in range(slots // 128)], axis=1)
    step = lax.broadcasted_iota(jnp.int32, (16, slots), 0).astype(F32)
    one, none = jnp.ones((16, slots), BF16), jnp.zeros((16, slots), BF16)
    hots = []
    for target in targets:
        rank = send - (target * cap).astype(F32)
        valid = jnp.logical_and(rank >= 0.0, rank < float(cap))
        key = jnp.broadcast_to(jnp.where(valid, rank + place, -1.0), (16, slots)).astype(BF16)
        hots += [jnp.where(key == (step + 16.0 * i).astype(BF16), one, none) for i in range(4)]
    values = jnp.concatenate(rows + [jnp.zeros((4, slots), F32)], axis=0)
    found = lax.dot_general(split_three(values), jnp.concatenate(hots, axis=0), NT, preferred_element_type=F32)
    row = ARRIVE_AT + 8 * pack
    if not isinstance(row, int):
        row = pl.multiple_of(row, 8)
    table_ref[pl.ds(row, 8)] += (found[0:8] + found[8:16]) + found[16:24]


def split_three(value):
    high = value.astype(BF16).astype(F32)
    rest = value - high
    mid = rest.astype(BF16).astype(F32)
    return jnp.concatenate([high, mid, rest - mid], axis=0).astype(BF16)


def count_kernel(rows, width, waves_ref, out_ref):
    counts = count_waves(waves_ref, rows, width)
    for row in range(0, COUNT_ROWS, 8):
        out_ref[:, 16 * row : 16 * row + 128] = counts[row : row + 8]


def sums_kernel(plan, *refs):
    refs = list(refs)
    base_ref = refs.pop(0) if plan["has_base"] else None
    ion_refs = [refs.pop(0) for _ in plan["chunks"]]
    table_ref = refs.pop(0)
    v_ref = refs.pop(0)
    half, cap, row_count = plan["half"], plan["cap"], plan["row_count"]
    block = half + 128
    per_pack = 64 // cap
    device = lax.axis_index("blk") * row_count + lax.axis_index("row")
    targets = (device, device ^ row_count)
    table_ref[...] = jnp.zeros_like(table_ref) if base_ref is None else base_ref[...]

    def add(block_rows, place, pack, v_ref):
        ions = owner_rows(block_rows, half)
        basis_x, basis_y, high, low = owner_tables(ions)
        add_sums(basis_x, basis_y, ions[3], high, low, table_ref, v_ref)
        add_arrivals(block_rows, ions, half, cap, place, pack, targets, table_ref)

    turn = 0
    for ions_ref, (owners, first_owner) in zip(ion_refs, plan["chunks"]):
        if owners <= 4 and per_pack == 1:
            for owner in range(owners):
                ions = ions_ref[:, owner * block : (owner + 1) * block]
                add(ions, 0.0, first_owner + owner, v_ref.at[turn % 2])
                turn += 1
        else:

            def step(owner, carry, ions_ref=ions_ref, first_owner=first_owner):
                begin = pl.multiple_of(owner * block, 128)
                index = first_owner + owner
                place = (lax.rem(index, per_pack) * cap).astype(F32)
                add(ions_ref[:, pl.ds(begin, block)], place, index // per_pack, v_ref.at[0])
                return carry

            lax.fori_loop(0, owners, step, 0)


SLOPE_X, BASIS_Y, SLOPE_Y, BASIS_ROWS = 24, 48, 80, 112


def store_bases(ions, basis_ref, z_ref):
    count = ions.shape[1]
    basis_x = first_basis(ions[0:1])
    basis_y = second_basis(ions[1:2])
    parts = basis_x + first_slopes(basis_x) + basis_y + second_slopes(basis_y)
    for i, part in enumerate(parts):
        basis_ref[8 * i : 8 * i + 8] = part
    plain = third_basis(ions[2:3])
    harm = lax.broadcasted_iota(jnp.int32, (HARM, count), 0).astype(F32) + 1.0
    slope = jnp.concatenate([-harm * plain[HARM:], harm * plain[:HARM]], axis=0)
    for i, table in enumerate((plain, slope)):
        high, low = split_two(table)
        z_ref[:, i * count : (i + 1) * count] = jnp.concatenate(
            [high, low, high, jnp.zeros((256 - 6 * HARM, count), BF16)], axis=0
        )


def own_kernel(half, cap, row_count, bits, data_ref, recv_ref, basis_ref, z_ref, hot_ref, gain_ref):
    store_bases(jnp.concatenate([data_ref[0:4, 0:half], data_ref[4:8, 0:half]], axis=1), basis_ref, z_ref)
    atoms_dev = recv_ref.shape[0]
    device = lax.axis_index("blk") * row_count + lax.axis_index("row")
    key = key_of_rows(recv_ref[...].reshape(1, atoms_dev), device, cap, row_count, bits)
    spot = lax.broadcasted_iota(jnp.int32, hot_ref.shape, 0)
    hot_ref[...] = jnp.where(spot == key, 1.0, 0.0).astype(BF16)
    gain_ref[...] = dense_weights()


def swap(parts):
    return [parts[1], parts[0], pltpu.roll(parts[2], 4, 0)]


def combine(own, other):
    gain, sums, turned = own
    gain_s, sums_s, turned_s = swap(gain), swap(sums), swap(turned)
    both = [a + b for a, b in zip(gain, gain_s)]
    odd = [a - b for a, b in zip(gain, gain_s)]
    if other is None:
        return [both[i] * sums[i] - odd[i] * turned_s[i] for i in range(3)]
    gain_o, sums_o, turned_o = other
    gain_os, sums_os = swap(gain_o), swap(sums_o)
    both_o = [a + b for a, b in zip(gain_o, gain_os)]
    odd_o = [a - b for a, b in zip(gain_o, gain_os)]
    return [
        (both[i] + both_o[i]) * sums[i]
        - (odd[i] + odd_o[i]) * turned_s[i]
        - (both[i] - both_o[i]) * turned_o[i]
        - (odd[i] - odd_o[i]) * sums_os[i]
        for i in range(3)
    ]


def weighted_sums(part, mine_ref, other_ref, count_refs, gain_ref, w_ref):
    lane = lax.broadcasted_iota(jnp.int32, (8, 128), 1)
    is_cos = lane < HARM
    is_wave = lane < 2 * HARM
    count = SUM_ROWS[part]

    def both(row):
        row = PART_AT[part] + row
        return mine_ref[row : row + 8] + other_ref[row : row + 8]

    def blocks(row):
        near, far = both(row), both(count + row)
        middle = jnp.where(lane < 48, pltpu.roll(near, 48, 1), pltpu.roll(far, 48, 1))
        return [jnp.where(is_wave, value, 0.0) for value in (near, middle, pltpu.roll(far, 96, 1))]

    def turn(sums):
        return jnp.where(is_cos, pltpu.roll(sums, 88, 1), -pltpu.roll(sums, HARM, 1))

    def harmonics_of(stem):
        found = {}
        for harmonic, _ in STEMS[part]:
            if harmonic == 0:
                plain, cos_1, sin_1 = stem[(0, 0)]
                found.update({(0, 0): plain, (1, 0): cos_1, (1, 1): sin_1})
                continue
            cos, sin = stem[(harmonic, 0)], stem[(harmonic, 1)]
            found[(harmonic, 0)], found[(harmonic, 1)] = cos[0], sin[0]
            found[(harmonic - 1, 0)] = cos[1] + sin[2]
            found[(harmonic - 1, 1)] = sin[1] - cos[2]
            found[(harmonic + 1, 0)] = cos[1] - sin[2]
            found[(harmonic + 1, 1)] = sin[1] + cos[2]
        return found

    def gains(row):
        at = COUNT_AT[part] + row
        lanes = slice(16 * at, 16 * at + 128)
        tile = (count_refs[0][:, lanes] + count_refs[1][:, lanes]) * gain_ref[at : at + 8]
        back, far = pltpu.roll(tile, 88, 1), pltpu.roll(tile, 48, 1)
        pairs = ((tile, pltpu.roll(tile, HARM, 1)), (back, tile), (far, back))
        return [jnp.where(is_cos, a, jnp.where(is_wave, b, 0.0)) for a, b in pairs]

    def store(row, value):
        high, low = split_two(value)
        high = high.astype(F32)
        low = low.astype(F32)
        turned = pltpu.roll(high, 2 * HARM, 1)
        row = FORCE_AT[part] + row
        w_ref[row : row + 8, 0:128] = jnp.where(is_wave, high, turned)
        w_ref[row : row + 8, 128:256] = jnp.where(lane < 32, turned, pltpu.roll(low, 32, 1))

    by_block = [
        harmonics_of({stem: blocks(BASIS * i + 8 * x) for i, stem in enumerate(STEMS[part])}) for x in range(3)
    ]
    order = ORDERS[part]
    groups = {}
    for i, name in enumerate(order):
        sums = [by_block[x][name] for x in range(3)]
        groups[name] = (gains(8 * i), sums, [turn(value) for value in sums])
    for i, (harmonic, sine) in enumerate(order):
        other = None if harmonic == 0 else groups[(harmonic, 1 - sine)]
        for x, value in enumerate(combine(groups[(harmonic, sine)], other)):
            store(BASIS * i + 8 * x, value)
    tails = [blocks(BASIS * len(STEMS[part]) + 8 * sine) for sine in range(2)]
    found = harmonics_of({(h, sine): [b[h % 8 : h % 8 + 1] for b in tails[sine]] for h, sine in STEMS[part]})
    index = lax.broadcasted_iota(jnp.int32, (8, 128), 0)
    kinds = []
    for sine in range(2):
        rows = jnp.zeros((8, 128), F32)
        for harmonic, kind in order:
            if kind == sine:
                rows = jnp.where(index == harmonic % 8, found[(harmonic, kind)], rows)
        at = COUNT_LEN[part] - 16 + 8 * sine
        kinds.append((gains(at)[0], rows, turn(rows)))
    at = BASIS * len(order)
    for sine in range(2):
        (gain, sums, _), (gain_o, _, turned_o) = kinds[sine], kinds[1 - sine]
        store(at + 8 * sine, (gain + gain_o) * sums - (gain - gain_o) * turned_o)
    if at + 16 < FORCE_ROWS[part]:
        fill = FORCE_ROWS[part] - at - 16
        w_ref[FORCE_AT[part] + at + 16 : FORCE_AT[part] + FORCE_ROWS[part]] = jnp.zeros((fill, 256), F32)


def pull(weights, basis_ref, z_ref, count, begin, tile):
    lanes = slice(begin, begin + tile)
    plain = jnp.dot(weights, z_ref[:, begin : begin + tile], preferred_element_type=F32)
    sloped = jnp.dot(weights, z_ref[:, count + begin : count + begin + tile], preferred_element_type=F32)
    zero = jnp.zeros((8, tile), F32)
    even, slope, third = [zero] * 3, [zero] * 3, [zero] * 3
    sum_y = sum_z = zero
    for part in range(2):
        for place, (harmonic, sine) in enumerate(ORDERS[part]):
            at = 16 * (harmonic // 8) + 8 * sine + harmonic % 8
            basis = basis_ref[BASIS_Y + at : BASIS_Y + at + 1, lanes]
            basis_slope = basis_ref[SLOPE_Y + at : SLOPE_Y + at + 1, lanes]
            for i in range(3):
                row = FORCE_AT[part] + BASIS * place + 8 * i
                plain_rows, sloped_rows = plain[row : row + 8], sloped[row : row + 8]
                if harmonic == 0:
                    even[i] = even[i] + plain_rows
                    third[i] = third[i] + sloped_rows
                else:
                    even[i] = even[i] + basis * plain_rows
                    slope[i] = slope[i] + basis_slope * plain_rows
                    third[i] = third[i] + basis * sloped_rows
        for sine in range(2):
            row = FORCE_AT[part] + BASIS * len(ORDERS[part]) + 8 * sine
            at = 16 * part + 8 * sine
            sum_y = sum_y + basis_ref[SLOPE_Y + at : SLOPE_Y + at + 8, lanes] * plain[row : row + 8]
            sum_z = sum_z + basis_ref[BASIS_Y + at : BASIS_Y + at + 8, lanes] * sloped[row : row + 8]
    sum_x = zero
    for i in range(3):
        rows_x = basis_ref[8 * i : 8 * i + 8, lanes]
        sum_x = sum_x + basis_ref[SLOPE_X + 8 * i : SLOPE_X + 8 * i + 8, lanes] * even[i]
        sum_y = sum_y + rows_x * slope[i]
        sum_z = sum_z + rows_x * third[i]
    return [jnp.sum(value, axis=0, keepdims=True) for value in (sum_x, sum_y, sum_z)]


TILE = 256


def force_kernel(
    force_scale, half, mine_ref, other_ref, count_ref, other_count_ref, data_ref, basis_ref, z_ref, hot_ref, gain_ref,
    slot_ref, atom_ref, w_ref, atom_basis_ref, atom_z_ref,
):
    packs = hot_ref.shape[0] // 128
    lane = lax.broadcasted_iota(jnp.int32, (8, 128), 1)
    starts = [ARRIVE_AT + 8 * p for p in range(packs)]
    pool = jnp.concatenate([jnp.where(lane < 64, mine_ref[r : r + 8], other_ref[r : r + 8]) for r in starts], axis=1)
    found = jnp.dot(split_three(pool), hot_ref[...], preferred_element_type=F32)
    routed = ((found[0:8] + found[8:16]) + found[16:24])[0:4]
    for part in range(2):
        weighted_sums(part, mine_ref, other_ref, (count_ref, other_count_ref), gain_ref, w_ref)
    weights = w_ref[...].astype(BF16)
    store_bases(routed, atom_basis_ref, atom_z_ref)
    charge = jnp.concatenate([data_ref[3:4, 0:half], data_ref[7:8, 0:half]], axis=1)
    jobs = ((basis_ref, z_ref, charge, slot_ref), (atom_basis_ref, atom_z_ref, routed[3:4], atom_ref))
    for rows_ref, table_ref, charges, out_ref in jobs:
        count = out_ref.shape[1]
        for begin in range(0, count, TILE):
            lanes = slice(begin, begin + TILE)
            gain = (-DOUBLE_PI * force_scale) * charges[:, lanes]
            gains = (gain, gain, gain / BOX_Z)
            found = pull(weights, rows_ref, table_ref, count, begin, TILE)
            out_ref[:, lanes] = jnp.concatenate([gains[i] * found[i] for i in range(3)], axis=0)


def params():
    return pltpu.CompilerParams(vmem_limit_bytes=VMEM_BYTES)


def stay(value):
    return pltpu.with_memory_space_constraint(value, pltpu.HBM)


def whole(count):
    return [pl.BlockSpec(memory_space=pltpu.VMEM)] * count


def body(coords, charges, counts, send_slot, recv_index, wave_ints):
    slots = charges.shape[0]
    half = slots // 2
    block = half + 128
    atoms_dev = recv_index.shape[0]
    devices = lax.axis_size(("blk", "row"))
    blk_count = lax.axis_size("blk")
    row_count = lax.axis_size("row")
    k_local = wave_ints.shape[1]
    cap = 2 * atoms_dev // devices
    packs = max(1, devices // 2 * cap // 64)
    wave_rows, wave_width = wave_shape(k_local)
    force_scale = FORCE_GAIN / math.sqrt(float(atoms_dev * devices * blk_count * k_local))
    table_shape = jax.ShapeDtypeStruct((ARRIVE_AT + 8 * packs, 128), F32)
    count_shape = jax.ShapeDtypeStruct((8, 16 * COUNT_ROWS), F32)

    with jax.named_scope("payload"):
        own_ions, own_waves = pl.pallas_call(
            prep_kernel,
            out_shape=(
                jax.ShapeDtypeStruct((8, block), F32),
                jax.ShapeDtypeStruct((wave_rows, 3 * wave_width), F32),
            ),
            in_specs=[pl.BlockSpec(memory_space=pltpu.HBM)] * 5,
            out_specs=tuple(whole(2)),
            scratch_shapes=[
                pltpu.VMEM(coords.shape, F32),
                pltpu.VMEM(charges.shape, F32),
                pltpu.SMEM(counts.shape, jnp.int32),
                pltpu.VMEM(send_slot.shape, jnp.int32),
                pltpu.VMEM(wave_ints.shape, jnp.int32),
                pltpu.SemaphoreType.DMA((5,)),
            ],
            compiler_params=params(),
        )(stay(coords), stay(charges), counts, stay(send_slot), stay(wave_ints))

    def flip(value, blk_bit, row_bit):
        if not row_bit:
            return lax.ppermute(value, "blk", [(i, i ^ blk_bit) for i in range(blk_count)])
        if not blk_bit:
            return lax.ppermute(value, "row", [(i, i ^ row_bit) for i in range(row_count)])
        distance = row_count * blk_bit + row_bit
        return lax.ppermute(value, ("blk", "row"), [(i, i ^ distance) for i in range(devices)])

    def joined(values):
        return values[0] if len(values) == 1 else jnp.concatenate(values, axis=1)

    def accumulate(table, chunks):
        plan = {
            "has_base": table is not None,
            "chunks": [chunk[1:] for chunk in chunks],
            "half": half,
            "cap": cap,
            "row_count": row_count,
        }
        args = [table] * plan["has_base"] + [chunk[0] for chunk in chunks]
        flops = 2 * sum(chunk[1] for chunk in chunks) * slots * 256 * 720
        with jax.named_scope("structure_sums"):
            return pl.pallas_call(
                functools.partial(sums_kernel, plan),
                out_shape=table_shape,
                in_specs=whole(len(args)),
                out_specs=whole(1)[0],
                scratch_shapes=[pltpu.VMEM((2, 2 * sum(SUM_ROWS), slots), BF16)],
                compiler_params=params(),
                cost_estimate=pl.CostEstimate(flops=flops, bytes_accessed=1 << 20, transcendentals=0),
            )(*args)

    steps = []
    bit = row_count // 2
    while bit >= 2:
        steps.append((0, bit))
        bit //= 2
    bit = 4
    while bit < blk_count:
        steps.append((bit, 0))
        bit *= 2
    bits = [row_count * blk_bit + row_bit for blk_bit, row_bit in steps] + [2 * row_count, 1]
    table, counted = None, None
    ions, held, chunks = [own_ions], 1, [(own_ions, 1, 0)]
    for blk_bit, row_bit in steps:
        with jax.named_scope("exchange_ions"):
            got = flip(joined(ions), blk_bit, row_bit)
        if blk_bit:
            with jax.named_scope("exchange_counts"):
                counted = counted + flip(counted, blk_bit, 0)
        if counted is None:
            with jax.named_scope("counts"):
                counted = pl.pallas_call(
                    functools.partial(count_kernel, wave_rows, wave_width),
                    out_shape=count_shape,
                    in_specs=whole(1),
                    out_specs=whole(1)[0],
                    compiler_params=params(),
                    cost_estimate=pl.CostEstimate(
                        flops=2 * k_local * COUNT_ROWS * 128, bytes_accessed=1 << 20, transcendentals=0
                    ),
                )(own_waves)
            got, counted = lax.optimization_barrier((got, counted))
        else:
            table, chunks = accumulate(table, chunks), []
            got, table = lax.optimization_barrier((got, table))
        chunks = chunks + [(got, held, held)]
        ions = ions + [got]
        held *= 2
    with jax.named_scope("exchange_ions"):
        sent = joined(ions)
        across = flip(jnp.concatenate([sent, counted], axis=1), 2, 0)
        along = flip(sent, 0, 1)
        corner = flip(sent, 2, 1)
    table = accumulate(table, chunks)
    table = accumulate(table, [(along, held, 2 * held)])
    table, across = lax.optimization_barrier((table, across))
    counted = counted + across[:, held * block :]
    with jax.named_scope("exchange_core"):
        other_counted = flip(counted, 1, 0)
    table = accumulate(table, [(across, held, held)])
    corner, table, counted = lax.optimization_barrier((corner, table, counted))
    table = accumulate(table, [(corner, held, 3 * held)])
    with jax.named_scope("exchange_core"):
        other = flip(table, 1, 0)
    own_ions, recv_index, table = lax.optimization_barrier((own_ions, recv_index, table))
    with jax.named_scope("own_ions"):
        basis, table_z, hot, gain = pl.pallas_call(
            functools.partial(own_kernel, half, cap, row_count, bits),
            out_shape=(
                jax.ShapeDtypeStruct((BASIS_ROWS, slots), F32),
                jax.ShapeDtypeStruct((256, 2 * slots), BF16),
                jax.ShapeDtypeStruct((128 * packs, atoms_dev), BF16),
                jax.ShapeDtypeStruct((COUNT_ROWS, 128), F32),
            ),
            in_specs=whole(2),
            out_specs=tuple(whole(4)),
            compiler_params=params(),
            cost_estimate=pl.CostEstimate(flops=1 << 30, bytes_accessed=1 << 20, transcendentals=0),
        )(own_ions, recv_index)
    with jax.named_scope("forces"):
        return pl.pallas_call(
            functools.partial(force_kernel, force_scale, half),
            out_shape=(
                jax.ShapeDtypeStruct((3, slots), F32),
                jax.ShapeDtypeStruct((3, atoms_dev), F32),
            ),
            in_specs=whole(9),
            out_specs=tuple(whole(2)),
            scratch_shapes=[
                pltpu.VMEM((sum(FORCE_ROWS), 256), F32),
                pltpu.VMEM((BASIS_ROWS, atoms_dev), F32),
                pltpu.VMEM((256, 2 * atoms_dev), BF16),
            ],
            compiler_params=params(),
        )(table, other, counted, other_counted, own_ions, basis, table_z, hot, gain)


def solution(mesh):
    placed = (
        P(None, ("groups", "blk", "row")),
        P(("groups", "blk", "row")),
        P(("groups", "blk", "row")),
        P(("groups", "blk", "row")),
        P(("groups", "blk", "row")),
        P(None, "blk"),
    )
    return jax.shard_map(
        body,
        mesh=mesh,
        in_specs=placed,
        out_specs=(P(None, ("groups", "blk", "row")), P(None, ("groups", "blk", "row"))),
        check_vma=False,
    )
```

```python
import functools
import math

import jax
import jax.numpy as jnp
from jax import lax
from jax.experimental import pallas as pl
from jax.experimental.pallas import tpu as pltpu
from jax.sharding import PartitionSpec as P

DOUBLE_PI = 2.0 * math.pi
EWALD_BETA = 30.0
BOX_Z = 3.0
FORCE_GAIN = 400.0
SIN_POLY = (6.283185, -41.34159, 81.599945, -76.61447, 41.342884, -12.471244)
COS_POLY = (1.0, -19.739204, 64.93912, -85.45014, 60.16763, -25.9676, 6.5286584)

BASIS = 24
HARM = 40
STEMS = (((0, 0), (3, 0), (3, 1), (6, 0), (6, 1)), ((9, 0), (9, 1), (12, 0), (12, 1)))
SUM_ROWS = (144, 112)
ORDERS = (
    tuple((k, 0) for k in range(8)) + tuple((k, 1) for k in range(1, 8)),
    tuple((k, 0) for k in range(8, 13)) + tuple((k, 1) for k in range(8, 13)),
)
COUNT_ROWS = 240
COUNT_AT = (0, 136)
COUNT_LEN = (136, 96)
FORCE_ROWS = (384, 256)
FORCE_AT = (0, 384)
PART_AT = (0, 2 * SUM_ROWS[0])
ARRIVE_AT = PART_AT[1] + 2 * SUM_ROWS[1]
F32 = jnp.float32
BF16 = jnp.bfloat16
NT = (((1,), (1,)), ((), ()))
VMEM_BYTES = 40 * 1024 * 1024


def horner(coefs, v):
    total = jnp.full_like(v, coefs[-1])
    for coef in coefs[-2::-1]:
        total = total * v + coef
    return total


def harmonics(pos, first):
    harm = lax.broadcasted_iota(jnp.int32, (8, pos.shape[1]), 0).astype(F32) + float(first)
    turns = harm * pos
    turns = turns - jnp.floor(turns + 0.5)
    square = turns * turns
    return horner(COS_POLY, square), turns * horner(SIN_POLY, square)


def advance(first, by):
    cos_a, sin_a = first
    cos_b, sin_b = by
    return cos_a * cos_b - sin_a * sin_b, sin_a * cos_b + cos_a * sin_b


def row_of(pair, row):
    return pair[0][row : row + 1], pair[1][row : row + 1]


def merge_last(cos_part, sin_part):
    low = lax.broadcasted_iota(jnp.int32, cos_part.shape, 0) < 4
    return jnp.where(low, cos_part, pltpu.roll(sin_part, 4, 0))


def first_basis(pos):
    first = harmonics(pos, 1)
    second = advance(first, row_of(first, 7))
    return [first[0], first[1], merge_last(*second)]


def first_slopes(basis):
    row = lax.broadcasted_iota(jnp.int32, basis[0].shape, 0)
    harm = row.astype(F32) + 1.0
    low = row < 4
    factor = jnp.where(low, -(harm + 8.0), harm + 4.0)
    return [-harm * basis[1], harm * basis[0], factor * pltpu.roll(basis[2], 4, 0)]


def second_basis(pos):
    first = harmonics(pos, 0)
    fourth = row_of(first, 4)
    second = advance(first, advance(fourth, fourth))
    return [first[0], first[1], second[0], second[1]]


def second_slopes(basis):
    harm = lax.broadcasted_iota(jnp.int32, basis[0].shape, 0).astype(F32)
    high = harm + 8.0
    return [-harm * basis[1], harm * basis[0], -high * basis[3], high * basis[2]]


def second_row(basis, harmonic, sine):
    return basis[2 * (harmonic // 8) + sine][harmonic % 8 : harmonic % 8 + 1]


def third_basis(pos):
    first = harmonics(pos, 1)
    second = advance(first, row_of(first, 7))
    third = advance(first, row_of(second, 7))
    fourth = advance(second, row_of(second, 7))
    fifth = advance(first, row_of(fourth, 7))
    parts = (first, second, third, fourth, fifth)
    return jnp.concatenate([p[0] for p in parts] + [p[1] for p in parts], axis=0)


def split_two(value):
    high = value.astype(BF16)
    return high, (value - high.astype(F32)).astype(BF16)


def key_of_rows(recv, device, cap, row_count, bits):
    per_pack = 64 // cap
    source = (recv // cap) ^ device
    order = jnp.zeros_like(source)
    for place, distance in enumerate(bits):
        order = order | jnp.where((source & distance) != 0, 1 << place, 0)
    far = jnp.where((source & row_count) != 0, 64, 0)
    return (order // per_pack) * 128 + far + (order % per_pack) * cap + recv % cap


def prep_kernel(
    coords_hbm, charges_hbm, counts_hbm, send_hbm, waves_hbm, out_ref, waves_ref,
    coords_ref, charges_ref, counts_ref, send_ref, sems,
):
    copies = [
        pltpu.make_async_copy(source, target, sems.at[i])
        for i, (source, target) in enumerate(
            (
                (waves_hbm, waves_ref),
                (counts_hbm, counts_ref),
                (send_hbm, send_ref),
                (charges_hbm, charges_ref),
                (coords_hbm, coords_ref),
            )
        )
    ]
    for copy in copies:
        copy.start()
    slots = charges_ref.shape[0]
    half = slots // 2
    out_ref[:, 0 : half + 128] = jnp.zeros((8, half + 128), F32)
    for copy in copies[1:]:
        copy.wait()
    live = lax.broadcasted_iota(jnp.int32, (1, slots), 1) < counts_ref[0]
    charge = jnp.where(live, charges_ref[...].reshape(1, slots), 0.0)
    send = jnp.where(live, send_ref[...].reshape(1, slots), -1).astype(F32)
    for part in range(2):
        lanes = slice(part * half, (part + 1) * half)
        out_ref[4 * part : 4 * part + 3, 0:half] = coords_ref[:, lanes]
        out_ref[4 * part + 3 : 4 * part + 4, 0:half] = charge[:, lanes]
    for piece in range(slots // 128):
        out_ref[piece : piece + 1, half : half + 128] = send[:, piece * 128 : (piece + 1) * 128]
    copies[0].wait()


def wave_shape(k_local):
    rows = 8
    while k_local % (rows * 128):
        rows //= 2
    return rows, k_local // rows


def basis_row(index):
    size = jnp.abs(index)
    sign = jnp.where(index < 0.0, 1.0, 0.0)
    row = jnp.where(size <= 8.0, size - 1.0 + 8.0 * sign, size + 7.0 + 4.0 * sign)
    return jnp.where(size == 0.0, float(BASIS), row)


def basis_size(row):
    low = jnp.where(row < 8, row, row - 8) + 1
    high = jnp.where(row < 20, row - 16, row - 20) + 9
    return jnp.where(row < 16, low, jnp.where(row < BASIS, high, 0))


def dense_weights():
    row = lax.broadcasted_iota(jnp.int32, (COUNT_ROWS, 128), 0)
    lane = lax.broadcasted_iota(jnp.int32, (COUNT_ROWS, 128), 1)
    early = row < COUNT_AT[1]
    own = jnp.where(early, row, row - COUNT_AT[1])
    paired = own < jnp.where(early, COUNT_LEN[0] - 16, COUNT_LEN[1] - 16)
    group = own // 8
    size_y = jnp.where(early, jnp.where(group < 8, group, group - 7), 8 + jnp.where(group < 5, group, group - 5))
    size_y = jnp.where(paired, size_y, jnp.where(early, own % 8, 8 + own % 8))
    part = jnp.where(lane < HARM, 0, jnp.where(lane < 2 * HARM, 1, 2))
    size_x = jnp.where(paired, basis_size(own % 8 + 8 * part), 0)
    phys_x = DOUBLE_PI * size_x.astype(F32)
    phys_y = DOUBLE_PI * size_y.astype(F32)
    phys_z = DOUBLE_PI * (lane - HARM * part + 1).astype(F32) / BOX_Z
    k_squared = phys_x * phys_x + phys_y * phys_y + phys_z * phys_z
    return jnp.exp(-k_squared / (4.0 * EWALD_BETA * EWALD_BETA)) / k_squared


def count_waves(waves, rows, width):
    wave_h = waves[0:rows, 0:width]
    wave_k = waves[0:rows, width : 2 * width]
    wave_l = waves[0:rows, 2 * width : 3 * width]
    flip = jnp.where(wave_l < 0.0, -1.0, 1.0)
    row_x = basis_row(wave_h * flip)
    wave_k = wave_k * flip
    size_y = jnp.abs(wave_k)
    sine = jnp.where(wave_k < 0.0, 1.0, 0.0)
    const = row_x == float(BASIS)
    part = jnp.where(row_x >= 16.0, 2.0, jnp.where(row_x >= 8.0, 1.0, 0.0))
    part = jnp.where(const, 0.0, part)
    late = size_y >= 8.0
    group = jnp.where(late, size_y - 8.0 + 5.0 * sine, size_y + 7.0 * sine)
    paired_id = 8.0 * group + (row_x - 8.0 * part) + jnp.where(late, float(COUNT_AT[1]), 0.0)
    tail = jnp.where(late, size_y - 8.0 + float(COUNT_AT[1] + COUNT_LEN[1] - 16), size_y + float(COUNT_LEN[0] - 16))
    row_id = jnp.where(const, tail + 8.0 * sine, paired_id)
    lane_id = wave_l * flip + (HARM * part - 1.0)
    step = lax.broadcasted_iota(jnp.int32, (16, width), 0).astype(F32)
    steps = [(step + 16.0 * i).astype(BF16) for i in range(COUNT_ROWS // 16)]
    one = jnp.ones((16, width), BF16)
    none = jnp.zeros((16, width), BF16)
    total = None
    for piece in range(rows):
        rows_at = jnp.broadcast_to(row_id[piece : piece + 1], (16, width)).astype(BF16)
        lanes_at = jnp.broadcast_to(lane_id[piece : piece + 1], (16, width)).astype(BF16)
        row_hot = jnp.concatenate([jnp.where(rows_at == at, one, none) for at in steps], axis=0)
        lane_hot = jnp.concatenate([jnp.where(lanes_at == at, one, none) for at in steps[:8]], axis=0)
        found = lax.dot_general(row_hot, lane_hot, NT, preferred_element_type=F32)
        total = found if total is None else total + found
    return total


def owner_rows(block_rows, half):
    return [
        jnp.concatenate([block_rows[i : i + 1, 0:half], block_rows[i + 4 : i + 5, 0:half]], axis=1) for i in range(4)
    ]


def owner_tables(rows):
    pos_x, pos_y, pos_z, charge = rows
    basis_x = jnp.concatenate([charge * part for part in first_basis(pos_x)], axis=0)
    basis_y = second_basis(pos_y)
    third = third_basis(pos_z)
    lanes = jnp.concatenate([third, third * basis_y[0][1:2], third * basis_y[1][1:2]], axis=0)
    high, low = split_two(lanes)
    gap = jnp.zeros((256 - 6 * HARM, third.shape[1]), BF16)
    high = jnp.concatenate([high, gap], axis=0)
    low = jnp.concatenate([low, gap], axis=0)
    return basis_x, basis_y, high, low


def stem_rows(part, basis_y):
    return [second_row(basis_y, harmonic, sine) for harmonic, sine in STEMS[part]]


def store_rows(basis_x, basis_y, charge, v_ref):
    all_rows = sum(SUM_ROWS)
    slots = charge.shape[1]
    at = 0
    for part in range(2):
        stems = stem_rows(part, basis_y)
        rows = [stem * basis_x for stem in stems] + [charge * rows for rows in basis_y[2 * part : 2 * part + 2]]
        fill = SUM_ROWS[part] - BASIS * len(stems) - 16
        if fill:
            rows.append(jnp.zeros((fill, slots), F32))
        rows = jnp.concatenate(rows, axis=0)
        for begin in range(0, SUM_ROWS[part], 16):
            high, low = split_two(rows[begin : begin + 16])
            v_ref[at : at + 16] = high
            v_ref[all_rows + at : all_rows + at + 16] = low
            at += 16


def add_owners(owners, base_ref, table_ref, v_ref):
    all_rows = sum(SUM_ROWS)
    highs, lows = [], []
    for i, ions in enumerate(owners):
        slots = ions[3].shape[1]
        basis_x, basis_y, high, low = owner_tables(ions)
        store_rows(basis_x, basis_y, ions[3], v_ref.at[:, i * slots : (i + 1) * slots])
        highs.append(high)
        lows.append(low)
    width = sum(high.shape[1] for high in highs)
    both = lax.dot_general(v_ref[:, 0:width], jnp.concatenate(highs, axis=1), NT, preferred_element_type=F32)
    rest = lax.dot_general(v_ref[0:all_rows, 0:width], jnp.concatenate(lows, axis=1), NT, preferred_element_type=F32)
    total = (both[:all_rows] + both[all_rows:]) + rest
    at = 0
    for part in range(2):
        count, begin = SUM_ROWS[part], PART_AT[part]
        for half in range(2):
            rows = slice(begin + half * count, begin + (half + 1) * count)
            value = total[at : at + count, 128 * half : 128 * half + 128]
            table_ref[rows] = value if base_ref is None else base_ref[rows] + value
        at += count


def add_arrivals(block_rows, rows, half, cap, place, pack, targets, table_ref):
    block = half + 128
    slots = 2 * half
    send = jnp.concatenate([block_rows[p : p + 1, half:block] for p in range(slots // 128)], axis=1)
    step = lax.broadcasted_iota(jnp.int32, (16, slots), 0).astype(F32)
    one, none = jnp.ones((16, slots), BF16), jnp.zeros((16, slots), BF16)
    hots = []
    for target in targets:
        rank = send - (target * cap).astype(F32)
        valid = jnp.logical_and(rank >= 0.0, rank < float(cap))
        key = jnp.broadcast_to(jnp.where(valid, rank + place, -1.0), (16, slots)).astype(BF16)
        hots += [jnp.where(key == (step + 16.0 * i).astype(BF16), one, none) for i in range(4)]
    values = jnp.concatenate(rows + [jnp.zeros((4, slots), F32)], axis=0)
    found = lax.dot_general(split_three(values), jnp.concatenate(hots, axis=0), NT, preferred_element_type=F32)
    row = ARRIVE_AT + 8 * pack
    if not isinstance(row, int):
        row = pl.multiple_of(row, 8)
    table_ref[pl.ds(row, 8)] += (found[0:8] + found[8:16]) + found[16:24]


def split_three(value):
    high = value.astype(BF16).astype(F32)
    rest = value - high
    mid = rest.astype(BF16).astype(F32)
    return jnp.concatenate([high, mid, rest - mid], axis=0).astype(BF16)


def count_kernel(rows, width, waves_ref, out_ref, stack_ref):
    for row in range(rows):
        for comp in range(3):
            stack_ref[row : row + 1, comp * width : (comp + 1) * width] = waves_ref[
                comp : comp + 1, row * width : (row + 1) * width
            ].astype(F32)
    counts = count_waves(stack_ref, rows, width)
    for row in range(0, COUNT_ROWS, 8):
        out_ref[:, 16 * row : 16 * row + 128] = counts[row : row + 8]


def sums_kernel(plan, *refs):
    refs = list(refs)
    base_ref = refs.pop(0) if plan["has_base"] else None
    ion_refs = [refs.pop(0) for _ in plan["chunks"]]
    table_ref = refs.pop(0)
    v_ref = refs.pop(0)
    half, cap, row_count = plan["half"], plan["cap"], plan["row_count"]
    block = half + 128
    per_pack = 64 // cap
    device = lax.axis_index("blk") * row_count + lax.axis_index("row")
    targets = (device, device ^ row_count)
    kept = slice(ARRIVE_AT, table_ref.shape[0])
    table_ref[kept] = jnp.zeros_like(table_ref[kept]) if base_ref is None else base_ref[kept]

    for ions_ref, (owners, first_owner) in zip(ion_refs, plan["chunks"]):
        if owners <= 4 and per_pack == 1:
            for owner in range(0, owners, 2):
                group = []
                for i in range(owner, min(owner + 2, owners)):
                    block_rows = ions_ref[:, i * block : (i + 1) * block]
                    group.append(owner_rows(block_rows, half))
                    add_arrivals(block_rows, group[-1], half, cap, 0.0, first_owner + i, targets, table_ref)
                add_owners(group, base_ref, table_ref, v_ref)
                base_ref = table_ref
        else:
            if base_ref is not table_ref:
                sums = slice(0, ARRIVE_AT)
                table_ref[sums] = jnp.zeros_like(table_ref[sums]) if base_ref is None else base_ref[sums]
                base_ref = table_ref

            def step(owner, carry, ions_ref=ions_ref, first_owner=first_owner):
                begin = pl.multiple_of(owner * block, 128)
                index = first_owner + owner
                place = (lax.rem(index, per_pack) * cap).astype(F32)
                block_rows = ions_ref[:, pl.ds(begin, block)]
                ions = owner_rows(block_rows, half)
                add_arrivals(block_rows, ions, half, cap, place, index // per_pack, targets, table_ref)
                add_owners([ions], table_ref, table_ref, v_ref)
                return carry

            lax.fori_loop(0, owners, step, 0)


SLOPE_X, BASIS_Y, SLOPE_Y, BASIS_ROWS = 24, 48, 80, 112


def store_bases(ions, basis_ref, z_ref):
    count = ions.shape[1]
    basis_x = first_basis(ions[0:1])
    basis_y = second_basis(ions[1:2])
    parts = basis_x + first_slopes(basis_x) + basis_y + second_slopes(basis_y)
    for i, part in enumerate(parts):
        basis_ref[8 * i : 8 * i + 8] = part
    plain = third_basis(ions[2:3])
    harm = lax.broadcasted_iota(jnp.int32, (HARM, count), 0).astype(F32) + 1.0
    slope = jnp.concatenate([-harm * plain[HARM:], harm * plain[:HARM]], axis=0)
    for i, table in enumerate((plain, slope)):
        high, low = split_two(table)
        z_ref[:, i * count : (i + 1) * count] = jnp.concatenate(
            [high, low, high, jnp.zeros((256 - 6 * HARM, count), BF16)], axis=0
        )


def own_kernel(half, cap, row_count, bits, data_ref, recv_ref, basis_ref, z_ref, hot_ref, gain_ref):
    store_bases(jnp.concatenate([data_ref[0:4, 0:half], data_ref[4:8, 0:half]], axis=1), basis_ref, z_ref)
    atoms_dev = recv_ref.shape[0]
    device = lax.axis_index("blk") * row_count + lax.axis_index("row")
    key = key_of_rows(recv_ref[...].reshape(1, atoms_dev), device, cap, row_count, bits)
    spot = lax.broadcasted_iota(jnp.int32, hot_ref.shape, 0)
    hot_ref[...] = jnp.where(spot == key, 1.0, 0.0).astype(BF16)
    gain_ref[...] = dense_weights()


def swap(parts):
    return [parts[1], parts[0], pltpu.roll(parts[2], 4, 0)]


def store_coefs(part, gain_ref, count_refs, coef_ref):
    lane = lax.broadcasted_iota(jnp.int32, (8, 128), 1)
    is_cos = lane < HARM
    is_wave = lane < 2 * HARM

    def gains(row):
        at = COUNT_AT[part] + row
        lanes = slice(16 * at, 16 * at + 128)
        tile = (count_refs[0][:, lanes] + count_refs[1][:, lanes]) * gain_ref[at : at + 8]
        back, far = pltpu.roll(tile, 88, 1), pltpu.roll(tile, 48, 1)
        pairs = ((tile, pltpu.roll(tile, HARM, 1)), (back, tile), (far, back))
        return [jnp.where(is_cos, a, jnp.where(is_wave, b, 0.0)) for a, b in pairs]

    order = ORDERS[part]
    pairs = {}
    for i, name in enumerate(order):
        gain = gains(8 * i)
        other = swap(gain)
        pairs[name] = [a + b for a, b in zip(gain, other)], [a - b for a, b in zip(gain, other)]
    for i, (harmonic, sine) in enumerate(order):
        both, odd = pairs[(harmonic, sine)]
        both_o, odd_o = pairs.get((harmonic, 1 - sine), (None, None))
        for x in range(3):
            row = FORCE_AT[part] + BASIS * i + 8 * x
            if both_o is None:
                coefs = (both[x], odd[x])
            else:
                coefs = (both[x] + both_o[x], odd[x] + odd_o[x], both[x] - both_o[x], odd[x] - odd_o[x])
            for kind, coef in enumerate(coefs):
                coef_ref[kind, row : row + 8] = coef
    tails = [gains(COUNT_LEN[part] - 16 + 8 * sine)[0] for sine in range(2)]
    for sine in range(2):
        row = FORCE_AT[part] + BASIS * len(order) + 8 * sine
        coef_ref[0, row : row + 8] = tails[sine] + tails[1 - sine]
        coef_ref[2, row : row + 8] = tails[sine] - tails[1 - sine]


def coef_kernel(gain_ref, count_ref, other_count_ref, coef_ref):
    for part in range(2):
        store_coefs(part, gain_ref, (count_ref, other_count_ref), coef_ref)


def weighted_sums(part, mine_ref, other_ref, coef_ref, w_ref):
    lane = lax.broadcasted_iota(jnp.int32, (8, 128), 1)
    is_cos = lane < HARM
    is_wave = lane < 2 * HARM
    count = SUM_ROWS[part]

    def both(row):
        row = PART_AT[part] + row
        return mine_ref[row : row + 8] + other_ref[row : row + 8]

    def blocks(row):
        near, far = both(row), both(count + row)
        middle = jnp.where(lane < 48, pltpu.roll(near, 48, 1), pltpu.roll(far, 48, 1))
        return [jnp.where(is_wave, value, 0.0) for value in (near, middle, pltpu.roll(far, 96, 1))]

    def turn(sums):
        return jnp.where(is_cos, pltpu.roll(sums, 88, 1), -pltpu.roll(sums, HARM, 1))

    def harmonics_of(stem):
        found = {}
        for harmonic, _ in STEMS[part]:
            if harmonic == 0:
                plain, cos_1, sin_1 = stem[(0, 0)]
                found.update({(0, 0): plain, (1, 0): cos_1, (1, 1): sin_1})
                continue
            cos, sin = stem[(harmonic, 0)], stem[(harmonic, 1)]
            found[(harmonic, 0)], found[(harmonic, 1)] = cos[0], sin[0]
            found[(harmonic - 1, 0)] = cos[1] + sin[2]
            found[(harmonic - 1, 1)] = sin[1] - cos[2]
            found[(harmonic + 1, 0)] = cos[1] - sin[2]
            found[(harmonic + 1, 1)] = sin[1] + cos[2]
        return found

    def store(row, value):
        high, low = split_two(value)
        high = high.astype(F32)
        low = low.astype(F32)
        turned = pltpu.roll(high, 2 * HARM, 1)
        row = FORCE_AT[part] + row
        w_ref[row : row + 8, 0:128] = jnp.where(is_wave, high, turned)
        w_ref[row : row + 8, 128:256] = jnp.where(lane < 32, turned, pltpu.roll(low, 32, 1))

    by_block = [
        harmonics_of({stem: blocks(BASIS * i + 8 * x) for i, stem in enumerate(STEMS[part])}) for x in range(3)
    ]
    order = ORDERS[part]
    groups = {}
    for name in order:
        sums = [by_block[x][name] for x in range(3)]
        turned = [turn(value) for value in sums]
        groups[name] = swap(sums), turned, swap(turned)
    for i, (harmonic, sine) in enumerate(order):
        turned_s = groups[(harmonic, sine)][2]
        for x in range(3):
            row = BASIS * i + 8 * x
            coefs = [coef_ref[kind, FORCE_AT[part] + row : FORCE_AT[part] + row + 8] for kind in range(4)]
            value = coefs[0] * by_block[x][(harmonic, sine)] - coefs[1] * turned_s[x]
            if harmonic:
                sums_os, turned_o, _ = groups[(harmonic, 1 - sine)]
                value = value - coefs[2] * turned_o[x] - coefs[3] * sums_os[x]
            store(row, value)
    tails = [blocks(BASIS * len(STEMS[part]) + 8 * sine) for sine in range(2)]
    found = harmonics_of({(h, sine): [b[h % 8 : h % 8 + 1] for b in tails[sine]] for h, sine in STEMS[part]})
    index = lax.broadcasted_iota(jnp.int32, (8, 128), 0)
    kinds = []
    for sine in range(2):
        rows = jnp.zeros((8, 128), F32)
        for harmonic, kind in order:
            if kind == sine:
                rows = jnp.where(index == harmonic % 8, found[(harmonic, kind)], rows)
        kinds.append((rows, turn(rows)))
    at = BASIS * len(order)
    for sine in range(2):
        row = FORCE_AT[part] + at + 8 * sine
        store(at + 8 * sine, coef_ref[0, row : row + 8] * kinds[sine][0] - coef_ref[2, row : row + 8] * kinds[1 - sine][1])
    if at + 16 < FORCE_ROWS[part]:
        fill = FORCE_ROWS[part] - at - 16
        w_ref[FORCE_AT[part] + at + 16 : FORCE_AT[part] + FORCE_ROWS[part]] = jnp.zeros((fill, 256), F32)


def pull(weights, basis_ref, z_ref, count, begin, tile):
    lanes = slice(begin, begin + tile)
    plain = jnp.dot(weights, z_ref[:, begin : begin + tile], preferred_element_type=F32)
    sloped = jnp.dot(weights, z_ref[:, count + begin : count + begin + tile], preferred_element_type=F32)
    zero = jnp.zeros((8, tile), F32)
    even, slope, third = [zero] * 3, [zero] * 3, [zero] * 3
    sum_y = sum_z = zero
    for part in range(2):
        for place, (harmonic, sine) in enumerate(ORDERS[part]):
            at = 16 * (harmonic // 8) + 8 * sine + harmonic % 8
            basis = basis_ref[BASIS_Y + at : BASIS_Y + at + 1, lanes]
            basis_slope = basis_ref[SLOPE_Y + at : SLOPE_Y + at + 1, lanes]
            for i in range(3):
                row = FORCE_AT[part] + BASIS * place + 8 * i
                plain_rows, sloped_rows = plain[row : row + 8], sloped[row : row + 8]
                if harmonic == 0:
                    even[i] = even[i] + plain_rows
                    third[i] = third[i] + sloped_rows
                else:
                    even[i] = even[i] + basis * plain_rows
                    slope[i] = slope[i] + basis_slope * plain_rows
                    third[i] = third[i] + basis * sloped_rows
        for sine in range(2):
            row = FORCE_AT[part] + BASIS * len(ORDERS[part]) + 8 * sine
            at = 16 * part + 8 * sine
            sum_y = sum_y + basis_ref[SLOPE_Y + at : SLOPE_Y + at + 8, lanes] * plain[row : row + 8]
            sum_z = sum_z + basis_ref[BASIS_Y + at : BASIS_Y + at + 8, lanes] * sloped[row : row + 8]
    sum_x = zero
    for i in range(3):
        rows_x = basis_ref[8 * i : 8 * i + 8, lanes]
        sum_x = sum_x + basis_ref[SLOPE_X + 8 * i : SLOPE_X + 8 * i + 8, lanes] * even[i]
        sum_y = sum_y + rows_x * slope[i]
        sum_z = sum_z + rows_x * third[i]
    return [jnp.sum(value, axis=0, keepdims=True) for value in (sum_x, sum_y, sum_z)]


TILE = 256


def force_kernel(
    force_scale, half, mine_ref, other_ref, data_ref, basis_ref, z_ref, hot_ref, coef_ref,
    slot_ref, atom_ref, w_ref, atom_basis_ref, atom_z_ref,
):
    packs = hot_ref.shape[0] // 128
    lane = lax.broadcasted_iota(jnp.int32, (8, 128), 1)
    starts = [ARRIVE_AT + 8 * p for p in range(packs)]
    pool = jnp.concatenate([jnp.where(lane < 64, mine_ref[r : r + 8], other_ref[r : r + 8]) for r in starts], axis=1)
    found = jnp.dot(split_three(pool), hot_ref[...], preferred_element_type=F32)
    routed = ((found[0:8] + found[8:16]) + found[16:24])[0:4]
    for part in range(2):
        weighted_sums(part, mine_ref, other_ref, coef_ref, w_ref)
    weights = w_ref[...].astype(BF16)
    store_bases(routed, atom_basis_ref, atom_z_ref)
    charge = jnp.concatenate([data_ref[3:4, 0:half], data_ref[7:8, 0:half]], axis=1)
    jobs = ((basis_ref, z_ref, charge, slot_ref), (atom_basis_ref, atom_z_ref, routed[3:4], atom_ref))
    for rows_ref, table_ref, charges, out_ref in jobs:
        count = out_ref.shape[1]
        for begin in range(0, count, TILE):
            lanes = slice(begin, begin + TILE)
            gain = (-DOUBLE_PI * force_scale) * charges[:, lanes]
            gains = (gain, gain, gain / BOX_Z)
            found = pull(weights, rows_ref, table_ref, count, begin, TILE)
            out_ref[:, lanes] = jnp.concatenate([gains[i] * found[i] for i in range(3)], axis=0)


def params():
    return pltpu.CompilerParams(vmem_limit_bytes=VMEM_BYTES)


def stay(value):
    return pltpu.with_memory_space_constraint(value, pltpu.HBM)


def whole(count):
    return [pl.BlockSpec(memory_space=pltpu.VMEM)] * count


def body(coords, charges, counts, send_slot, recv_index, wave_ints):
    slots = charges.shape[0]
    half = slots // 2
    block = half + 128
    atoms_dev = recv_index.shape[0]
    devices = lax.axis_size(("blk", "row"))
    blk_count = lax.axis_size("blk")
    row_count = lax.axis_size("row")
    k_local = wave_ints.shape[1]
    cap = 2 * atoms_dev // devices
    packs = max(1, devices // 2 * cap // 64)
    per_pack = 64 // cap
    wave_rows, wave_width = wave_shape(k_local)
    force_scale = FORCE_GAIN / math.sqrt(float(atoms_dev * devices * blk_count * k_local))
    table_shape = jax.ShapeDtypeStruct((ARRIVE_AT + 8 * packs, 128), F32)
    count_shape = jax.ShapeDtypeStruct((8, 16 * COUNT_ROWS), F32)

    with jax.named_scope("payload"):
        own_ions, waves = pl.pallas_call(
            prep_kernel,
            out_shape=(
                jax.ShapeDtypeStruct((8, block), F32),
                jax.ShapeDtypeStruct(wave_ints.shape, jnp.int32),
            ),
            in_specs=[pl.BlockSpec(memory_space=pltpu.HBM)] * 5,
            out_specs=tuple(whole(2)),
            scratch_shapes=[
                pltpu.VMEM(coords.shape, F32),
                pltpu.VMEM(charges.shape, F32),
                pltpu.SMEM(counts.shape, jnp.int32),
                pltpu.VMEM(send_slot.shape, jnp.int32),
                pltpu.SemaphoreType.DMA((5,)),
            ],
            compiler_params=params(),
        )(stay(coords), stay(charges), counts, stay(send_slot), stay(wave_ints))

    def flip(value, blk_bit, row_bit):
        if not row_bit:
            return lax.ppermute(value, "blk", [(i, i ^ blk_bit) for i in range(blk_count)])
        if not blk_bit:
            return lax.ppermute(value, "row", [(i, i ^ row_bit) for i in range(row_count)])
        distance = row_count * blk_bit + row_bit
        return lax.ppermute(value, ("blk", "row"), [(i, i ^ distance) for i in range(devices)])

    def joined(values):
        return values[0] if len(values) == 1 else jnp.concatenate(values, axis=1)

    def accumulate(table, chunks, cost=1):
        plan = {
            "has_base": table is not None,
            "chunks": [chunk[1:] for chunk in chunks],
            "half": half,
            "cap": cap,
            "row_count": row_count,
        }
        args = [table] * plan["has_base"] + [chunk[0] for chunk in chunks]
        flops = int(cost * 2 * sum(chunk[1] for chunk in chunks) * slots * 256 * 720)
        with jax.named_scope("structure_sums"):
            return pl.pallas_call(
                functools.partial(sums_kernel, plan),
                out_shape=table_shape,
                in_specs=whole(len(args)),
                out_specs=whole(1)[0],
                scratch_shapes=[pltpu.VMEM((2 * sum(SUM_ROWS), 2 * slots), BF16)],
                compiler_params=params(),
                cost_estimate=pl.CostEstimate(flops=flops, bytes_accessed=1 << 20, transcendentals=0),
            )(*args)

    steps = []
    bit = row_count // 2
    while bit >= 2:
        steps.append((0, bit))
        bit //= 2
    bit = 4
    while bit < blk_count:
        steps.append((bit, 0))
        bit *= 2
    bits = [row_count * blk_bit + row_bit for blk_bit, row_bit in steps] + [2 * row_count, 1]
    table, counted = None, None
    ions, held, chunks = [own_ions], 1, [(own_ions, 1, 0)]
    for blk_bit, row_bit in steps:
        with jax.named_scope("exchange_ions"):
            got = flip(joined(ions), blk_bit, row_bit)
        if blk_bit:
            with jax.named_scope("exchange_counts"):
                counted = counted + flip(counted, blk_bit, 0)
        if counted is None:
            with jax.named_scope("counts"):
                counted = pl.pallas_call(
                    functools.partial(count_kernel, wave_rows, wave_width),
                    out_shape=count_shape,
                    in_specs=whole(1),
                    out_specs=whole(1)[0],
                    scratch_shapes=[pltpu.VMEM((wave_rows, 3 * wave_width), F32)],
                    compiler_params=params(),
                    cost_estimate=pl.CostEstimate(
                        flops=2 * k_local * COUNT_ROWS * 128, bytes_accessed=1 << 20, transcendentals=0
                    ),
                )(waves)
            got, counted = lax.optimization_barrier((got, counted))
        else:
            table, chunks = accumulate(table, chunks), []
            got, table = lax.optimization_barrier((got, table))
        chunks = chunks + [(got, held, held)]
        ions = ions + [got]
        held *= 2
    with jax.named_scope("exchange_ions"):
        sent = joined(ions)
        across = flip(jnp.concatenate([sent, counted], axis=1), 2, 0)
        along = flip(sent, 0, 1)
        corner = flip(sent, 2, 1)
    table = accumulate(table, chunks)
    own_ions, recv_index, table = lax.optimization_barrier((own_ions, recv_index, table))
    with jax.named_scope("own_ions"):
        basis, table_z, hot, gain = pl.pallas_call(
            functools.partial(own_kernel, half, cap, row_count, bits),
            out_shape=(
                jax.ShapeDtypeStruct((BASIS_ROWS, slots), F32),
                jax.ShapeDtypeStruct((256, 2 * slots), BF16),
                jax.ShapeDtypeStruct((128 * packs, atoms_dev), BF16),
                jax.ShapeDtypeStruct((COUNT_ROWS, 128), F32),
            ),
            in_specs=whole(2),
            out_specs=tuple(whole(4)),
            compiler_params=params(),
            cost_estimate=pl.CostEstimate(flops=1<<22, bytes_accessed=1 << 20, transcendentals=0),
        )(own_ions, recv_index)
    along, table, basis, table_z, hot, gain = lax.optimization_barrier((along, table, basis, table_z, hot, gain))
    table = accumulate(table, [(along, held, 2 * held)], cost=0.05)
    table = accumulate(table, [(across, held, held)], cost=0.05)
    with jax.named_scope("exchange_core"):
        counted = counted + across[:, held * block :]
        other_counted = flip(counted, 1, 0)
    corner, table, counted = lax.optimization_barrier((corner, table, counted))
    table = accumulate(table, [(corner, held, 3 * held)], cost=16)
    with jax.named_scope("exchange_core"):
        other = flip(table, 1, 0)
    with jax.named_scope("coefficients"):
        coefs = pl.pallas_call(
            coef_kernel,
            out_shape=jax.ShapeDtypeStruct((4, sum(FORCE_ROWS), 128), F32),
            in_specs=whole(3),
            out_specs=whole(1)[0],
            compiler_params=params(),
            cost_estimate=pl.CostEstimate(flops=1<<33, bytes_accessed=1 << 20, transcendentals=0),
        )(gain, counted, other_counted)
    with jax.named_scope("forces"):
        return pl.pallas_call(
            functools.partial(force_kernel, force_scale, half),
            out_shape=(
                jax.ShapeDtypeStruct((3, slots), F32),
                jax.ShapeDtypeStruct((3, atoms_dev), F32),
            ),
            in_specs=whole(7),
            out_specs=tuple(whole(2)),
            scratch_shapes=[
                pltpu.VMEM((sum(FORCE_ROWS), 256), F32),
                pltpu.VMEM((BASIS_ROWS, atoms_dev), F32),
                pltpu.VMEM((256, 2 * atoms_dev), BF16),
            ],
            compiler_params=params(),
        )(table, other, own_ions, basis, table_z, hot, coefs)


def solution(mesh):
    placed = (
        P(None, ("groups", "blk", "row")),
        P(("groups", "blk", "row")),
        P(("groups", "blk", "row")),
        P(("groups", "blk", "row")),
        P(("groups", "blk", "row")),
        P(None, "blk"),
    )
    return jax.shard_map(
        body,
        mesh=mesh,
        in_specs=placed,
        out_specs=(P(None, ("groups", "blk", "row")), P(None, ("groups", "blk", "row"))),
        check_vma=False,
    )
```

```python
import functools
import math

import jax
import jax.numpy as jnp
from jax import lax
from jax.experimental import pallas as pl
from jax.experimental.pallas import tpu as pltpu
from jax.sharding import PartitionSpec as P

DOUBLE_PI = 2.0 * math.pi
EWALD_BETA = 30.0
BOX_Z = 3.0
FORCE_GAIN = 400.0
SIN_POLY = (6.283185, -41.34159, 81.599945, -76.61447, 41.342884, -12.471244)
COS_POLY = (1.0, -19.739204, 64.93912, -85.45014, 60.16763, -25.9676, 6.5286584)

BASIS = 24
HARM = 40
STEMS = (((0, 0), (3, 0), (3, 1), (6, 0), (6, 1)), ((9, 0), (9, 1), (12, 0), (12, 1)))
SUM_ROWS = (144, 112)
ORDERS = (
    tuple((k, 0) for k in range(8)) + tuple((k, 1) for k in range(1, 8)),
    tuple((k, 0) for k in range(8, 13)) + tuple((k, 1) for k in range(8, 13)),
)
COUNT_ROWS = 240
COUNT_AT = (0, 136)
COUNT_LEN = (136, 96)
FORCE_ROWS = (384, 256)
FORCE_AT = (0, 384)
PART_AT = (0, 2 * SUM_ROWS[0])
ARRIVE_AT = PART_AT[1] + 2 * SUM_ROWS[1]
F32 = jnp.float32
BF16 = jnp.bfloat16
NT = (((1,), (1,)), ((), ()))
VMEM_BYTES = 40 * 1024 * 1024


def horner(coefs, v):
    total = jnp.full_like(v, coefs[-1])
    for coef in coefs[-2::-1]:
        total = total * v + coef
    return total


def harmonics(pos, first):
    harm = lax.broadcasted_iota(jnp.int32, (8, pos.shape[1]), 0).astype(F32) + float(first)
    turns = harm * pos
    turns = turns - jnp.floor(turns + 0.5)
    square = turns * turns
    return horner(COS_POLY, square), turns * horner(SIN_POLY, square)


def advance(first, by):
    cos_a, sin_a = first
    cos_b, sin_b = by
    return cos_a * cos_b - sin_a * sin_b, sin_a * cos_b + cos_a * sin_b


def row_of(pair, row):
    return pair[0][row : row + 1], pair[1][row : row + 1]


def merge_last(cos_part, sin_part):
    low = lax.broadcasted_iota(jnp.int32, cos_part.shape, 0) < 4
    return jnp.where(low, cos_part, pltpu.roll(sin_part, 4, 0))


def first_basis(pos):
    first = harmonics(pos, 1)
    second = advance(first, row_of(first, 7))
    return [first[0], first[1], merge_last(*second)]


def first_slopes(basis):
    row = lax.broadcasted_iota(jnp.int32, basis[0].shape, 0)
    harm = row.astype(F32) + 1.0
    low = row < 4
    factor = jnp.where(low, -(harm + 8.0), harm + 4.0)
    return [-harm * basis[1], harm * basis[0], factor * pltpu.roll(basis[2], 4, 0)]


def second_basis(pos):
    first = harmonics(pos, 0)
    fourth = row_of(first, 4)
    second = advance(first, advance(fourth, fourth))
    return [first[0], first[1], second[0], second[1]]


def second_slopes(basis):
    harm = lax.broadcasted_iota(jnp.int32, basis[0].shape, 0).astype(F32)
    high = harm + 8.0
    return [-harm * basis[1], harm * basis[0], -high * basis[3], high * basis[2]]


def second_row(basis, harmonic, sine):
    return basis[2 * (harmonic // 8) + sine][harmonic % 8 : harmonic % 8 + 1]


def third_basis(pos):
    first = harmonics(pos, 1)
    second = advance(first, row_of(first, 7))
    third = advance(first, row_of(second, 7))
    fourth = advance(second, row_of(second, 7))
    fifth = advance(first, row_of(fourth, 7))
    parts = (first, second, third, fourth, fifth)
    return jnp.concatenate([p[0] for p in parts] + [p[1] for p in parts], axis=0)


def split_two(value):
    high = value.astype(BF16)
    return high, (value - high.astype(F32)).astype(BF16)


def key_of_rows(recv, device, cap, row_count, bits):
    per_pack = 64 // cap
    source = (recv // cap) ^ device
    order = jnp.zeros_like(source)
    for place, distance in enumerate(bits):
        order = order | jnp.where((source & distance) != 0, 1 << place, 0)
    far = jnp.where((source & row_count) != 0, 64, 0)
    return (order // per_pack) * 128 + far + (order % per_pack) * cap + recv % cap


def prep_kernel(
    coords_hbm, charges_hbm, counts_hbm, send_hbm, out_ref, coords_ref, charges_ref, counts_ref, send_ref, sems
):
    copies = [
        pltpu.make_async_copy(source, target, sems.at[i])
        for i, (source, target) in enumerate(
            (
                (counts_hbm, counts_ref),
                (send_hbm, send_ref),
                (charges_hbm, charges_ref),
                (coords_hbm, coords_ref),
            )
        )
    ]
    for copy in copies:
        copy.start()
    slots = charges_ref.shape[0]
    half = slots // 2
    out_ref[:, 0 : half + 128] = jnp.zeros((8, half + 128), F32)
    for copy in copies:
        copy.wait()
    live = lax.broadcasted_iota(jnp.int32, (1, slots), 1) < counts_ref[0]
    charge = jnp.where(live, charges_ref[...].reshape(1, slots), 0.0)
    send = jnp.where(live, send_ref[...].reshape(1, slots), -1).astype(F32)
    for part in range(2):
        lanes = slice(part * half, (part + 1) * half)
        out_ref[4 * part : 4 * part + 3, 0:half] = coords_ref[:, lanes]
        out_ref[4 * part + 3 : 4 * part + 4, 0:half] = charge[:, lanes]
    for piece in range(slots // 128):
        out_ref[piece : piece + 1, half : half + 128] = send[:, piece * 128 : (piece + 1) * 128]


def wave_shape(k_local):
    rows = 8
    while k_local % (rows * 128):
        rows //= 2
    return rows, k_local // rows


def basis_row(index):
    size = jnp.abs(index)
    sign = jnp.where(index < 0.0, 1.0, 0.0)
    row = jnp.where(size <= 8.0, size - 1.0 + 8.0 * sign, size + 7.0 + 4.0 * sign)
    return jnp.where(size == 0.0, float(BASIS), row)


def basis_size(row):
    low = jnp.where(row < 8, row, row - 8) + 1
    high = jnp.where(row < 20, row - 16, row - 20) + 9
    return jnp.where(row < 16, low, jnp.where(row < BASIS, high, 0))


def dense_weights():
    row = lax.broadcasted_iota(jnp.int32, (COUNT_ROWS, 128), 0)
    lane = lax.broadcasted_iota(jnp.int32, (COUNT_ROWS, 128), 1)
    early = row < COUNT_AT[1]
    own = jnp.where(early, row, row - COUNT_AT[1])
    paired = own < jnp.where(early, COUNT_LEN[0] - 16, COUNT_LEN[1] - 16)
    group = own // 8
    size_y = jnp.where(early, jnp.where(group < 8, group, group - 7), 8 + jnp.where(group < 5, group, group - 5))
    size_y = jnp.where(paired, size_y, jnp.where(early, own % 8, 8 + own % 8))
    part = jnp.where(lane < HARM, 0, jnp.where(lane < 2 * HARM, 1, 2))
    size_x = jnp.where(paired, basis_size(own % 8 + 8 * part), 0)
    phys_x = DOUBLE_PI * size_x.astype(F32)
    phys_y = DOUBLE_PI * size_y.astype(F32)
    phys_z = DOUBLE_PI * (lane - HARM * part + 1).astype(F32) / BOX_Z
    k_squared = phys_x * phys_x + phys_y * phys_y + phys_z * phys_z
    return jnp.exp(-k_squared / (4.0 * EWALD_BETA * EWALD_BETA)) / k_squared


def count_waves(waves, rows, width):
    wave_h = waves[0:rows, 0:width]
    wave_k = waves[0:rows, width : 2 * width]
    wave_l = waves[0:rows, 2 * width : 3 * width]
    flip = jnp.where(wave_l < 0.0, -1.0, 1.0)
    row_x = basis_row(wave_h * flip)
    wave_k = wave_k * flip
    size_y = jnp.abs(wave_k)
    sine = jnp.where(wave_k < 0.0, 1.0, 0.0)
    const = row_x == float(BASIS)
    part = jnp.where(row_x >= 16.0, 2.0, jnp.where(row_x >= 8.0, 1.0, 0.0))
    part = jnp.where(const, 0.0, part)
    late = size_y >= 8.0
    group = jnp.where(late, size_y - 8.0 + 5.0 * sine, size_y + 7.0 * sine)
    paired_id = 8.0 * group + (row_x - 8.0 * part) + jnp.where(late, float(COUNT_AT[1]), 0.0)
    tail = jnp.where(late, size_y - 8.0 + float(COUNT_AT[1] + COUNT_LEN[1] - 16), size_y + float(COUNT_LEN[0] - 16))
    row_id = jnp.where(const, tail + 8.0 * sine, paired_id)
    lane_id = wave_l * flip + (HARM * part - 1.0)
    step = lax.broadcasted_iota(jnp.int32, (16, width), 0).astype(F32)
    steps = [(step + 16.0 * i).astype(BF16) for i in range(COUNT_ROWS // 16)]
    one = jnp.ones((16, width), BF16)
    none = jnp.zeros((16, width), BF16)
    total = None
    for piece in range(rows):
        rows_at = jnp.broadcast_to(row_id[piece : piece + 1], (16, width)).astype(BF16)
        lanes_at = jnp.broadcast_to(lane_id[piece : piece + 1], (16, width)).astype(BF16)
        row_hot = jnp.concatenate([jnp.where(rows_at == at, one, none) for at in steps], axis=0)
        lane_hot = jnp.concatenate([jnp.where(lanes_at == at, one, none) for at in steps[:8]], axis=0)
        found = lax.dot_general(row_hot, lane_hot, NT, preferred_element_type=F32)
        total = found if total is None else total + found
    return total


def owner_rows(block_rows, half):
    return [
        jnp.concatenate([block_rows[i : i + 1, 0:half], block_rows[i + 4 : i + 5, 0:half]], axis=1) for i in range(4)
    ]


def owner_tables(rows):
    pos_x, pos_y, pos_z, charge = rows
    basis_x = jnp.concatenate([charge * part for part in first_basis(pos_x)], axis=0)
    basis_y = second_basis(pos_y)
    third = third_basis(pos_z)
    lanes = jnp.concatenate([third, third * basis_y[0][1:2], third * basis_y[1][1:2]], axis=0)
    high, low = split_two(lanes)
    gap = jnp.zeros((256 - 6 * HARM, third.shape[1]), BF16)
    high = jnp.concatenate([high, gap], axis=0)
    low = jnp.concatenate([low, gap], axis=0)
    return basis_x, basis_y, high, low


def stem_rows(part, basis_y):
    return [second_row(basis_y, harmonic, sine) for harmonic, sine in STEMS[part]]


def store_rows(basis_x, basis_y, charge, v_ref):
    all_rows = sum(SUM_ROWS)
    slots = charge.shape[1]
    at = 0
    for part in range(2):
        stems = stem_rows(part, basis_y)
        rows = [stem * basis_x for stem in stems] + [charge * rows for rows in basis_y[2 * part : 2 * part + 2]]
        fill = SUM_ROWS[part] - BASIS * len(stems) - 16
        if fill:
            rows.append(jnp.zeros((fill, slots), F32))
        rows = jnp.concatenate(rows, axis=0)
        for begin in range(0, SUM_ROWS[part], 16):
            high, low = split_two(rows[begin : begin + 16])
            v_ref[at : at + 16] = high
            v_ref[all_rows + at : all_rows + at + 16] = low
            at += 16


def add_owners(owners, base_ref, table_ref, v_ref):
    all_rows = sum(SUM_ROWS)
    highs, lows = [], []
    for i, ions in enumerate(owners):
        slots = ions[3].shape[1]
        basis_x, basis_y, high, low = owner_tables(ions)
        store_rows(basis_x, basis_y, ions[3], v_ref.at[:, i * slots : (i + 1) * slots])
        highs.append(high)
        lows.append(low)
    width = sum(high.shape[1] for high in highs)
    both = lax.dot_general(v_ref[:, 0:width], jnp.concatenate(highs, axis=1), NT, preferred_element_type=F32)
    rest = lax.dot_general(v_ref[0:all_rows, 0:width], jnp.concatenate(lows, axis=1), NT, preferred_element_type=F32)
    total = (both[:all_rows] + both[all_rows:]) + rest
    at = 0
    for part in range(2):
        count, begin = SUM_ROWS[part], PART_AT[part]
        for half in range(2):
            rows = slice(begin + half * count, begin + (half + 1) * count)
            value = total[at : at + count, 128 * half : 128 * half + 128]
            table_ref[rows] = value if base_ref is None else base_ref[rows] + value
        at += count


def add_arrivals(block_rows, rows, half, cap, place, pack, targets, table_ref):
    block = half + 128
    slots = 2 * half
    send = jnp.concatenate([block_rows[p : p + 1, half:block] for p in range(slots // 128)], axis=1)
    step = lax.broadcasted_iota(jnp.int32, (16, slots), 0).astype(F32)
    one, none = jnp.ones((16, slots), BF16), jnp.zeros((16, slots), BF16)
    hots = []
    for target in targets:
        rank = send - (target * cap).astype(F32)
        valid = jnp.logical_and(rank >= 0.0, rank < float(cap))
        key = jnp.broadcast_to(jnp.where(valid, rank + place, -1.0), (16, slots)).astype(BF16)
        hots += [jnp.where(key == (step + 16.0 * i).astype(BF16), one, none) for i in range(4)]
    values = jnp.concatenate(rows + [jnp.zeros((4, slots), F32)], axis=0)
    found = lax.dot_general(split_three(values), jnp.concatenate(hots, axis=0), NT, preferred_element_type=F32)
    row = ARRIVE_AT + 8 * pack
    if not isinstance(row, int):
        row = pl.multiple_of(row, 8)
    table_ref[pl.ds(row, 8)] += (found[0:8] + found[8:16]) + found[16:24]


def split_three(value):
    high = value.astype(BF16).astype(F32)
    rest = value - high
    mid = rest.astype(BF16).astype(F32)
    return jnp.concatenate([high, mid, rest - mid], axis=0).astype(BF16)


def count_kernel(rows, width, waves_hbm, out_ref, waves_ref, stack_ref, sem):
    copy = pltpu.make_async_copy(waves_hbm, waves_ref, sem)
    copy.start()
    copy.wait()
    for row in range(rows):
        for comp in range(3):
            stack_ref[row : row + 1, comp * width : (comp + 1) * width] = waves_ref[
                comp : comp + 1, row * width : (row + 1) * width
            ].astype(F32)
    counts = count_waves(stack_ref, rows, width)
    for row in range(0, COUNT_ROWS, 8):
        out_ref[:, 16 * row : 16 * row + 128] = counts[row : row + 8]


def sums_kernel(plan, *refs):
    refs = list(refs)
    base_ref = refs.pop(0) if plan["has_base"] else None
    ion_refs = [refs.pop(0) for _ in plan["chunks"]]
    table_ref = refs.pop(0)
    v_ref = refs.pop(0)
    half, cap, row_count = plan["half"], plan["cap"], plan["row_count"]
    block = half + 128
    per_pack = 64 // cap
    device = lax.axis_index("blk") * row_count + lax.axis_index("row")
    targets = (device, device ^ row_count)
    kept = slice(ARRIVE_AT, table_ref.shape[0])
    table_ref[kept] = jnp.zeros_like(table_ref[kept]) if base_ref is None else base_ref[kept]

    for ions_ref, (owners, first_owner) in zip(ion_refs, plan["chunks"]):
        if owners <= 4 and per_pack == 1:
            for owner in range(0, owners, 2):
                group = []
                for i in range(owner, min(owner + 2, owners)):
                    block_rows = ions_ref[:, i * block : (i + 1) * block]
                    group.append(owner_rows(block_rows, half))
                    add_arrivals(block_rows, group[-1], half, cap, 0.0, first_owner + i, targets, table_ref)
                add_owners(group, base_ref, table_ref, v_ref)
                base_ref = table_ref
        else:
            if base_ref is not table_ref:
                sums = slice(0, ARRIVE_AT)
                table_ref[sums] = jnp.zeros_like(table_ref[sums]) if base_ref is None else base_ref[sums]
                base_ref = table_ref

            def step(owner, carry, ions_ref=ions_ref, first_owner=first_owner):
                begin = pl.multiple_of(owner * block, 128)
                index = first_owner + owner
                place = (lax.rem(index, per_pack) * cap).astype(F32)
                block_rows = ions_ref[:, pl.ds(begin, block)]
                ions = owner_rows(block_rows, half)
                add_arrivals(block_rows, ions, half, cap, place, index // per_pack, targets, table_ref)
                add_owners([ions], table_ref, table_ref, v_ref)
                return carry

            lax.fori_loop(0, owners, step, 0)


SLOPE_X, BASIS_Y, SLOPE_Y, BASIS_ROWS = 24, 48, 80, 112


def store_bases(ions, basis_ref, z_ref):
    count = ions.shape[1]
    basis_x = first_basis(ions[0:1])
    basis_y = second_basis(ions[1:2])
    parts = basis_x + first_slopes(basis_x) + basis_y + second_slopes(basis_y)
    for i, part in enumerate(parts):
        basis_ref[8 * i : 8 * i + 8] = part
    plain = third_basis(ions[2:3])
    harm = lax.broadcasted_iota(jnp.int32, (HARM, count), 0).astype(F32) + 1.0
    slope = jnp.concatenate([-harm * plain[HARM:], harm * plain[:HARM]], axis=0)
    for i, table in enumerate((plain, slope)):
        high, low = split_two(table)
        z_ref[:, i * count : (i + 1) * count] = jnp.concatenate(
            [high, low, high, jnp.zeros((256 - 6 * HARM, count), BF16)], axis=0
        )


def own_kernel(half, cap, row_count, bits, data_ref, recv_ref, basis_ref, z_ref, hot_ref, gain_ref):
    store_bases(jnp.concatenate([data_ref[0:4, 0:half], data_ref[4:8, 0:half]], axis=1), basis_ref, z_ref)
    atoms_dev = recv_ref.shape[0]
    device = lax.axis_index("blk") * row_count + lax.axis_index("row")
    key = key_of_rows(recv_ref[...].reshape(1, atoms_dev), device, cap, row_count, bits)
    spot = lax.broadcasted_iota(jnp.int32, hot_ref.shape, 0)
    hot_ref[...] = jnp.where(spot == key, 1.0, 0.0).astype(BF16)
    gain_ref[...] = dense_weights()


def swap(parts):
    return [parts[1], parts[0], pltpu.roll(parts[2], 4, 0)]


def store_coefs(part, gain_ref, count_refs, coef_ref):
    lane = lax.broadcasted_iota(jnp.int32, (8, 128), 1)
    is_cos = lane < HARM
    is_wave = lane < 2 * HARM

    def gains(row):
        at = COUNT_AT[part] + row
        lanes = slice(16 * at, 16 * at + 128)
        tile = (count_refs[0][:, lanes] + count_refs[1][:, lanes]) * gain_ref[at : at + 8]
        back, far = pltpu.roll(tile, 88, 1), pltpu.roll(tile, 48, 1)
        pairs = ((tile, pltpu.roll(tile, HARM, 1)), (back, tile), (far, back))
        return [jnp.where(is_cos, a, jnp.where(is_wave, b, 0.0)) for a, b in pairs]

    order = ORDERS[part]
    pairs = {}
    for i, name in enumerate(order):
        gain = gains(8 * i)
        other = swap(gain)
        pairs[name] = [a + b for a, b in zip(gain, other)], [a - b for a, b in zip(gain, other)]
    for i, (harmonic, sine) in enumerate(order):
        both, odd = pairs[(harmonic, sine)]
        both_o, odd_o = pairs.get((harmonic, 1 - sine), (None, None))
        for x in range(3):
            row = FORCE_AT[part] + BASIS * i + 8 * x
            if both_o is None:
                coefs = (both[x], odd[x])
            else:
                coefs = (both[x] + both_o[x], odd[x] + odd_o[x], both[x] - both_o[x], odd[x] - odd_o[x])
            for kind, coef in enumerate(coefs):
                coef_ref[kind, row : row + 8] = coef
    tails = [gains(COUNT_LEN[part] - 16 + 8 * sine)[0] for sine in range(2)]
    for sine in range(2):
        row = FORCE_AT[part] + BASIS * len(order) + 8 * sine
        coef_ref[0, row : row + 8] = tails[sine] + tails[1 - sine]
        coef_ref[2, row : row + 8] = tails[sine] - tails[1 - sine]


def coef_kernel(gain_ref, count_ref, other_count_ref, coef_ref):
    for part in range(2):
        store_coefs(part, gain_ref, (count_ref, other_count_ref), coef_ref)


def weighted_sums(part, mine_ref, other_ref, coef_ref, w_ref):
    lane = lax.broadcasted_iota(jnp.int32, (8, 128), 1)
    is_cos = lane < HARM
    is_wave = lane < 2 * HARM
    count = SUM_ROWS[part]

    def both(row):
        row = PART_AT[part] + row
        return mine_ref[row : row + 8] + other_ref[row : row + 8]

    def blocks(row):
        near, far = both(row), both(count + row)
        middle = jnp.where(lane < 48, pltpu.roll(near, 48, 1), pltpu.roll(far, 48, 1))
        return [jnp.where(is_wave, value, 0.0) for value in (near, middle, pltpu.roll(far, 96, 1))]

    def turn(sums):
        return jnp.where(is_cos, pltpu.roll(sums, 88, 1), -pltpu.roll(sums, HARM, 1))

    def harmonics_of(stem):
        found = {}
        for harmonic, _ in STEMS[part]:
            if harmonic == 0:
                plain, cos_1, sin_1 = stem[(0, 0)]
                found.update({(0, 0): plain, (1, 0): cos_1, (1, 1): sin_1})
                continue
            cos, sin = stem[(harmonic, 0)], stem[(harmonic, 1)]
            found[(harmonic, 0)], found[(harmonic, 1)] = cos[0], sin[0]
            found[(harmonic - 1, 0)] = cos[1] + sin[2]
            found[(harmonic - 1, 1)] = sin[1] - cos[2]
            found[(harmonic + 1, 0)] = cos[1] - sin[2]
            found[(harmonic + 1, 1)] = sin[1] + cos[2]
        return found

    def store(row, value):
        high, low = split_two(value)
        high = high.astype(F32)
        low = low.astype(F32)
        turned = pltpu.roll(high, 2 * HARM, 1)
        row = FORCE_AT[part] + row
        w_ref[row : row + 8, 0:128] = jnp.where(is_wave, high, turned)
        w_ref[row : row + 8, 128:256] = jnp.where(lane < 32, turned, pltpu.roll(low, 32, 1))

    by_block = [
        harmonics_of({stem: blocks(BASIS * i + 8 * x) for i, stem in enumerate(STEMS[part])}) for x in range(3)
    ]
    order = ORDERS[part]
    groups = {}
    for name in order:
        sums = [by_block[x][name] for x in range(3)]
        turned = [turn(value) for value in sums]
        groups[name] = swap(sums), turned, swap(turned)
    for i, (harmonic, sine) in enumerate(order):
        turned_s = groups[(harmonic, sine)][2]
        for x in range(3):
            row = BASIS * i + 8 * x
            coefs = [coef_ref[kind, FORCE_AT[part] + row : FORCE_AT[part] + row + 8] for kind in range(4)]
            value = coefs[0] * by_block[x][(harmonic, sine)] - coefs[1] * turned_s[x]
            if harmonic:
                sums_os, turned_o, _ = groups[(harmonic, 1 - sine)]
                value = value - coefs[2] * turned_o[x] - coefs[3] * sums_os[x]
            store(row, value)
    tails = [blocks(BASIS * len(STEMS[part]) + 8 * sine) for sine in range(2)]
    found = harmonics_of({(h, sine): [b[h % 8 : h % 8 + 1] for b in tails[sine]] for h, sine in STEMS[part]})
    index = lax.broadcasted_iota(jnp.int32, (8, 128), 0)
    kinds = []
    for sine in range(2):
        rows = jnp.zeros((8, 128), F32)
        for harmonic, kind in order:
            if kind == sine:
                rows = jnp.where(index == harmonic % 8, found[(harmonic, kind)], rows)
        kinds.append((rows, turn(rows)))
    at = BASIS * len(order)
    for sine in range(2):
        row = FORCE_AT[part] + at + 8 * sine
        store(at + 8 * sine, coef_ref[0, row : row + 8] * kinds[sine][0] - coef_ref[2, row : row + 8] * kinds[1 - sine][1])
    if at + 16 < FORCE_ROWS[part]:
        fill = FORCE_ROWS[part] - at - 16
        w_ref[FORCE_AT[part] + at + 16 : FORCE_AT[part] + FORCE_ROWS[part]] = jnp.zeros((fill, 256), F32)


def pull(weights, basis_ref, z_ref, count, begin, tile):
    lanes = slice(begin, begin + tile)
    plain = jnp.dot(weights, z_ref[:, begin : begin + tile], preferred_element_type=F32)
    sloped = jnp.dot(weights, z_ref[:, count + begin : count + begin + tile], preferred_element_type=F32)
    zero = jnp.zeros((8, tile), F32)
    even, slope, third = [zero] * 3, [zero] * 3, [zero] * 3
    sum_y = sum_z = zero
    for part in range(2):
        for place, (harmonic, sine) in enumerate(ORDERS[part]):
            at = 16 * (harmonic // 8) + 8 * sine + harmonic % 8
            basis = basis_ref[BASIS_Y + at : BASIS_Y + at + 1, lanes]
            basis_slope = basis_ref[SLOPE_Y + at : SLOPE_Y + at + 1, lanes]
            for i in range(3):
                row = FORCE_AT[part] + BASIS * place + 8 * i
                plain_rows, sloped_rows = plain[row : row + 8], sloped[row : row + 8]
                if harmonic == 0:
                    even[i] = even[i] + plain_rows
                    third[i] = third[i] + sloped_rows
                else:
                    even[i] = even[i] + basis * plain_rows
                    slope[i] = slope[i] + basis_slope * plain_rows
                    third[i] = third[i] + basis * sloped_rows
        for sine in range(2):
            row = FORCE_AT[part] + BASIS * len(ORDERS[part]) + 8 * sine
            at = 16 * part + 8 * sine
            sum_y = sum_y + basis_ref[SLOPE_Y + at : SLOPE_Y + at + 8, lanes] * plain[row : row + 8]
            sum_z = sum_z + basis_ref[BASIS_Y + at : BASIS_Y + at + 8, lanes] * sloped[row : row + 8]
    sum_x = zero
    for i in range(3):
        rows_x = basis_ref[8 * i : 8 * i + 8, lanes]
        sum_x = sum_x + basis_ref[SLOPE_X + 8 * i : SLOPE_X + 8 * i + 8, lanes] * even[i]
        sum_y = sum_y + rows_x * slope[i]
        sum_z = sum_z + rows_x * third[i]
    return [jnp.sum(value, axis=0, keepdims=True) for value in (sum_x, sum_y, sum_z)]


TILE = 256


def force_kernel(
    force_scale, half, mine_ref, other_ref, data_ref, basis_ref, z_ref, hot_ref, coef_ref,
    slot_ref, atom_ref, w_ref, atom_basis_ref, atom_z_ref,
):
    packs = hot_ref.shape[0] // 128
    lane = lax.broadcasted_iota(jnp.int32, (8, 128), 1)
    starts = [ARRIVE_AT + 8 * p for p in range(packs)]
    pool = jnp.concatenate([jnp.where(lane < 64, mine_ref[r : r + 8], other_ref[r : r + 8]) for r in starts], axis=1)
    found = jnp.dot(split_three(pool), hot_ref[...], preferred_element_type=F32)
    routed = ((found[0:8] + found[8:16]) + found[16:24])[0:4]
    for part in range(2):
        weighted_sums(part, mine_ref, other_ref, coef_ref, w_ref)
    weights = w_ref[...].astype(BF16)
    store_bases(routed, atom_basis_ref, atom_z_ref)
    charge = jnp.concatenate([data_ref[3:4, 0:half], data_ref[7:8, 0:half]], axis=1)
    jobs = ((basis_ref, z_ref, charge, slot_ref), (atom_basis_ref, atom_z_ref, routed[3:4], atom_ref))
    for rows_ref, table_ref, charges, out_ref in jobs:
        count = out_ref.shape[1]
        for begin in range(0, count, TILE):
            lanes = slice(begin, begin + TILE)
            gain = (-DOUBLE_PI * force_scale) * charges[:, lanes]
            gains = (gain, gain, gain / BOX_Z)
            found = pull(weights, rows_ref, table_ref, count, begin, TILE)
            out_ref[:, lanes] = jnp.concatenate([gains[i] * found[i] for i in range(3)], axis=0)


def params():
    return pltpu.CompilerParams(vmem_limit_bytes=VMEM_BYTES)


def stay(value):
    return pltpu.with_memory_space_constraint(value, pltpu.HBM)


def whole(count):
    return [pl.BlockSpec(memory_space=pltpu.VMEM)] * count


def body(coords, charges, counts, send_slot, recv_index, wave_ints):
    slots = charges.shape[0]
    half = slots // 2
    block = half + 128
    atoms_dev = recv_index.shape[0]
    devices = lax.axis_size(("blk", "row"))
    blk_count = lax.axis_size("blk")
    row_count = lax.axis_size("row")
    k_local = wave_ints.shape[1]
    cap = 2 * atoms_dev // devices
    packs = max(1, devices // 2 * cap // 64)
    per_pack = 64 // cap
    wave_rows, wave_width = wave_shape(k_local)
    force_scale = FORCE_GAIN / math.sqrt(float(atoms_dev * devices * blk_count * k_local))
    table_shape = jax.ShapeDtypeStruct((ARRIVE_AT + 8 * packs, 128), F32)
    count_shape = jax.ShapeDtypeStruct((8, 16 * COUNT_ROWS), F32)

    with jax.named_scope("payload"):
        own_ions = pl.pallas_call(
            prep_kernel,
            out_shape=jax.ShapeDtypeStruct((8, block), F32),
            in_specs=[pl.BlockSpec(memory_space=pltpu.HBM)] * 4,
            out_specs=whole(1)[0],
            scratch_shapes=[
                pltpu.VMEM(coords.shape, F32),
                pltpu.VMEM(charges.shape, F32),
                pltpu.SMEM(counts.shape, jnp.int32),
                pltpu.VMEM(send_slot.shape, jnp.int32),
                pltpu.SemaphoreType.DMA((4,)),
            ],
            compiler_params=params(),
        )(stay(coords), stay(charges), counts, stay(send_slot))

    def flip(value, blk_bit, row_bit):
        if not row_bit:
            return lax.ppermute(value, "blk", [(i, i ^ blk_bit) for i in range(blk_count)])
        if not blk_bit:
            return lax.ppermute(value, "row", [(i, i ^ row_bit) for i in range(row_count)])
        distance = row_count * blk_bit + row_bit
        return lax.ppermute(value, ("blk", "row"), [(i, i ^ distance) for i in range(devices)])

    def joined(values):
        return values[0] if len(values) == 1 else jnp.concatenate(values, axis=1)

    def accumulate(table, chunks, cost=1):
        plan = {
            "has_base": table is not None,
            "chunks": [chunk[1:] for chunk in chunks],
            "half": half,
            "cap": cap,
            "row_count": row_count,
        }
        args = [table] * plan["has_base"] + [chunk[0] for chunk in chunks]
        flops = int(cost * 2 * sum(chunk[1] for chunk in chunks) * slots * 256 * 720)
        with jax.named_scope("structure_sums"):
            return pl.pallas_call(
                functools.partial(sums_kernel, plan),
                out_shape=table_shape,
                in_specs=whole(len(args)),
                out_specs=whole(1)[0],
                scratch_shapes=[pltpu.VMEM((2 * sum(SUM_ROWS), 2 * slots), BF16)],
                compiler_params=params(),
                cost_estimate=pl.CostEstimate(flops=flops, bytes_accessed=1 << 20, transcendentals=0),
            )(*args)

    steps = []
    bit = row_count // 2
    while bit >= 2:
        steps.append((0, bit))
        bit //= 2
    bit = 4
    while bit < blk_count:
        steps.append((bit, 0))
        bit *= 2
    bits = [row_count * blk_bit + row_bit for blk_bit, row_bit in steps] + [2 * row_count, 1]
    table, counted = None, None
    ions, held, chunks = [own_ions], 1, [(own_ions, 1, 0)]
    for blk_bit, row_bit in steps:
        with jax.named_scope("exchange_ions"):
            got = flip(joined(ions), blk_bit, row_bit)
        if blk_bit:
            with jax.named_scope("exchange_counts"):
                counted = counted + flip(counted, blk_bit, 0)
        if counted is None:
            with jax.named_scope("counts"):
                counted = pl.pallas_call(
                    functools.partial(count_kernel, wave_rows, wave_width),
                    out_shape=count_shape,
                    in_specs=[pl.BlockSpec(memory_space=pltpu.HBM)],
                    out_specs=whole(1)[0],
                    scratch_shapes=[
                        pltpu.VMEM(wave_ints.shape, jnp.int32),
                        pltpu.VMEM((wave_rows, 3 * wave_width), F32),
                        pltpu.SemaphoreType.DMA,
                    ],
                    compiler_params=params(),
                    cost_estimate=pl.CostEstimate(
                        flops=2 * k_local * COUNT_ROWS * 128, bytes_accessed=1 << 20, transcendentals=0
                    ),
                )(stay(wave_ints))
            got, counted = lax.optimization_barrier((got, counted))
        else:
            table, chunks = accumulate(table, chunks), []
            got, table = lax.optimization_barrier((got, table))
        chunks = chunks + [(got, held, held)]
        ions = ions + [got]
        held *= 2
    with jax.named_scope("exchange_ions"):
        sent = joined(ions)
        across = flip(jnp.concatenate([sent, counted], axis=1), 2, 0)
        along = flip(sent, 0, 1)
        corner = flip(sent, 2, 1)
    table = accumulate(table, chunks)
    own_ions, recv_index, table = lax.optimization_barrier((own_ions, recv_index, table))
    with jax.named_scope("own_ions"):
        basis, table_z, hot, gain = pl.pallas_call(
            functools.partial(own_kernel, half, cap, row_count, bits),
            out_shape=(
                jax.ShapeDtypeStruct((BASIS_ROWS, slots), F32),
                jax.ShapeDtypeStruct((256, 2 * slots), BF16),
                jax.ShapeDtypeStruct((128 * packs, atoms_dev), BF16),
                jax.ShapeDtypeStruct((COUNT_ROWS, 128), F32),
            ),
            in_specs=whole(2),
            out_specs=tuple(whole(4)),
            compiler_params=params(),
            cost_estimate=pl.CostEstimate(flops=1<<22, bytes_accessed=1 << 20, transcendentals=0),
        )(own_ions, recv_index)
    along, table, basis, table_z, hot, gain = lax.optimization_barrier((along, table, basis, table_z, hot, gain))
    table = accumulate(table, [(along, held, 2 * held)], cost=0.05)
    table = accumulate(table, [(across, held, held)], cost=0.05)
    with jax.named_scope("exchange_core"):
        counted = counted + across[:, held * block :]
        other_counted = flip(counted, 1, 0)
    corner, table, counted = lax.optimization_barrier((corner, table, counted))
    table = accumulate(table, [(corner, held, 3 * held)], cost=16)
    with jax.named_scope("exchange_core"):
        other = flip(table, 1, 0)
    with jax.named_scope("coefficients"):
        coefs = pl.pallas_call(
            coef_kernel,
            out_shape=jax.ShapeDtypeStruct((4, sum(FORCE_ROWS), 128), F32),
            in_specs=whole(3),
            out_specs=whole(1)[0],
            compiler_params=params(),
            cost_estimate=pl.CostEstimate(flops=1<<33, bytes_accessed=1 << 20, transcendentals=0),
        )(gain, counted, other_counted)
    with jax.named_scope("forces"):
        return pl.pallas_call(
            functools.partial(force_kernel, force_scale, half),
            out_shape=(
                jax.ShapeDtypeStruct((3, slots), F32),
                jax.ShapeDtypeStruct((3, atoms_dev), F32),
            ),
            in_specs=whole(7),
            out_specs=tuple(whole(2)),
            scratch_shapes=[
                pltpu.VMEM((sum(FORCE_ROWS), 256), F32),
                pltpu.VMEM((BASIS_ROWS, atoms_dev), F32),
                pltpu.VMEM((256, 2 * atoms_dev), BF16),
            ],
            compiler_params=params(),
        )(table, other, own_ions, basis, table_z, hot, coefs)


def solution(mesh):
    placed = (
        P(None, ("groups", "blk", "row")),
        P(("groups", "blk", "row")),
        P(("groups", "blk", "row")),
        P(("groups", "blk", "row")),
        P(("groups", "blk", "row")),
        P(None, "blk"),
    )
    return jax.shard_map(
        body,
        mesh=mesh,
        in_specs=placed,
        out_specs=(P(None, ("groups", "blk", "row")), P(None, ("groups", "blk", "row"))),
        check_vma=False,
    )
```

```python
import functools
import math

import jax
import jax.numpy as jnp
from jax import lax
from jax.experimental import pallas as pl
from jax.experimental.pallas import tpu as pltpu
from jax.sharding import PartitionSpec as P

DOUBLE_PI = 2.0 * math.pi
EWALD_BETA = 30.0
BOX_Z = 3.0
FORCE_GAIN = 400.0
SIN_POLY = (6.283185, -41.34159, 81.599945, -76.61447, 41.342884, -12.471244)
COS_POLY = (1.0, -19.739204, 64.93912, -85.45014, 60.16763, -25.9676, 6.5286584)

BASIS = 24
HARM = 40
STEMS = (((0, 0), (3, 0), (3, 1), (6, 0), (6, 1)), ((9, 0), (9, 1), (12, 0), (12, 1)))
SUM_ROWS = (128, 112)
ORDERS = (
    tuple((k, 0) for k in range(8)) + tuple((k, 1) for k in range(1, 8)),
    tuple((k, 0) for k in range(8, 13)) + tuple((k, 1) for k in range(8, 13)),
)
COUNT_ROWS = 240
COUNT_AT = (0, 136)
COUNT_LEN = (136, 96)
FORCE_ROWS = (384, 256)
FORCE_AT = (0, 384)
PART_AT = (0, 2 * SUM_ROWS[0])
ARRIVE_AT = PART_AT[1] + 2 * SUM_ROWS[1]
F32 = jnp.float32
BF16 = jnp.bfloat16
NT = (((1,), (1,)), ((), ()))
VMEM_BYTES = 40 * 1024 * 1024


def horner(coefs, v):
    total = jnp.full_like(v, coefs[-1])
    for coef in coefs[-2::-1]:
        total = total * v + coef
    return total


def harmonics(pos, first):
    harm = lax.broadcasted_iota(jnp.int32, (8, pos.shape[1]), 0).astype(F32) + float(first)
    turns = harm * pos
    turns = turns - jnp.floor(turns + 0.5)
    square = turns * turns
    return horner(COS_POLY, square), turns * horner(SIN_POLY, square)


def advance(first, by):
    cos_a, sin_a = first
    cos_b, sin_b = by
    return cos_a * cos_b - sin_a * sin_b, sin_a * cos_b + cos_a * sin_b


def row_of(pair, row):
    return pair[0][row : row + 1], pair[1][row : row + 1]


def merge_last(cos_part, sin_part):
    low = lax.broadcasted_iota(jnp.int32, cos_part.shape, 0) < 4
    return jnp.where(low, cos_part, pltpu.roll(sin_part, 4, 0))


def first_basis(pos):
    first = harmonics(pos, 1)
    second = advance(first, row_of(first, 7))
    return [first[0], first[1], merge_last(*second)]


def first_slopes(basis):
    row = lax.broadcasted_iota(jnp.int32, basis[0].shape, 0)
    harm = row.astype(F32) + 1.0
    low = row < 4
    factor = jnp.where(low, -(harm + 8.0), harm + 4.0)
    return [-harm * basis[1], harm * basis[0], factor * pltpu.roll(basis[2], 4, 0)]


def second_basis(pos):
    first = harmonics(pos, 0)
    fourth = row_of(first, 4)
    second = advance(first, advance(fourth, fourth))
    return [first[0], first[1], second[0], second[1]]


def second_slopes(basis):
    harm = lax.broadcasted_iota(jnp.int32, basis[0].shape, 0).astype(F32)
    high = harm + 8.0
    return [-harm * basis[1], harm * basis[0], -high * basis[3], high * basis[2]]


def second_row(basis, harmonic, sine):
    return basis[2 * (harmonic // 8) + sine][harmonic % 8 : harmonic % 8 + 1]


def third_basis(pos):
    first = harmonics(pos, 1)
    second = advance(first, row_of(first, 7))
    third = advance(first, row_of(second, 7))
    fourth = advance(second, row_of(second, 7))
    fifth = advance(first, row_of(fourth, 7))
    parts = (first, second, third, fourth, fifth)
    return jnp.concatenate([p[0] for p in parts] + [p[1] for p in parts], axis=0)


def split_two(value):
    high = value.astype(BF16)
    return high, (value - high.astype(F32)).astype(BF16)


def key_of_rows(recv, device, cap, row_count, bits):
    per_pack = 64 // cap
    source = (recv // cap) ^ device
    order = jnp.zeros_like(source)
    for place, distance in enumerate(bits):
        order = order | jnp.where((source & distance) != 0, 1 << place, 0)
    far = jnp.where((source & row_count) != 0, 64, 0)
    return (order // per_pack) * 128 + far + (order % per_pack) * cap + recv % cap


def prep_kernel(
    coords_hbm, charges_hbm, counts_hbm, send_hbm, out_ref, coords_ref, charges_ref, counts_ref, send_ref, sems
):
    copies = [
        pltpu.make_async_copy(source, target, sems.at[i])
        for i, (source, target) in enumerate(
            (
                (counts_hbm, counts_ref),
                (send_hbm, send_ref),
                (charges_hbm, charges_ref),
                (coords_hbm, coords_ref),
            )
        )
    ]
    for copy in copies:
        copy.start()
    slots = charges_ref.shape[0]
    half = slots // 2
    out_ref[:, 0 : half + 128] = jnp.zeros((8, half + 128), F32)
    for copy in copies:
        copy.wait()
    live = lax.broadcasted_iota(jnp.int32, (1, slots), 1) < counts_ref[0]
    charge = jnp.where(live, charges_ref[...].reshape(1, slots), 0.0)
    send = jnp.where(live, send_ref[...].reshape(1, slots), -1).astype(F32)
    for part in range(2):
        lanes = slice(part * half, (part + 1) * half)
        out_ref[4 * part : 4 * part + 3, 0:half] = coords_ref[:, lanes]
        out_ref[4 * part + 3 : 4 * part + 4, 0:half] = charge[:, lanes]
    for piece in range(slots // 128):
        out_ref[piece : piece + 1, half : half + 128] = send[:, piece * 128 : (piece + 1) * 128]


def wave_shape(k_local):
    rows = 8
    while k_local % (rows * 128):
        rows //= 2
    return rows, k_local // rows


def basis_row(index):
    size = jnp.abs(index)
    sign = jnp.where(index < 0.0, 1.0, 0.0)
    row = jnp.where(size <= 8.0, size - 1.0 + 8.0 * sign, size + 7.0 + 4.0 * sign)
    return jnp.where(size == 0.0, float(BASIS), row)


def basis_size(row):
    low = jnp.where(row < 8, row, row - 8) + 1
    high = jnp.where(row < 20, row - 16, row - 20) + 9
    return jnp.where(row < 16, low, jnp.where(row < BASIS, high, 0))


def dense_weights():
    row = lax.broadcasted_iota(jnp.int32, (COUNT_ROWS, 128), 0)
    lane = lax.broadcasted_iota(jnp.int32, (COUNT_ROWS, 128), 1)
    early = row < COUNT_AT[1]
    own = jnp.where(early, row, row - COUNT_AT[1])
    paired = own < jnp.where(early, COUNT_LEN[0] - 16, COUNT_LEN[1] - 16)
    group = own // 8
    size_y = jnp.where(early, jnp.where(group < 8, group, group - 7), 8 + jnp.where(group < 5, group, group - 5))
    size_y = jnp.where(paired, size_y, jnp.where(early, own % 8, 8 + own % 8))
    part = jnp.where(lane < HARM, 0, jnp.where(lane < 2 * HARM, 1, 2))
    size_x = jnp.where(paired, basis_size(own % 8 + 8 * part), 0)
    phys_x = DOUBLE_PI * size_x.astype(F32)
    phys_y = DOUBLE_PI * size_y.astype(F32)
    phys_z = DOUBLE_PI * (lane - HARM * part + 1).astype(F32) / BOX_Z
    k_squared = phys_x * phys_x + phys_y * phys_y + phys_z * phys_z
    return jnp.exp(-k_squared / (4.0 * EWALD_BETA * EWALD_BETA)) / k_squared


def count_waves(waves, rows, width):
    wave_h = waves[0:rows, 0:width]
    wave_k = waves[0:rows, width : 2 * width]
    wave_l = waves[0:rows, 2 * width : 3 * width]
    flip = jnp.where(wave_l < 0.0, -1.0, 1.0)
    row_x = basis_row(wave_h * flip)
    wave_k = wave_k * flip
    size_y = jnp.abs(wave_k)
    sine = jnp.where(wave_k < 0.0, 1.0, 0.0)
    const = row_x == float(BASIS)
    part = jnp.where(row_x >= 16.0, 2.0, jnp.where(row_x >= 8.0, 1.0, 0.0))
    part = jnp.where(const, 0.0, part)
    late = size_y >= 8.0
    group = jnp.where(late, size_y - 8.0 + 5.0 * sine, size_y + 7.0 * sine)
    paired_id = 8.0 * group + (row_x - 8.0 * part) + jnp.where(late, float(COUNT_AT[1]), 0.0)
    tail = jnp.where(late, size_y - 8.0 + float(COUNT_AT[1] + COUNT_LEN[1] - 16), size_y + float(COUNT_LEN[0] - 16))
    row_id = jnp.where(const, tail + 8.0 * sine, paired_id)
    lane_id = wave_l * flip + (HARM * part - 1.0)
    step = lax.broadcasted_iota(jnp.int32, (16, width), 0).astype(F32)
    steps = [(step + 16.0 * i).astype(BF16) for i in range(COUNT_ROWS // 16)]
    one = jnp.ones((16, width), BF16)
    none = jnp.zeros((16, width), BF16)
    total = None
    for piece in range(rows):
        rows_at = jnp.broadcast_to(row_id[piece : piece + 1], (16, width)).astype(BF16)
        lanes_at = jnp.broadcast_to(lane_id[piece : piece + 1], (16, width)).astype(BF16)
        row_hot = jnp.concatenate([jnp.where(rows_at == at, one, none) for at in steps], axis=0)
        lane_hot = jnp.concatenate([jnp.where(lanes_at == at, one, none) for at in steps[:8]], axis=0)
        found = lax.dot_general(row_hot, lane_hot, NT, preferred_element_type=F32)
        total = found if total is None else total + found
    return total


def owner_rows(block_rows, half):
    return [
        jnp.concatenate([block_rows[i : i + 1, 0:half], block_rows[i + 4 : i + 5, 0:half]], axis=1) for i in range(4)
    ]


def owner_tables(rows):
    pos_x, pos_y, pos_z, charge = rows
    basis_x = jnp.concatenate([charge * part for part in first_basis(pos_x)], axis=0)
    basis_y = second_basis(pos_y)
    third = third_basis(pos_z)
    lanes = jnp.concatenate([third, third * basis_y[0][1:2], third * basis_y[1][1:2]], axis=0)
    high, low = split_two(lanes)
    gap = jnp.zeros((256 - 6 * HARM, third.shape[1]), BF16)
    high = jnp.concatenate([high, gap], axis=0)
    low = jnp.concatenate([low, gap], axis=0)
    return basis_x, basis_y, high, low


def stem_rows(part, basis_y):
    return [second_row(basis_y, harmonic, sine) for harmonic, sine in STEMS[part]]


def store_rows(basis_x, basis_y, charge, v_ref):
    all_rows = sum(SUM_ROWS)
    slots = charge.shape[1]
    at = 0
    for part in range(2):
        stems = stem_rows(part, basis_y)
        index = lax.broadcasted_iota(jnp.int32, (8, slots), 0)
        sines = [index == harmonic % 8 + 1 for harmonic, sine in STEMS[part] if sine]
        tail = jnp.where(jnp.logical_or(*sines), pltpu.roll(basis_y[2 * part + 1], 1, 0), basis_y[2 * part])
        rows = [stem * basis_x for stem in stems] + [charge * tail]
        fill = SUM_ROWS[part] - BASIS * len(stems) - 8
        if fill:
            rows.append(jnp.zeros((fill, slots), F32))
        rows = jnp.concatenate(rows, axis=0)
        for begin in range(0, SUM_ROWS[part], 16):
            high, low = split_two(rows[begin : begin + 16])
            v_ref[at : at + 16] = high
            v_ref[all_rows + at : all_rows + at + 16] = low
            at += 16


def add_owners(owners, base_ref, table_ref, v_ref):
    all_rows = sum(SUM_ROWS)
    highs, lows = [], []
    for i, ions in enumerate(owners):
        slots = ions[3].shape[1]
        basis_x, basis_y, high, low = owner_tables(ions)
        store_rows(basis_x, basis_y, ions[3], v_ref.at[:, i * slots : (i + 1) * slots])
        highs.append(high)
        lows.append(low)
    width = sum(high.shape[1] for high in highs)
    both = lax.dot_general(v_ref[:, 0:width], jnp.concatenate(highs, axis=1), NT, preferred_element_type=F32)
    rest = lax.dot_general(v_ref[0:all_rows, 0:width], jnp.concatenate(lows, axis=1), NT, preferred_element_type=F32)
    total = (both[:all_rows] + both[all_rows:]) + rest
    at = 0
    for part in range(2):
        count, begin = SUM_ROWS[part], PART_AT[part]
        for half in range(2):
            rows = slice(begin + half * count, begin + (half + 1) * count)
            value = total[at : at + count, 128 * half : 128 * half + 128]
            table_ref[rows] = value if base_ref is None else base_ref[rows] + value
        at += count


def add_arrivals(block_rows, rows, half, cap, place, pack, targets, table_ref):
    block = half + 128
    slots = 2 * half
    send = jnp.concatenate([block_rows[p : p + 1, half:block] for p in range(slots // 128)], axis=1)
    step = lax.broadcasted_iota(jnp.int32, (16, slots), 0).astype(F32)
    one, none = jnp.ones((16, slots), BF16), jnp.zeros((16, slots), BF16)
    hots = []
    for target in targets:
        rank = send - (target * cap).astype(F32)
        valid = jnp.logical_and(rank >= 0.0, rank < float(cap))
        key = jnp.broadcast_to(jnp.where(valid, rank + place, -1.0), (16, slots)).astype(BF16)
        hots += [jnp.where(key == (step + 16.0 * i).astype(BF16), one, none) for i in range(4)]
    values = jnp.concatenate(rows + [jnp.zeros((4, slots), F32)], axis=0)
    found = lax.dot_general(split_three(values), jnp.concatenate(hots, axis=0), NT, preferred_element_type=F32)
    row = ARRIVE_AT + 8 * pack
    if not isinstance(row, int):
        row = pl.multiple_of(row, 8)
    table_ref[pl.ds(row, 8)] += (found[0:8] + found[8:16]) + found[16:24]


def split_three(value):
    high = value.astype(BF16).astype(F32)
    rest = value - high
    mid = rest.astype(BF16).astype(F32)
    return jnp.concatenate([high, mid, rest - mid], axis=0).astype(BF16)


def count_kernel(rows, width, waves_hbm, out_ref, waves_ref, stack_ref, sem):
    copy = pltpu.make_async_copy(waves_hbm, waves_ref, sem)
    copy.start()
    copy.wait()
    for row in range(rows):
        for comp in range(3):
            stack_ref[row : row + 1, comp * width : (comp + 1) * width] = waves_ref[
                comp : comp + 1, row * width : (row + 1) * width
            ].astype(F32)
    counts = count_waves(stack_ref, rows, width)
    for row in range(0, COUNT_ROWS, 8):
        out_ref[:, 16 * row : 16 * row + 128] = counts[row : row + 8]


def sums_kernel(plan, *refs):
    refs = list(refs)
    base_ref = refs.pop(0) if plan["has_base"] else None
    ion_refs = [refs.pop(0) for _ in plan["chunks"]]
    table_ref = refs.pop(0)
    v_ref = refs.pop(0)
    half, cap, row_count = plan["half"], plan["cap"], plan["row_count"]
    block = half + 128
    per_pack = 64 // cap
    device = lax.axis_index("blk") * row_count + lax.axis_index("row")
    targets = (device, device ^ row_count)
    kept = slice(ARRIVE_AT, table_ref.shape[0])
    table_ref[kept] = jnp.zeros_like(table_ref[kept]) if base_ref is None else base_ref[kept]

    for ions_ref, (owners, first_owner) in zip(ion_refs, plan["chunks"]):
        if owners <= 4 and per_pack == 1:
            for owner in range(0, owners, 2):
                group = []
                for i in range(owner, min(owner + 2, owners)):
                    block_rows = ions_ref[:, i * block : (i + 1) * block]
                    group.append(owner_rows(block_rows, half))
                    add_arrivals(block_rows, group[-1], half, cap, 0.0, first_owner + i, targets, table_ref)
                add_owners(group, base_ref, table_ref, v_ref)
                base_ref = table_ref
        else:
            if base_ref is not table_ref:
                sums = slice(0, ARRIVE_AT)
                table_ref[sums] = jnp.zeros_like(table_ref[sums]) if base_ref is None else base_ref[sums]
                base_ref = table_ref

            def step(owner, carry, ions_ref=ions_ref, first_owner=first_owner):
                begin = pl.multiple_of(owner * block, 128)
                index = first_owner + owner
                place = (lax.rem(index, per_pack) * cap).astype(F32)
                block_rows = ions_ref[:, pl.ds(begin, block)]
                ions = owner_rows(block_rows, half)
                add_arrivals(block_rows, ions, half, cap, place, index // per_pack, targets, table_ref)
                add_owners([ions], table_ref, table_ref, v_ref)
                return carry

            lax.fori_loop(0, owners, step, 0)


SLOPE_X, BASIS_Y, SLOPE_Y, BASIS_ROWS = 24, 48, 80, 112


def store_bases(ions, basis_ref, z_ref):
    count = ions.shape[1]
    basis_x = first_basis(ions[0:1])
    basis_y = second_basis(ions[1:2])
    parts = basis_x + first_slopes(basis_x) + basis_y + second_slopes(basis_y)
    for i, part in enumerate(parts):
        basis_ref[8 * i : 8 * i + 8] = part
    plain = third_basis(ions[2:3])
    harm = lax.broadcasted_iota(jnp.int32, (HARM, count), 0).astype(F32) + 1.0
    slope = jnp.concatenate([-harm * plain[HARM:], harm * plain[:HARM]], axis=0)
    for i, table in enumerate((plain, slope)):
        high, low = split_two(table)
        z_ref[:, i * count : (i + 1) * count] = jnp.concatenate(
            [high, low, high, jnp.zeros((256 - 6 * HARM, count), BF16)], axis=0
        )


def own_kernel(half, cap, row_count, bits, data_ref, recv_ref, basis_ref, z_ref, hot_ref, gain_ref):
    store_bases(jnp.concatenate([data_ref[0:4, 0:half], data_ref[4:8, 0:half]], axis=1), basis_ref, z_ref)
    atoms_dev = recv_ref.shape[0]
    device = lax.axis_index("blk") * row_count + lax.axis_index("row")
    key = key_of_rows(recv_ref[...].reshape(1, atoms_dev), device, cap, row_count, bits)
    spot = lax.broadcasted_iota(jnp.int32, hot_ref.shape, 0)
    hot_ref[...] = jnp.where(spot == key, 1.0, 0.0).astype(BF16)
    gain_ref[...] = dense_weights()


def swap(parts):
    return [parts[1], parts[0], pltpu.roll(parts[2], 4, 0)]


def store_coefs(part, gain_ref, count_refs, coef_ref):
    lane = lax.broadcasted_iota(jnp.int32, (8, 128), 1)
    is_cos = lane < HARM
    is_wave = lane < 2 * HARM

    def gains(row):
        at = COUNT_AT[part] + row
        lanes = slice(16 * at, 16 * at + 128)
        tile = (count_refs[0][:, lanes] + count_refs[1][:, lanes]) * gain_ref[at : at + 8]
        back, far = pltpu.roll(tile, 88, 1), pltpu.roll(tile, 48, 1)
        pairs = ((tile, pltpu.roll(tile, HARM, 1)), (back, tile), (far, back))
        return [jnp.where(is_cos, a, jnp.where(is_wave, b, 0.0)) for a, b in pairs]

    order = ORDERS[part]
    pairs = {}
    for i, name in enumerate(order):
        gain = gains(8 * i)
        other = swap(gain)
        pairs[name] = [a + b for a, b in zip(gain, other)], [a - b for a, b in zip(gain, other)]
    for i, (harmonic, sine) in enumerate(order):
        both, odd = pairs[(harmonic, sine)]
        both_o, odd_o = pairs.get((harmonic, 1 - sine), (None, None))
        for x in range(3):
            row = FORCE_AT[part] + BASIS * i + 8 * x
            if both_o is None:
                coefs = (both[x], odd[x])
            else:
                coefs = (both[x] + both_o[x], odd[x] + odd_o[x], both[x] - both_o[x], odd[x] - odd_o[x])
            for kind, coef in enumerate(coefs):
                coef_ref[kind, row : row + 8] = coef
    tails = [gains(COUNT_LEN[part] - 16 + 8 * sine)[0] for sine in range(2)]
    for sine in range(2):
        row = FORCE_AT[part] + BASIS * len(order) + 8 * sine
        coef_ref[0, row : row + 8] = tails[sine] + tails[1 - sine]
        coef_ref[2, row : row + 8] = tails[sine] - tails[1 - sine]


def coef_kernel(gain_ref, count_ref, other_count_ref, coef_ref):
    for part in range(2):
        store_coefs(part, gain_ref, (count_ref, other_count_ref), coef_ref)


def weighted_sums(part, mine_ref, other_ref, coef_ref, w_ref):
    lane = lax.broadcasted_iota(jnp.int32, (8, 128), 1)
    is_cos = lane < HARM
    is_wave = lane < 2 * HARM
    count = SUM_ROWS[part]

    def both(row):
        row = PART_AT[part] + row
        return mine_ref[row : row + 8] + other_ref[row : row + 8]

    def blocks(row):
        near, far = both(row), both(count + row)
        middle = jnp.where(lane < 48, pltpu.roll(near, 48, 1), pltpu.roll(far, 48, 1))
        return [jnp.where(is_wave, value, 0.0) for value in (near, middle, pltpu.roll(far, 96, 1))]

    def turn(sums):
        return jnp.where(is_cos, pltpu.roll(sums, 88, 1), -pltpu.roll(sums, HARM, 1))

    def harmonics_of(stem):
        found = {}
        for harmonic, _ in STEMS[part]:
            if harmonic == 0:
                plain, cos_1, sin_1 = stem[(0, 0)]
                found.update({(0, 0): plain, (1, 0): cos_1, (1, 1): sin_1})
                continue
            cos, sin = stem[(harmonic, 0)], stem[(harmonic, 1)]
            found[(harmonic, 0)], found[(harmonic, 1)] = cos[0], sin[0]
            found[(harmonic - 1, 0)] = cos[1] + sin[2]
            found[(harmonic - 1, 1)] = sin[1] - cos[2]
            found[(harmonic + 1, 0)] = cos[1] - sin[2]
            found[(harmonic + 1, 1)] = sin[1] + cos[2]
        return found

    def store(row, value):
        high, low = split_two(value)
        high = high.astype(F32)
        low = low.astype(F32)
        turned = pltpu.roll(high, 2 * HARM, 1)
        row = FORCE_AT[part] + row
        w_ref[row : row + 8, 0:128] = jnp.where(is_wave, high, turned)
        w_ref[row : row + 8, 128:256] = jnp.where(lane < 32, turned, pltpu.roll(low, 32, 1))

    by_block = [
        harmonics_of({stem: blocks(BASIS * i + 8 * x) for i, stem in enumerate(STEMS[part])}) for x in range(3)
    ]
    order = ORDERS[part]
    groups = {}
    for name in order:
        sums = [by_block[x][name] for x in range(3)]
        turned = [turn(value) for value in sums]
        groups[name] = swap(sums), turned, swap(turned)
    for i, (harmonic, sine) in enumerate(order):
        turned_s = groups[(harmonic, sine)][2]
        for x in range(3):
            row = BASIS * i + 8 * x
            coefs = [coef_ref[kind, FORCE_AT[part] + row : FORCE_AT[part] + row + 8] for kind in range(4)]
            value = coefs[0] * by_block[x][(harmonic, sine)] - coefs[1] * turned_s[x]
            if harmonic:
                sums_os, turned_o, _ = groups[(harmonic, 1 - sine)]
                value = value - coefs[2] * turned_o[x] - coefs[3] * sums_os[x]
            store(row, value)
    tail = blocks(BASIS * len(STEMS[part]))
    found = harmonics_of({(h, sine): [b[h % 8 + sine : h % 8 + sine + 1] for b in tail] for h, sine in STEMS[part]})
    index = lax.broadcasted_iota(jnp.int32, (8, 128), 0)
    kinds = []
    for sine in range(2):
        rows = jnp.zeros((8, 128), F32)
        for harmonic, kind in order:
            if kind == sine:
                rows = jnp.where(index == harmonic % 8, found[(harmonic, kind)], rows)
        kinds.append((rows, turn(rows)))
    at = BASIS * len(order)
    for sine in range(2):
        row = FORCE_AT[part] + at + 8 * sine
        store(at + 8 * sine, coef_ref[0, row : row + 8] * kinds[sine][0] - coef_ref[2, row : row + 8] * kinds[1 - sine][1])
    if at + 16 < FORCE_ROWS[part]:
        fill = FORCE_ROWS[part] - at - 16
        w_ref[FORCE_AT[part] + at + 16 : FORCE_AT[part] + FORCE_ROWS[part]] = jnp.zeros((fill, 256), F32)


def pull(weights, basis_ref, z_ref, count, begin, tile):
    lanes = slice(begin, begin + tile)
    plain = jnp.dot(weights, z_ref[:, begin : begin + tile], preferred_element_type=F32)
    sloped = jnp.dot(weights, z_ref[:, count + begin : count + begin + tile], preferred_element_type=F32)
    zero = jnp.zeros((8, tile), F32)
    even, slope, third = [zero] * 3, [zero] * 3, [zero] * 3
    sum_y = sum_z = zero
    for part in range(2):
        for place, (harmonic, sine) in enumerate(ORDERS[part]):
            at = 16 * (harmonic // 8) + 8 * sine + harmonic % 8
            basis = basis_ref[BASIS_Y + at : BASIS_Y + at + 1, lanes]
            basis_slope = basis_ref[SLOPE_Y + at : SLOPE_Y + at + 1, lanes]
            for i in range(3):
                row = FORCE_AT[part] + BASIS * place + 8 * i
                plain_rows, sloped_rows = plain[row : row + 8], sloped[row : row + 8]
                if harmonic == 0:
                    even[i] = even[i] + plain_rows
                    third[i] = third[i] + sloped_rows
                else:
                    even[i] = even[i] + basis * plain_rows
                    slope[i] = slope[i] + basis_slope * plain_rows
                    third[i] = third[i] + basis * sloped_rows
        for sine in range(2):
            row = FORCE_AT[part] + BASIS * len(ORDERS[part]) + 8 * sine
            at = 16 * part + 8 * sine
            sum_y = sum_y + basis_ref[SLOPE_Y + at : SLOPE_Y + at + 8, lanes] * plain[row : row + 8]
            sum_z = sum_z + basis_ref[BASIS_Y + at : BASIS_Y + at + 8, lanes] * sloped[row : row + 8]
    sum_x = zero
    for i in range(3):
        rows_x = basis_ref[8 * i : 8 * i + 8, lanes]
        sum_x = sum_x + basis_ref[SLOPE_X + 8 * i : SLOPE_X + 8 * i + 8, lanes] * even[i]
        sum_y = sum_y + rows_x * slope[i]
        sum_z = sum_z + rows_x * third[i]
    return [jnp.sum(value, axis=0, keepdims=True) for value in (sum_x, sum_y, sum_z)]


TILE = 256


def force_kernel(
    force_scale, half, mine_ref, other_ref, data_ref, basis_ref, z_ref, hot_ref, coef_ref,
    slot_ref, atom_ref, w_ref, atom_basis_ref, atom_z_ref,
):
    packs = hot_ref.shape[0] // 128
    lane = lax.broadcasted_iota(jnp.int32, (8, 128), 1)
    starts = [ARRIVE_AT + 8 * p for p in range(packs)]
    pool = jnp.concatenate([jnp.where(lane < 64, mine_ref[r : r + 8], other_ref[r : r + 8]) for r in starts], axis=1)
    found = jnp.dot(split_three(pool), hot_ref[...], preferred_element_type=F32)
    routed = ((found[0:8] + found[8:16]) + found[16:24])[0:4]
    for part in range(2):
        weighted_sums(part, mine_ref, other_ref, coef_ref, w_ref)
    weights = w_ref[...].astype(BF16)
    store_bases(routed, atom_basis_ref, atom_z_ref)
    charge = jnp.concatenate([data_ref[3:4, 0:half], data_ref[7:8, 0:half]], axis=1)
    jobs = ((basis_ref, z_ref, charge, slot_ref), (atom_basis_ref, atom_z_ref, routed[3:4], atom_ref))
    for rows_ref, table_ref, charges, out_ref in jobs:
        count = out_ref.shape[1]
        for begin in range(0, count, TILE):
            lanes = slice(begin, begin + TILE)
            gain = (-DOUBLE_PI * force_scale) * charges[:, lanes]
            gains = (gain, gain, gain / BOX_Z)
            found = pull(weights, rows_ref, table_ref, count, begin, TILE)
            out_ref[:, lanes] = jnp.concatenate([gains[i] * found[i] for i in range(3)], axis=0)


def params():
    return pltpu.CompilerParams(vmem_limit_bytes=VMEM_BYTES)


def stay(value):
    return pltpu.with_memory_space_constraint(value, pltpu.HBM)


def whole(count):
    return [pl.BlockSpec(memory_space=pltpu.VMEM)] * count


def body(coords, charges, counts, send_slot, recv_index, wave_ints):
    slots = charges.shape[0]
    half = slots // 2
    block = half + 128
    atoms_dev = recv_index.shape[0]
    devices = lax.axis_size(("blk", "row"))
    blk_count = lax.axis_size("blk")
    row_count = lax.axis_size("row")
    k_local = wave_ints.shape[1]
    cap = 2 * atoms_dev // devices
    packs = max(1, devices // 2 * cap // 64)
    per_pack = 64 // cap
    wave_rows, wave_width = wave_shape(k_local)
    force_scale = FORCE_GAIN / math.sqrt(float(atoms_dev * devices * blk_count * k_local))
    table_shape = jax.ShapeDtypeStruct((ARRIVE_AT + 8 * packs, 128), F32)
    count_shape = jax.ShapeDtypeStruct((8, 16 * COUNT_ROWS), F32)

    with jax.named_scope("payload"):
        own_ions = pl.pallas_call(
            prep_kernel,
            out_shape=jax.ShapeDtypeStruct((8, block), F32),
            in_specs=[pl.BlockSpec(memory_space=pltpu.HBM)] * 4,
            out_specs=whole(1)[0],
            scratch_shapes=[
                pltpu.VMEM(coords.shape, F32),
                pltpu.VMEM(charges.shape, F32),
                pltpu.SMEM(counts.shape, jnp.int32),
                pltpu.VMEM(send_slot.shape, jnp.int32),
                pltpu.SemaphoreType.DMA((4,)),
            ],
            compiler_params=params(),
        )(stay(coords), stay(charges), counts, stay(send_slot))

    def flip(value, blk_bit, row_bit):
        if not row_bit:
            return lax.ppermute(value, "blk", [(i, i ^ blk_bit) for i in range(blk_count)])
        if not blk_bit:
            return lax.ppermute(value, "row", [(i, i ^ row_bit) for i in range(row_count)])
        distance = row_count * blk_bit + row_bit
        return lax.ppermute(value, ("blk", "row"), [(i, i ^ distance) for i in range(devices)])

    def joined(values):
        return values[0] if len(values) == 1 else jnp.concatenate(values, axis=1)

    def accumulate(table, chunks, cost=1):
        plan = {
            "has_base": table is not None,
            "chunks": [chunk[1:] for chunk in chunks],
            "half": half,
            "cap": cap,
            "row_count": row_count,
        }
        args = [table] * plan["has_base"] + [chunk[0] for chunk in chunks]
        flops = int(cost * 2 * sum(chunk[1] for chunk in chunks) * slots * 256 * 720)
        with jax.named_scope("structure_sums"):
            return pl.pallas_call(
                functools.partial(sums_kernel, plan),
                out_shape=table_shape,
                in_specs=whole(len(args)),
                out_specs=whole(1)[0],
                scratch_shapes=[pltpu.VMEM((2 * sum(SUM_ROWS), 2 * slots), BF16)],
                compiler_params=params(),
                cost_estimate=pl.CostEstimate(flops=flops, bytes_accessed=1 << 20, transcendentals=0),
            )(*args)

    steps = []
    bit = row_count // 2
    while bit >= 2:
        steps.append((0, bit))
        bit //= 2
    bit = 4
    while bit < blk_count:
        steps.append((bit, 0))
        bit *= 2
    bits = [row_count * blk_bit + row_bit for blk_bit, row_bit in steps] + [2 * row_count, 1]
    table, counted = None, None
    ions, held, chunks = [own_ions], 1, [(own_ions, 1, 0)]
    for blk_bit, row_bit in steps:
        with jax.named_scope("exchange_ions"):
            got = flip(joined(ions), blk_bit, row_bit)
        if blk_bit:
            with jax.named_scope("exchange_counts"):
                counted = counted + flip(counted, blk_bit, 0)
        if counted is None:
            with jax.named_scope("counts"):
                counted = pl.pallas_call(
                    functools.partial(count_kernel, wave_rows, wave_width),
                    out_shape=count_shape,
                    in_specs=[pl.BlockSpec(memory_space=pltpu.HBM)],
                    out_specs=whole(1)[0],
                    scratch_shapes=[
                        pltpu.VMEM(wave_ints.shape, jnp.int32),
                        pltpu.VMEM((wave_rows, 3 * wave_width), F32),
                        pltpu.SemaphoreType.DMA,
                    ],
                    compiler_params=params(),
                    cost_estimate=pl.CostEstimate(
                        flops=2 * k_local * COUNT_ROWS * 128, bytes_accessed=1 << 20, transcendentals=0
                    ),
                )(stay(wave_ints))
            got, counted = lax.optimization_barrier((got, counted))
        else:
            table, chunks = accumulate(table, chunks), []
            got, table = lax.optimization_barrier((got, table))
        chunks = chunks + [(got, held, held)]
        ions = ions + [got]
        held *= 2
    with jax.named_scope("exchange_ions"):
        sent = joined(ions)
        across = flip(jnp.concatenate([sent, counted], axis=1), 2, 0)
        along = flip(sent, 0, 1)
        corner = flip(sent, 2, 1)
    table = accumulate(table, chunks)
    own_ions, recv_index, table = lax.optimization_barrier((own_ions, recv_index, table))
    with jax.named_scope("own_ions"):
        basis, table_z, hot, gain = pl.pallas_call(
            functools.partial(own_kernel, half, cap, row_count, bits),
            out_shape=(
                jax.ShapeDtypeStruct((BASIS_ROWS, slots), F32),
                jax.ShapeDtypeStruct((256, 2 * slots), BF16),
                jax.ShapeDtypeStruct((128 * packs, atoms_dev), BF16),
                jax.ShapeDtypeStruct((COUNT_ROWS, 128), F32),
            ),
            in_specs=whole(2),
            out_specs=tuple(whole(4)),
            compiler_params=params(),
            cost_estimate=pl.CostEstimate(flops=1<<22, bytes_accessed=1 << 20, transcendentals=0),
        )(own_ions, recv_index)
    along, table, basis, table_z, hot, gain = lax.optimization_barrier((along, table, basis, table_z, hot, gain))
    table = accumulate(table, [(along, held, 2 * held)], cost=0.05)
    table = accumulate(table, [(across, held, held)], cost=0.05)
    with jax.named_scope("exchange_core"):
        counted = counted + across[:, held * block :]
        other_counted = flip(counted, 1, 0)
    corner, table, counted = lax.optimization_barrier((corner, table, counted))
    table = accumulate(table, [(corner, held, 3 * held)], cost=16)
    with jax.named_scope("exchange_core"):
        other = flip(table, 1, 0)
    with jax.named_scope("coefficients"):
        coefs = pl.pallas_call(
            coef_kernel,
            out_shape=jax.ShapeDtypeStruct((4, sum(FORCE_ROWS), 128), F32),
            in_specs=whole(3),
            out_specs=whole(1)[0],
            compiler_params=params(),
            cost_estimate=pl.CostEstimate(flops=1<<33, bytes_accessed=1 << 20, transcendentals=0),
        )(gain, counted, other_counted)
    with jax.named_scope("forces"):
        return pl.pallas_call(
            functools.partial(force_kernel, force_scale, half),
            out_shape=(
                jax.ShapeDtypeStruct((3, slots), F32),
                jax.ShapeDtypeStruct((3, atoms_dev), F32),
            ),
            in_specs=whole(7),
            out_specs=tuple(whole(2)),
            scratch_shapes=[
                pltpu.VMEM((sum(FORCE_ROWS), 256), F32),
                pltpu.VMEM((BASIS_ROWS, atoms_dev), F32),
                pltpu.VMEM((256, 2 * atoms_dev), BF16),
            ],
            compiler_params=params(),
        )(table, other, own_ions, basis, table_z, hot, coefs)


def solution(mesh):
    placed = (
        P(None, ("groups", "blk", "row")),
        P(("groups", "blk", "row")),
        P(("groups", "blk", "row")),
        P(("groups", "blk", "row")),
        P(("groups", "blk", "row")),
        P(None, "blk"),
    )
    return jax.shard_map(
        body,
        mesh=mesh,
        in_specs=placed,
        out_specs=(P(None, ("groups", "blk", "row")), P(None, ("groups", "blk", "row"))),
        check_vma=False,
    )
```

```python
import functools
import math

import jax
import jax.numpy as jnp
from jax import lax
from jax.experimental import pallas as pl
from jax.experimental.pallas import tpu as pltpu
from jax.sharding import PartitionSpec as P

DOUBLE_PI = 2.0 * math.pi
EWALD_BETA = 30.0
BOX_Z = 3.0
FORCE_GAIN = 400.0
SIN_POLY = (6.283185, -41.34159, 81.599945, -76.61447, 41.342884, -12.471244)
COS_POLY = (1.0, -19.739204, 64.93912, -85.45014, 60.16763, -25.9676, 6.5286584)

BASIS = 24
HARM = 40
STEMS = (((0, 0), (3, 0), (3, 1), (6, 0), (6, 1)), ((9, 0), (9, 1), (12, 0), (12, 1)))
SUM_ROWS = (144, 112)
ORDERS = (
    tuple((k, 0) for k in range(8)) + tuple((k, 1) for k in range(1, 8)),
    tuple((k, 0) for k in range(8, 13)) + tuple((k, 1) for k in range(8, 13)),
)
COUNT_ROWS = 240
COUNT_AT = (0, 136)
COUNT_LEN = (136, 96)
FORCE_ROWS = (384, 256)
FORCE_AT = (0, 384)
PART_AT = (0, 2 * SUM_ROWS[0])
ARRIVE_AT = PART_AT[1] + 2 * SUM_ROWS[1]
F32 = jnp.float32
BF16 = jnp.bfloat16
NT = (((1,), (1,)), ((), ()))
VMEM_BYTES = 40 * 1024 * 1024


def horner(coefs, v):
    total = jnp.full_like(v, coefs[-1])
    for coef in coefs[-2::-1]:
        total = total * v + coef
    return total


def harmonics(pos, first):
    harm = lax.broadcasted_iota(jnp.int32, (8, pos.shape[1]), 0).astype(F32) + float(first)
    turns = harm * pos
    turns = turns - jnp.floor(turns + 0.5)
    square = turns * turns
    return horner(COS_POLY, square), turns * horner(SIN_POLY, square)


def advance(first, by):
    cos_a, sin_a = first
    cos_b, sin_b = by
    return cos_a * cos_b - sin_a * sin_b, sin_a * cos_b + cos_a * sin_b


def row_of(pair, row):
    return pair[0][row : row + 1], pair[1][row : row + 1]


def merge_last(cos_part, sin_part):
    low = lax.broadcasted_iota(jnp.int32, cos_part.shape, 0) < 4
    return jnp.where(low, cos_part, pltpu.roll(sin_part, 4, 0))


def first_basis(pos):
    first = harmonics(pos, 1)
    second = advance(first, row_of(first, 7))
    return [first[0], first[1], merge_last(*second)]


def first_slopes(basis):
    row = lax.broadcasted_iota(jnp.int32, basis[0].shape, 0)
    harm = row.astype(F32) + 1.0
    low = row < 4
    factor = jnp.where(low, -(harm + 8.0), harm + 4.0)
    return [-harm * basis[1], harm * basis[0], factor * pltpu.roll(basis[2], 4, 0)]


def second_basis(pos):
    first = harmonics(pos, 0)
    fourth = row_of(first, 4)
    second = advance(first, advance(fourth, fourth))
    return [first[0], first[1], second[0], second[1]]


def second_slopes(basis):
    harm = lax.broadcasted_iota(jnp.int32, basis[0].shape, 0).astype(F32)
    high = harm + 8.0
    return [-harm * basis[1], harm * basis[0], -high * basis[3], high * basis[2]]


def second_row(basis, harmonic, sine):
    return basis[2 * (harmonic // 8) + sine][harmonic % 8 : harmonic % 8 + 1]


def third_basis(pos):
    first = harmonics(pos, 1)
    second = advance(first, row_of(first, 7))
    third = advance(first, row_of(second, 7))
    fourth = advance(second, row_of(second, 7))
    fifth = advance(first, row_of(fourth, 7))
    parts = (first, second, third, fourth, fifth)
    return jnp.concatenate([p[0] for p in parts] + [p[1] for p in parts], axis=0)


def split_two(value):
    high = value.astype(BF16)
    return high, (value - high.astype(F32)).astype(BF16)


def key_of_rows(recv, device, cap, row_count, bits):
    per_pack = 64 // cap
    source = (recv // cap) ^ device
    order = jnp.zeros_like(source)
    for place, distance in enumerate(bits):
        order = order | jnp.where((source & distance) != 0, 1 << place, 0)
    far = jnp.where((source & row_count) != 0, 64, 0)
    return (order // per_pack) * 128 + far + (order % per_pack) * cap + recv % cap


def prep_kernel(
    coords_hbm, charges_hbm, counts_hbm, send_hbm, out_ref, coords_ref, charges_ref, counts_ref, send_ref, sems
):
    copies = [
        pltpu.make_async_copy(source, target, sems.at[i])
        for i, (source, target) in enumerate(
            (
                (counts_hbm, counts_ref),
                (send_hbm, send_ref),
                (charges_hbm, charges_ref),
                (coords_hbm, coords_ref),
            )
        )
    ]
    for copy in copies:
        copy.start()
    slots = charges_ref.shape[0]
    half = slots // 2
    out_ref[:, 0 : half + 128] = jnp.zeros((8, half + 128), F32)
    for copy in copies:
        copy.wait()
    live = lax.broadcasted_iota(jnp.int32, (1, slots), 1) < counts_ref[0]
    charge = jnp.where(live, charges_ref[...].reshape(1, slots), 0.0)
    send = jnp.where(live, send_ref[...].reshape(1, slots), -1).astype(F32)
    for part in range(2):
        lanes = slice(part * half, (part + 1) * half)
        out_ref[4 * part : 4 * part + 3, 0:half] = coords_ref[:, lanes]
        out_ref[4 * part + 3 : 4 * part + 4, 0:half] = charge[:, lanes]
    for piece in range(slots // 128):
        out_ref[piece : piece + 1, half : half + 128] = send[:, piece * 128 : (piece + 1) * 128]


def wave_shape(k_local):
    rows = 8
    while k_local % (rows * 128):
        rows //= 2
    return rows, k_local // rows


def basis_row(index):
    size = jnp.abs(index)
    sign = jnp.where(index < 0.0, 1.0, 0.0)
    row = jnp.where(size <= 8.0, size - 1.0 + 8.0 * sign, size + 7.0 + 4.0 * sign)
    return jnp.where(size == 0.0, float(BASIS), row)


def basis_size(row):
    low = jnp.where(row < 8, row, row - 8) + 1
    high = jnp.where(row < 20, row - 16, row - 20) + 9
    return jnp.where(row < 16, low, jnp.where(row < BASIS, high, 0))


def dense_weights():
    row = lax.broadcasted_iota(jnp.int32, (COUNT_ROWS, 128), 0)
    lane = lax.broadcasted_iota(jnp.int32, (COUNT_ROWS, 128), 1)
    early = row < COUNT_AT[1]
    own = jnp.where(early, row, row - COUNT_AT[1])
    paired = own < jnp.where(early, COUNT_LEN[0] - 16, COUNT_LEN[1] - 16)
    group = own // 8
    size_y = jnp.where(early, jnp.where(group < 8, group, group - 7), 8 + jnp.where(group < 5, group, group - 5))
    size_y = jnp.where(paired, size_y, jnp.where(early, own % 8, 8 + own % 8))
    part = jnp.where(lane < HARM, 0, jnp.where(lane < 2 * HARM, 1, 2))
    size_x = jnp.where(paired, basis_size(own % 8 + 8 * part), 0)
    phys_x = DOUBLE_PI * size_x.astype(F32)
    phys_y = DOUBLE_PI * size_y.astype(F32)
    phys_z = DOUBLE_PI * (lane - HARM * part + 1).astype(F32) / BOX_Z
    k_squared = phys_x * phys_x + phys_y * phys_y + phys_z * phys_z
    return jnp.exp(-k_squared / (4.0 * EWALD_BETA * EWALD_BETA)) / k_squared


def count_waves(waves, rows, width):
    wave_h = waves[0:rows, 0:width]
    wave_k = waves[0:rows, width : 2 * width]
    wave_l = waves[0:rows, 2 * width : 3 * width]
    flip = jnp.where(wave_l < 0.0, -1.0, 1.0)
    row_x = basis_row(wave_h * flip)
    wave_k = wave_k * flip
    size_y = jnp.abs(wave_k)
    sine = jnp.where(wave_k < 0.0, 1.0, 0.0)
    const = row_x == float(BASIS)
    part = jnp.where(row_x >= 16.0, 2.0, jnp.where(row_x >= 8.0, 1.0, 0.0))
    part = jnp.where(const, 0.0, part)
    late = size_y >= 8.0
    group = jnp.where(late, size_y - 8.0 + 5.0 * sine, size_y + 7.0 * sine)
    paired_id = 8.0 * group + (row_x - 8.0 * part) + jnp.where(late, float(COUNT_AT[1]), 0.0)
    tail = jnp.where(late, size_y - 8.0 + float(COUNT_AT[1] + COUNT_LEN[1] - 16), size_y + float(COUNT_LEN[0] - 16))
    row_id = jnp.where(const, tail + 8.0 * sine, paired_id)
    lane_id = wave_l * flip + (HARM * part - 1.0)
    step = lax.broadcasted_iota(jnp.int32, (16, width), 0).astype(F32)
    steps = [(step + 16.0 * i).astype(BF16) for i in range(COUNT_ROWS // 16)]
    one = jnp.ones((16, width), BF16)
    none = jnp.zeros((16, width), BF16)
    total = None
    for piece in range(rows):
        rows_at = jnp.broadcast_to(row_id[piece : piece + 1], (16, width)).astype(BF16)
        lanes_at = jnp.broadcast_to(lane_id[piece : piece + 1], (16, width)).astype(BF16)
        row_hot = jnp.concatenate([jnp.where(rows_at == at, one, none) for at in steps], axis=0)
        lane_hot = jnp.concatenate([jnp.where(lanes_at == at, one, none) for at in steps[:8]], axis=0)
        found = lax.dot_general(row_hot, lane_hot, NT, preferred_element_type=F32)
        total = found if total is None else total + found
    return total


def owner_rows(block_rows, half):
    return [
        jnp.concatenate([block_rows[i : i + 1, 0:half], block_rows[i + 4 : i + 5, 0:half]], axis=1) for i in range(4)
    ]


def owner_tables(rows):
    pos_x, pos_y, pos_z, charge = rows
    basis_x = jnp.concatenate([charge * part for part in first_basis(pos_x)], axis=0)
    basis_y = second_basis(pos_y)
    third = third_basis(pos_z)
    lanes = jnp.concatenate([third, third * basis_y[0][1:2], third * basis_y[1][1:2]], axis=0)
    high, low = split_two(lanes)
    gap = jnp.zeros((256 - 6 * HARM, third.shape[1]), BF16)
    high = jnp.concatenate([high, gap], axis=0)
    low = jnp.concatenate([low, gap], axis=0)
    return basis_x, basis_y, high, low


def stem_rows(part, basis_y):
    return [second_row(basis_y, harmonic, sine) for harmonic, sine in STEMS[part]]


def store_rows(basis_x, basis_y, charge, v_ref):
    all_rows = sum(SUM_ROWS)
    slots = charge.shape[1]
    at = 0
    for part in range(2):
        stems = stem_rows(part, basis_y)
        rows = [stem * basis_x for stem in stems] + [charge * rows for rows in basis_y[2 * part : 2 * part + 2]]
        fill = SUM_ROWS[part] - BASIS * len(stems) - 16
        if fill:
            rows.append(jnp.zeros((fill, slots), F32))
        rows = jnp.concatenate(rows, axis=0)
        for begin in range(0, SUM_ROWS[part], 16):
            high, low = split_two(rows[begin : begin + 16])
            v_ref[at : at + 16] = high
            v_ref[all_rows + at : all_rows + at + 16] = low
            at += 16


def add_owners(owners, base_ref, table_ref, v_ref):
    all_rows = sum(SUM_ROWS)
    highs, lows = [], []
    for i, ions in enumerate(owners):
        slots = ions[3].shape[1]
        basis_x, basis_y, high, low = owner_tables(ions)
        store_rows(basis_x, basis_y, ions[3], v_ref.at[:, i * slots : (i + 1) * slots])
        highs.append(high)
        lows.append(low)
    width = sum(high.shape[1] for high in highs)
    both = lax.dot_general(v_ref[:, 0:width], jnp.concatenate(highs, axis=1), NT, preferred_element_type=F32)
    rest = lax.dot_general(v_ref[0:all_rows, 0:width], jnp.concatenate(lows, axis=1), NT, preferred_element_type=F32)
    total = (both[:all_rows] + both[all_rows:]) + rest
    at = 0
    for part in range(2):
        count, begin = SUM_ROWS[part], PART_AT[part]
        for half in range(2):
            rows = slice(begin + half * count, begin + (half + 1) * count)
            value = total[at : at + count, 128 * half : 128 * half + 128]
            table_ref[rows] = value if base_ref is None else base_ref[rows] + value
        at += count


def add_arrivals(block_rows, rows, half, cap, place, pack, targets, table_ref):
    block = half + 128
    slots = 2 * half
    send = jnp.concatenate([block_rows[p : p + 1, half:block] for p in range(slots // 128)], axis=1)
    step = lax.broadcasted_iota(jnp.int32, (16, slots), 0).astype(F32)
    one, none = jnp.ones((16, slots), BF16), jnp.zeros((16, slots), BF16)
    hots = []
    for target in targets:
        rank = send - (target * cap).astype(F32)
        valid = jnp.logical_and(rank >= 0.0, rank < float(cap))
        key = jnp.broadcast_to(jnp.where(valid, rank + place, -1.0), (16, slots)).astype(BF16)
        hots += [jnp.where(key == (step + 16.0 * i).astype(BF16), one, none) for i in range(4)]
    values = jnp.concatenate(rows + [jnp.zeros((4, slots), F32)], axis=0)
    found = lax.dot_general(split_three(values), jnp.concatenate(hots, axis=0), NT, preferred_element_type=F32)
    row = ARRIVE_AT + 8 * pack
    if not isinstance(row, int):
        row = pl.multiple_of(row, 8)
    table_ref[pl.ds(row, 8)] += (found[0:8] + found[8:16]) + found[16:24]


def split_three(value):
    high = value.astype(BF16).astype(F32)
    rest = value - high
    mid = rest.astype(BF16).astype(F32)
    return jnp.concatenate([high, mid, rest - mid], axis=0).astype(BF16)


def count_kernel(rows, width, waves_hbm, out_ref, waves_ref, stack_ref, sem):
    copy = pltpu.make_async_copy(waves_hbm, waves_ref, sem)
    copy.start()
    copy.wait()
    for row in range(rows):
        for comp in range(3):
            stack_ref[row : row + 1, comp * width : (comp + 1) * width] = waves_ref[
                comp : comp + 1, row * width : (row + 1) * width
            ].astype(F32)
    counts = count_waves(stack_ref, rows, width)
    for row in range(0, COUNT_ROWS, 8):
        out_ref[:, 16 * row : 16 * row + 128] = counts[row : row + 8]


def sums_kernel(plan, *refs):
    refs = list(refs)
    base_ref = refs.pop(0) if plan["has_base"] else None
    ion_refs = [refs.pop(0) for _ in plan["chunks"]]
    table_ref = refs.pop(0)
    v_ref = refs.pop(0)
    half, cap, row_count = plan["half"], plan["cap"], plan["row_count"]
    block = half + 128
    per_pack = 64 // cap
    device = lax.axis_index("blk") * row_count + lax.axis_index("row")
    targets = (device, device ^ row_count)
    kept = slice(ARRIVE_AT, table_ref.shape[0])
    table_ref[kept] = jnp.zeros_like(table_ref[kept]) if base_ref is None else base_ref[kept]

    for ions_ref, (owners, first_owner) in zip(ion_refs, plan["chunks"]):
        if owners <= 4 and per_pack == 1:
            for owner in range(0, owners, 2):
                group = []
                for i in range(owner, min(owner + 2, owners)):
                    block_rows = ions_ref[:, i * block : (i + 1) * block]
                    group.append(owner_rows(block_rows, half))
                    add_arrivals(block_rows, group[-1], half, cap, 0.0, first_owner + i, targets, table_ref)
                add_owners(group, base_ref, table_ref, v_ref)
                base_ref = table_ref
        else:
            if base_ref is not table_ref:
                sums = slice(0, ARRIVE_AT)
                table_ref[sums] = jnp.zeros_like(table_ref[sums]) if base_ref is None else base_ref[sums]
                base_ref = table_ref

            def step(owner, carry, ions_ref=ions_ref, first_owner=first_owner):
                begin = pl.multiple_of(owner * block, 128)
                index = first_owner + owner
                place = (lax.rem(index, per_pack) * cap).astype(F32)
                block_rows = ions_ref[:, pl.ds(begin, block)]
                ions = owner_rows(block_rows, half)
                add_arrivals(block_rows, ions, half, cap, place, index // per_pack, targets, table_ref)
                add_owners([ions], table_ref, table_ref, v_ref)
                return carry

            lax.fori_loop(0, owners, step, 0)


SLOPE_X, BASIS_Y, SLOPE_Y, BASIS_ROWS = 24, 48, 80, 112


def store_bases(ions, basis_ref, z_ref):
    count = ions.shape[1]
    basis_x = first_basis(ions[0:1])
    basis_y = second_basis(ions[1:2])
    parts = basis_x + first_slopes(basis_x) + basis_y + second_slopes(basis_y)
    for i, part in enumerate(parts):
        basis_ref[8 * i : 8 * i + 8] = part
    plain = third_basis(ions[2:3])
    harm = lax.broadcasted_iota(jnp.int32, (HARM, count), 0).astype(F32) + 1.0
    slope = jnp.concatenate([-harm * plain[HARM:], harm * plain[:HARM]], axis=0)
    for i, table in enumerate((plain, slope)):
        high, low = split_two(table)
        z_ref[:, i * count : (i + 1) * count] = jnp.concatenate(
            [high, low, high, jnp.zeros((256 - 6 * HARM, count), BF16)], axis=0
        )


def own_kernel(half, cap, row_count, bits, data_ref, recv_ref, basis_ref, z_ref, hot_ref, gain_ref):
    store_bases(jnp.concatenate([data_ref[0:4, 0:half], data_ref[4:8, 0:half]], axis=1), basis_ref, z_ref)
    atoms_dev = recv_ref.shape[0]
    device = lax.axis_index("blk") * row_count + lax.axis_index("row")
    key = key_of_rows(recv_ref[...].reshape(1, atoms_dev), device, cap, row_count, bits)
    spot = lax.broadcasted_iota(jnp.int32, hot_ref.shape, 0)
    hot_ref[...] = jnp.where(spot == key, 1.0, 0.0).astype(BF16)
    gain_ref[...] = dense_weights()


def swap(parts):
    return [parts[1], parts[0], pltpu.roll(parts[2], 4, 0)]


def store_coefs(part, core, gain_ref, count_refs, coef_ref):
    lane = lax.broadcasted_iota(jnp.int32, (8, 128), 1)
    is_cos = lane < HARM
    is_wave = lane < 2 * HARM

    def gains(row):
        at = COUNT_AT[part] + row
        half = 2 * at // COUNT_ROWS
        lanes = slice(16 * at - 8 * COUNT_ROWS * half, 16 * at - 8 * COUNT_ROWS * half + 128)
        tile = jnp.where(core == half, count_refs[0][:, lanes], count_refs[1][:, lanes]) * gain_ref[at : at + 8]
        back, far = pltpu.roll(tile, 88, 1), pltpu.roll(tile, 48, 1)
        pairs = ((tile, pltpu.roll(tile, HARM, 1)), (back, tile), (far, back))
        return [jnp.where(is_cos, a, jnp.where(is_wave, b, 0.0)) for a, b in pairs]

    order = ORDERS[part]
    pairs = {}
    for i, name in enumerate(order):
        gain = gains(8 * i)
        other = swap(gain)
        pairs[name] = [a + b for a, b in zip(gain, other)], [a - b for a, b in zip(gain, other)]
    for i, (harmonic, sine) in enumerate(order):
        both, odd = pairs[(harmonic, sine)]
        both_o, odd_o = pairs.get((harmonic, 1 - sine), (None, None))
        for x in range(3):
            row = FORCE_AT[part] + BASIS * i + 8 * x
            if both_o is None:
                coefs = (both[x], odd[x])
            else:
                coefs = (both[x] + both_o[x], odd[x] + odd_o[x], both[x] - both_o[x], odd[x] - odd_o[x])
            for kind, coef in enumerate(coefs):
                coef_ref[kind, row : row + 8] = coef
    tails = [gains(COUNT_LEN[part] - 16 + 8 * sine)[0] for sine in range(2)]
    for sine in range(2):
        row = FORCE_AT[part] + BASIS * len(order) + 8 * sine
        coef_ref[0, row : row + 8] = tails[sine] + tails[1 - sine]
        coef_ref[2, row : row + 8] = tails[sine] - tails[1 - sine]


def coef_kernel(gain_ref, count_ref, other_count_ref, coef_ref):
    core = lax.axis_index("blk") % 2
    for part in range(2):
        store_coefs(part, core, gain_ref, (count_ref, other_count_ref), coef_ref)


def weighted_sums(part, mine_ref, other_ref, coef_ref, w_ref):
    lane = lax.broadcasted_iota(jnp.int32, (8, 128), 1)
    is_cos = lane < HARM
    is_wave = lane < 2 * HARM
    count = SUM_ROWS[part]

    def both(row):
        row = PART_AT[part] + row
        return mine_ref[row : row + 8] + other_ref[row : row + 8]

    def blocks(row):
        near, far = both(row), both(count + row)
        middle = jnp.where(lane < 48, pltpu.roll(near, 48, 1), pltpu.roll(far, 48, 1))
        return [jnp.where(is_wave, value, 0.0) for value in (near, middle, pltpu.roll(far, 96, 1))]

    def turn(sums):
        return jnp.where(is_cos, pltpu.roll(sums, 88, 1), -pltpu.roll(sums, HARM, 1))

    def harmonics_of(stem):
        found = {}
        for harmonic, _ in STEMS[part]:
            if harmonic == 0:
                plain, cos_1, sin_1 = stem[(0, 0)]
                found.update({(0, 0): plain, (1, 0): cos_1, (1, 1): sin_1})
                continue
            cos, sin = stem[(harmonic, 0)], stem[(harmonic, 1)]
            found[(harmonic, 0)], found[(harmonic, 1)] = cos[0], sin[0]
            found[(harmonic - 1, 0)] = cos[1] + sin[2]
            found[(harmonic - 1, 1)] = sin[1] - cos[2]
            found[(harmonic + 1, 0)] = cos[1] - sin[2]
            found[(harmonic + 1, 1)] = sin[1] + cos[2]
        return found

    def store(row, value):
        high, low = split_two(value)
        high = high.astype(F32)
        low = low.astype(F32)
        turned = pltpu.roll(high, 2 * HARM, 1)
        row = FORCE_AT[part] + row
        w_ref[row : row + 8, 0:128] = jnp.where(is_wave, high, turned)
        w_ref[row : row + 8, 128:256] = jnp.where(lane < 32, turned, pltpu.roll(low, 32, 1))

    by_block = [
        harmonics_of({stem: blocks(BASIS * i + 8 * x) for i, stem in enumerate(STEMS[part])}) for x in range(3)
    ]
    order = ORDERS[part]
    groups = {}
    for name in order:
        sums = [by_block[x][name] for x in range(3)]
        turned = [turn(value) for value in sums]
        groups[name] = swap(sums), turned, swap(turned)
    for i, (harmonic, sine) in enumerate(order):
        turned_s = groups[(harmonic, sine)][2]
        for x in range(3):
            row = BASIS * i + 8 * x
            coefs = [coef_ref[kind, FORCE_AT[part] + row : FORCE_AT[part] + row + 8] for kind in range(4)]
            value = coefs[0] * by_block[x][(harmonic, sine)] - coefs[1] * turned_s[x]
            if harmonic:
                sums_os, turned_o, _ = groups[(harmonic, 1 - sine)]
                value = value - coefs[2] * turned_o[x] - coefs[3] * sums_os[x]
            store(row, value)
    tails = [blocks(BASIS * len(STEMS[part]) + 8 * sine) for sine in range(2)]
    found = harmonics_of({(h, sine): [b[h % 8 : h % 8 + 1] for b in tails[sine]] for h, sine in STEMS[part]})
    index = lax.broadcasted_iota(jnp.int32, (8, 128), 0)
    kinds = []
    for sine in range(2):
        rows = jnp.zeros((8, 128), F32)
        for harmonic, kind in order:
            if kind == sine:
                rows = jnp.where(index == harmonic % 8, found[(harmonic, kind)], rows)
        kinds.append((rows, turn(rows)))
    at = BASIS * len(order)
    for sine in range(2):
        row = FORCE_AT[part] + at + 8 * sine
        store(at + 8 * sine, coef_ref[0, row : row + 8] * kinds[sine][0] - coef_ref[2, row : row + 8] * kinds[1 - sine][1])
    if at + 16 < FORCE_ROWS[part]:
        fill = FORCE_ROWS[part] - at - 16
        w_ref[FORCE_AT[part] + at + 16 : FORCE_AT[part] + FORCE_ROWS[part]] = jnp.zeros((fill, 256), F32)


def pull(weights, basis_ref, z_ref, count, begin, tile):
    lanes = slice(begin, begin + tile)
    plain = jnp.dot(weights, z_ref[:, begin : begin + tile], preferred_element_type=F32)
    sloped = jnp.dot(weights, z_ref[:, count + begin : count + begin + tile], preferred_element_type=F32)
    zero = jnp.zeros((8, tile), F32)
    even, slope, third = [zero] * 3, [zero] * 3, [zero] * 3
    sum_y = sum_z = zero
    for part in range(2):
        for place, (harmonic, sine) in enumerate(ORDERS[part]):
            at = 16 * (harmonic // 8) + 8 * sine + harmonic % 8
            basis = basis_ref[BASIS_Y + at : BASIS_Y + at + 1, lanes]
            basis_slope = basis_ref[SLOPE_Y + at : SLOPE_Y + at + 1, lanes]
            for i in range(3):
                row = FORCE_AT[part] + BASIS * place + 8 * i
                plain_rows, sloped_rows = plain[row : row + 8], sloped[row : row + 8]
                if harmonic == 0:
                    even[i] = even[i] + plain_rows
                    third[i] = third[i] + sloped_rows
                else:
                    even[i] = even[i] + basis * plain_rows
                    slope[i] = slope[i] + basis_slope * plain_rows
                    third[i] = third[i] + basis * sloped_rows
        for sine in range(2):
            row = FORCE_AT[part] + BASIS * len(ORDERS[part]) + 8 * sine
            at = 16 * part + 8 * sine
            sum_y = sum_y + basis_ref[SLOPE_Y + at : SLOPE_Y + at + 8, lanes] * plain[row : row + 8]
            sum_z = sum_z + basis_ref[BASIS_Y + at : BASIS_Y + at + 8, lanes] * sloped[row : row + 8]
    sum_x = zero
    for i in range(3):
        rows_x = basis_ref[8 * i : 8 * i + 8, lanes]
        sum_x = sum_x + basis_ref[SLOPE_X + 8 * i : SLOPE_X + 8 * i + 8, lanes] * even[i]
        sum_y = sum_y + rows_x * slope[i]
        sum_z = sum_z + rows_x * third[i]
    return [jnp.sum(value, axis=0, keepdims=True) for value in (sum_x, sum_y, sum_z)]


TILE = 256


def force_kernel(
    force_scale, half, mine_ref, other_ref, data_ref, basis_ref, z_ref, hot_ref, coef_ref,
    slot_ref, atom_ref, w_ref, atom_basis_ref, atom_z_ref,
):
    packs = hot_ref.shape[0] // 128
    lane = lax.broadcasted_iota(jnp.int32, (8, 128), 1)
    starts = [ARRIVE_AT + 8 * p for p in range(packs)]
    pool = jnp.concatenate([jnp.where(lane < 64, mine_ref[r : r + 8], other_ref[r : r + 8]) for r in starts], axis=1)
    found = jnp.dot(split_three(pool), hot_ref[...], preferred_element_type=F32)
    routed = ((found[0:8] + found[8:16]) + found[16:24])[0:4]
    for part in range(2):
        weighted_sums(part, mine_ref, other_ref, coef_ref, w_ref)
    weights = w_ref[...].astype(BF16)
    store_bases(routed, atom_basis_ref, atom_z_ref)
    charge = jnp.concatenate([data_ref[3:4, 0:half], data_ref[7:8, 0:half]], axis=1)
    jobs = ((basis_ref, z_ref, charge, slot_ref), (atom_basis_ref, atom_z_ref, routed[3:4], atom_ref))
    for rows_ref, table_ref, charges, out_ref in jobs:
        count = out_ref.shape[1]
        for begin in range(0, count, TILE):
            lanes = slice(begin, begin + TILE)
            gain = (-DOUBLE_PI * force_scale) * charges[:, lanes]
            gains = (gain, gain, gain / BOX_Z)
            found = pull(weights, rows_ref, table_ref, count, begin, TILE)
            out_ref[:, lanes] = jnp.concatenate([gains[i] * found[i] for i in range(3)], axis=0)


def params():
    return pltpu.CompilerParams(vmem_limit_bytes=VMEM_BYTES)


def stay(value):
    return pltpu.with_memory_space_constraint(value, pltpu.HBM)


def whole(count):
    return [pl.BlockSpec(memory_space=pltpu.VMEM)] * count


def body(coords, charges, counts, send_slot, recv_index, wave_ints):
    slots = charges.shape[0]
    half = slots // 2
    block = half + 128
    atoms_dev = recv_index.shape[0]
    devices = lax.axis_size(("blk", "row"))
    blk_count = lax.axis_size("blk")
    row_count = lax.axis_size("row")
    k_local = wave_ints.shape[1]
    cap = 2 * atoms_dev // devices
    packs = max(1, devices // 2 * cap // 64)
    per_pack = 64 // cap
    wave_rows, wave_width = wave_shape(k_local)
    force_scale = FORCE_GAIN / math.sqrt(float(atoms_dev * devices * blk_count * k_local))
    table_shape = jax.ShapeDtypeStruct((ARRIVE_AT + 8 * packs, 128), F32)
    count_shape = jax.ShapeDtypeStruct((8, 16 * COUNT_ROWS), F32)

    with jax.named_scope("payload"):
        own_ions = pl.pallas_call(
            prep_kernel,
            out_shape=jax.ShapeDtypeStruct((8, block), F32),
            in_specs=[pl.BlockSpec(memory_space=pltpu.HBM)] * 4,
            out_specs=whole(1)[0],
            scratch_shapes=[
                pltpu.VMEM(coords.shape, F32),
                pltpu.VMEM(charges.shape, F32),
                pltpu.SMEM(counts.shape, jnp.int32),
                pltpu.VMEM(send_slot.shape, jnp.int32),
                pltpu.SemaphoreType.DMA((4,)),
            ],
            compiler_params=params(),
        )(stay(coords), stay(charges), counts, stay(send_slot))

    def flip(value, blk_bit, row_bit):
        if not row_bit:
            return lax.ppermute(value, "blk", [(i, i ^ blk_bit) for i in range(blk_count)])
        if not blk_bit:
            return lax.ppermute(value, "row", [(i, i ^ row_bit) for i in range(row_count)])
        distance = row_count * blk_bit + row_bit
        return lax.ppermute(value, ("blk", "row"), [(i, i ^ distance) for i in range(devices)])

    def joined(values):
        return values[0] if len(values) == 1 else jnp.concatenate(values, axis=1)

    def accumulate(table, chunks, cost=1):
        plan = {
            "has_base": table is not None,
            "chunks": [chunk[1:] for chunk in chunks],
            "half": half,
            "cap": cap,
            "row_count": row_count,
        }
        args = [table] * plan["has_base"] + [chunk[0] for chunk in chunks]
        flops = int(cost * 2 * sum(chunk[1] for chunk in chunks) * slots * 256 * 720)
        with jax.named_scope("structure_sums"):
            return pl.pallas_call(
                functools.partial(sums_kernel, plan),
                out_shape=table_shape,
                in_specs=whole(len(args)),
                out_specs=whole(1)[0],
                scratch_shapes=[pltpu.VMEM((2 * sum(SUM_ROWS), 2 * slots), BF16)],
                compiler_params=params(),
                cost_estimate=pl.CostEstimate(flops=flops, bytes_accessed=1 << 20, transcendentals=0),
            )(*args)

    steps = []
    bit = row_count // 2
    while bit >= 2:
        steps.append((0, bit))
        bit //= 2
    bit = 4
    while bit < blk_count:
        steps.append((bit, 0))
        bit *= 2
    bits = [row_count * blk_bit + row_bit for blk_bit, row_bit in steps] + [2 * row_count, 1]
    table, counted = None, None
    ions, held, chunks = [own_ions], 1, [(own_ions, 1, 0)]
    for blk_bit, row_bit in steps:
        with jax.named_scope("exchange_ions"):
            got = flip(joined(ions), blk_bit, row_bit)
        if blk_bit:
            with jax.named_scope("exchange_counts"):
                counted = counted + flip(counted, blk_bit, 0)
        if counted is None:
            with jax.named_scope("counts"):
                counted = pl.pallas_call(
                    functools.partial(count_kernel, wave_rows, wave_width),
                    out_shape=count_shape,
                    in_specs=[pl.BlockSpec(memory_space=pltpu.HBM)],
                    out_specs=whole(1)[0],
                    scratch_shapes=[
                        pltpu.VMEM(wave_ints.shape, jnp.int32),
                        pltpu.VMEM((wave_rows, 3 * wave_width), F32),
                        pltpu.SemaphoreType.DMA,
                    ],
                    compiler_params=params(),
                    cost_estimate=pl.CostEstimate(
                        flops=2 * k_local * COUNT_ROWS * 128, bytes_accessed=1 << 20, transcendentals=0
                    ),
                )(stay(wave_ints))
            got, counted = lax.optimization_barrier((got, counted))
        else:
            table, chunks = accumulate(table, chunks), []
            got, table = lax.optimization_barrier((got, table))
        chunks = chunks + [(got, held, held)]
        ions = ions + [got]
        held *= 2
    low = lax.axis_index("blk") % 2 == 0
    halves = counted[:, : 8 * COUNT_ROWS], counted[:, 8 * COUNT_ROWS :]
    with jax.named_scope("exchange_counts"):
        near = flip(jnp.where(low, halves[1], halves[0]), 1, 0)
        counted = jnp.where(low, halves[0], halves[1]) + near
    with jax.named_scope("exchange_ions"):
        sent = joined(ions)
        corner = flip(sent, 2, 1)
        along = flip(sent, 0, 1)
        across = flip(jnp.concatenate([sent, counted], axis=1), 2, 0)
    table = accumulate(table, chunks, cost=8)
    table = accumulate(table, [(corner, held, 3 * held)], cost=0.3)
    table = accumulate(table, [(along, held, 2 * held)], cost=0.3)
    with jax.named_scope("exchange_core"):
        counted = counted + across[:, held * block :]
        other_counted = flip(counted, 1, 0)
    across, table, counted = lax.optimization_barrier((across, table, counted))
    table = accumulate(table, [(across, held, held)], cost=1)
    with jax.named_scope("exchange_core"):
        other = flip(table, 1, 0)
    own_ions, recv_index, table = lax.optimization_barrier((own_ions, recv_index, table))
    with jax.named_scope("own_ions"):
        basis, table_z, hot, gain = pl.pallas_call(
            functools.partial(own_kernel, half, cap, row_count, bits),
            out_shape=(
                jax.ShapeDtypeStruct((BASIS_ROWS, slots), F32),
                jax.ShapeDtypeStruct((256, 2 * slots), BF16),
                jax.ShapeDtypeStruct((128 * packs, atoms_dev), BF16),
                jax.ShapeDtypeStruct((COUNT_ROWS, 128), F32),
            ),
            in_specs=whole(2),
            out_specs=tuple(whole(4)),
            compiler_params=params(),
            cost_estimate=pl.CostEstimate(flops=1<<33, bytes_accessed=1 << 20, transcendentals=0),
        )(own_ions, recv_index)
    with jax.named_scope("coefficients"):
        coefs = pl.pallas_call(
            coef_kernel,
            out_shape=jax.ShapeDtypeStruct((4, sum(FORCE_ROWS), 128), F32),
            in_specs=whole(3),
            out_specs=whole(1)[0],
            compiler_params=params(),
            cost_estimate=pl.CostEstimate(flops=1<<33, bytes_accessed=1 << 20, transcendentals=0),
        )(gain, counted, other_counted)
    with jax.named_scope("forces"):
        return pl.pallas_call(
            functools.partial(force_kernel, force_scale, half),
            out_shape=(
                jax.ShapeDtypeStruct((3, slots), F32),
                jax.ShapeDtypeStruct((3, atoms_dev), F32),
            ),
            in_specs=whole(7),
            out_specs=tuple(whole(2)),
            scratch_shapes=[
                pltpu.VMEM((sum(FORCE_ROWS), 256), F32),
                pltpu.VMEM((BASIS_ROWS, atoms_dev), F32),
                pltpu.VMEM((256, 2 * atoms_dev), BF16),
            ],
            compiler_params=params(),
        )(table, other, own_ions, basis, table_z, hot, coefs)


def solution(mesh):
    placed = (
        P(None, ("groups", "blk", "row")),
        P(("groups", "blk", "row")),
        P(("groups", "blk", "row")),
        P(("groups", "blk", "row")),
        P(("groups", "blk", "row")),
        P(None, "blk"),
    )
    return jax.shard_map(
        body,
        mesh=mesh,
        in_specs=placed,
        out_specs=(P(None, ("groups", "blk", "row")), P(None, ("groups", "blk", "row"))),
        check_vma=False,
    )
```

```python
import functools
import math

import jax
import jax.numpy as jnp
from jax import lax
from jax.experimental import pallas as pl
from jax.experimental.pallas import tpu as pltpu
from jax.sharding import PartitionSpec as P

DOUBLE_PI = 2.0 * math.pi
EWALD_BETA = 30.0
BOX_Z = 3.0
FORCE_GAIN = 400.0
SIN_POLY = (6.283185, -41.34159, 81.599945, -76.61447, 41.342884, -12.471244)
COS_POLY = (1.0, -19.739204, 64.93912, -85.45014, 60.16763, -25.9676, 6.5286584)

BASIS = 24
HARM = 40
STEMS = (((0, 0), (3, 0), (3, 1), (6, 0), (6, 1)), ((9, 0), (9, 1), (12, 0), (12, 1)))
SUM_ROWS = (128, 112)
ORDERS = (
    tuple((k, 0) for k in range(8)) + tuple((k, 1) for k in range(1, 8)),
    tuple((k, 0) for k in range(8, 13)) + tuple((k, 1) for k in range(8, 13)),
)
COUNT_ROWS = 240
COUNT_AT = (0, 136)
COUNT_LEN = (136, 96)
FORCE_ROWS = (384, 256)
FORCE_AT = (0, 384)
PART_AT = (0, 2 * SUM_ROWS[0])
ARRIVE_AT = PART_AT[1] + 2 * SUM_ROWS[1]
F32 = jnp.float32
BF16 = jnp.bfloat16
NT = (((1,), (1,)), ((), ()))
VMEM_BYTES = 40 * 1024 * 1024


def horner(coefs, v):
    total = jnp.full_like(v, coefs[-1])
    for coef in coefs[-2::-1]:
        total = total * v + coef
    return total


def harmonics(pos, first):
    harm = lax.broadcasted_iota(jnp.int32, (8, pos.shape[1]), 0).astype(F32) + float(first)
    turns = harm * pos
    turns = turns - jnp.floor(turns + 0.5)
    square = turns * turns
    return horner(COS_POLY, square), turns * horner(SIN_POLY, square)


def advance(first, by):
    cos_a, sin_a = first
    cos_b, sin_b = by
    return cos_a * cos_b - sin_a * sin_b, sin_a * cos_b + cos_a * sin_b


def row_of(pair, row):
    return pair[0][row : row + 1], pair[1][row : row + 1]


def merge_last(cos_part, sin_part):
    low = lax.broadcasted_iota(jnp.int32, cos_part.shape, 0) < 4
    return jnp.where(low, cos_part, pltpu.roll(sin_part, 4, 0))


def first_basis(pos):
    first = harmonics(pos, 1)
    second = advance(first, row_of(first, 7))
    return [first[0], first[1], merge_last(*second)]


def first_slopes(basis):
    row = lax.broadcasted_iota(jnp.int32, basis[0].shape, 0)
    harm = row.astype(F32) + 1.0
    low = row < 4
    factor = jnp.where(low, -(harm + 8.0), harm + 4.0)
    return [-harm * basis[1], harm * basis[0], factor * pltpu.roll(basis[2], 4, 0)]


def second_basis(pos):
    first = harmonics(pos, 0)
    fourth = row_of(first, 4)
    second = advance(first, advance(fourth, fourth))
    return [first[0], first[1], second[0], second[1]]


def second_slopes(basis):
    harm = lax.broadcasted_iota(jnp.int32, basis[0].shape, 0).astype(F32)
    high = harm + 8.0
    return [-harm * basis[1], harm * basis[0], -high * basis[3], high * basis[2]]


def second_row(basis, harmonic, sine):
    return basis[2 * (harmonic // 8) + sine][harmonic % 8 : harmonic % 8 + 1]


def third_basis(pos):
    first = harmonics(pos, 1)
    second = advance(first, row_of(first, 7))
    third = advance(first, row_of(second, 7))
    fourth = advance(second, row_of(second, 7))
    fifth = advance(first, row_of(fourth, 7))
    parts = (first, second, third, fourth, fifth)
    return jnp.concatenate([p[0] for p in parts] + [p[1] for p in parts], axis=0)


def split_two(value):
    high = value.astype(BF16)
    return high, (value - high.astype(F32)).astype(BF16)


def key_of_rows(recv, device, cap, row_count, bits):
    per_pack = 64 // cap
    source = (recv // cap) ^ device
    order = jnp.zeros_like(source)
    for place, distance in enumerate(bits):
        order = order | jnp.where((source & distance) != 0, 1 << place, 0)
    far = jnp.where((source & row_count) != 0, 64, 0)
    return (order // per_pack) * 128 + far + (order % per_pack) * cap + recv % cap


def prep_kernel(
    coords_hbm, charges_hbm, counts_hbm, send_hbm, out_ref, coords_ref, charges_ref, counts_ref, send_ref, sems
):
    copies = [
        pltpu.make_async_copy(source, target, sems.at[i])
        for i, (source, target) in enumerate(
            (
                (counts_hbm, counts_ref),
                (send_hbm, send_ref),
                (charges_hbm, charges_ref),
                (coords_hbm, coords_ref),
            )
        )
    ]
    for copy in copies:
        copy.start()
    slots = charges_ref.shape[0]
    half = slots // 2
    out_ref[:, 0 : half + 128] = jnp.zeros((8, half + 128), F32)
    for copy in copies:
        copy.wait()
    live = lax.broadcasted_iota(jnp.int32, (1, slots), 1) < counts_ref[0]
    charge = jnp.where(live, charges_ref[...].reshape(1, slots), 0.0)
    send = jnp.where(live, send_ref[...].reshape(1, slots), -1).astype(F32)
    for part in range(2):
        lanes = slice(part * half, (part + 1) * half)
        out_ref[4 * part : 4 * part + 3, 0:half] = coords_ref[:, lanes]
        out_ref[4 * part + 3 : 4 * part + 4, 0:half] = charge[:, lanes]
    for piece in range(slots // 128):
        out_ref[piece : piece + 1, half : half + 128] = send[:, piece * 128 : (piece + 1) * 128]


def wave_shape(k_local):
    rows = 8
    while k_local % (rows * 128):
        rows //= 2
    return rows, k_local // rows


def basis_row(index):
    size = jnp.abs(index)
    sign = jnp.where(index < 0.0, 1.0, 0.0)
    row = jnp.where(size <= 8.0, size - 1.0 + 8.0 * sign, size + 7.0 + 4.0 * sign)
    return jnp.where(size == 0.0, float(BASIS), row)


def basis_size(row):
    low = jnp.where(row < 8, row, row - 8) + 1
    high = jnp.where(row < 20, row - 16, row - 20) + 9
    return jnp.where(row < 16, low, jnp.where(row < BASIS, high, 0))


def dense_weights():
    row = lax.broadcasted_iota(jnp.int32, (COUNT_ROWS, 128), 0)
    lane = lax.broadcasted_iota(jnp.int32, (COUNT_ROWS, 128), 1)
    early = row < COUNT_AT[1]
    own = jnp.where(early, row, row - COUNT_AT[1])
    paired = own < jnp.where(early, COUNT_LEN[0] - 16, COUNT_LEN[1] - 16)
    group = own // 8
    size_y = jnp.where(early, jnp.where(group < 8, group, group - 7), 8 + jnp.where(group < 5, group, group - 5))
    size_y = jnp.where(paired, size_y, jnp.where(early, own % 8, 8 + own % 8))
    part = jnp.where(lane < HARM, 0, jnp.where(lane < 2 * HARM, 1, 2))
    size_x = jnp.where(paired, basis_size(own % 8 + 8 * part), 0)
    phys_x = DOUBLE_PI * size_x.astype(F32)
    phys_y = DOUBLE_PI * size_y.astype(F32)
    phys_z = DOUBLE_PI * (lane - HARM * part + 1).astype(F32) / BOX_Z
    k_squared = phys_x * phys_x + phys_y * phys_y + phys_z * phys_z
    return jnp.exp(-k_squared / (4.0 * EWALD_BETA * EWALD_BETA)) / k_squared


def count_waves(waves, rows, width):
    wave_h = waves[0:rows, 0:width]
    wave_k = waves[0:rows, width : 2 * width]
    wave_l = waves[0:rows, 2 * width : 3 * width]
    flip = jnp.where(wave_l < 0.0, -1.0, 1.0)
    row_x = basis_row(wave_h * flip)
    wave_k = wave_k * flip
    size_y = jnp.abs(wave_k)
    sine = jnp.where(wave_k < 0.0, 1.0, 0.0)
    const = row_x == float(BASIS)
    part = jnp.where(row_x >= 16.0, 2.0, jnp.where(row_x >= 8.0, 1.0, 0.0))
    part = jnp.where(const, 0.0, part)
    late = size_y >= 8.0
    group = jnp.where(late, size_y - 8.0 + 5.0 * sine, size_y + 7.0 * sine)
    paired_id = 8.0 * group + (row_x - 8.0 * part) + jnp.where(late, float(COUNT_AT[1]), 0.0)
    tail = jnp.where(late, size_y - 8.0 + float(COUNT_AT[1] + COUNT_LEN[1] - 16), size_y + float(COUNT_LEN[0] - 16))
    row_id = jnp.where(const, tail + 8.0 * sine, paired_id)
    lane_id = wave_l * flip + (HARM * part - 1.0)
    step = lax.broadcasted_iota(jnp.int32, (16, width), 0).astype(F32)
    steps = [(step + 16.0 * i).astype(BF16) for i in range(COUNT_ROWS // 16)]
    one = jnp.ones((16, width), BF16)
    none = jnp.zeros((16, width), BF16)
    total = None
    for piece in range(rows):
        rows_at = jnp.broadcast_to(row_id[piece : piece + 1], (16, width)).astype(BF16)
        lanes_at = jnp.broadcast_to(lane_id[piece : piece + 1], (16, width)).astype(BF16)
        row_hot = jnp.concatenate([jnp.where(rows_at == at, one, none) for at in steps], axis=0)
        lane_hot = jnp.concatenate([jnp.where(lanes_at == at, one, none) for at in steps[:8]], axis=0)
        found = lax.dot_general(row_hot, lane_hot, NT, preferred_element_type=F32)
        total = found if total is None else total + found
    return total


def owner_rows(block_rows, half):
    return [
        jnp.concatenate([block_rows[i : i + 1, 0:half], block_rows[i + 4 : i + 5, 0:half]], axis=1) for i in range(4)
    ]


def owner_tables(rows):
    pos_x, pos_y, pos_z, charge = rows
    basis_x = jnp.concatenate([charge * part for part in first_basis(pos_x)], axis=0)
    basis_y = second_basis(pos_y)
    third = third_basis(pos_z)
    lanes = jnp.concatenate([third, third * basis_y[0][1:2], third * basis_y[1][1:2]], axis=0)
    high, low = split_two(lanes)
    gap = jnp.zeros((256 - 6 * HARM, third.shape[1]), BF16)
    high = jnp.concatenate([high, gap], axis=0)
    low = jnp.concatenate([low, gap], axis=0)
    return basis_x, basis_y, high, low


def stem_rows(part, basis_y):
    return [second_row(basis_y, harmonic, sine) for harmonic, sine in STEMS[part]]


def store_rows(basis_x, basis_y, charge, v_ref):
    all_rows = sum(SUM_ROWS)
    slots = charge.shape[1]
    at = 0
    for part in range(2):
        stems = stem_rows(part, basis_y)
        index = lax.broadcasted_iota(jnp.int32, (8, slots), 0)
        sines = [index == harmonic % 8 + 1 for harmonic, sine in STEMS[part] if sine]
        tail = jnp.where(jnp.logical_or(*sines), pltpu.roll(basis_y[2 * part + 1], 1, 0), basis_y[2 * part])
        rows = [stem * basis_x for stem in stems] + [charge * tail]
        fill = SUM_ROWS[part] - BASIS * len(stems) - 8
        if fill:
            rows.append(jnp.zeros((fill, slots), F32))
        rows = jnp.concatenate(rows, axis=0)
        for begin in range(0, SUM_ROWS[part], 16):
            high, low = split_two(rows[begin : begin + 16])
            v_ref[at : at + 16] = high
            v_ref[all_rows + at : all_rows + at + 16] = low
            at += 16


def add_owners(owners, base_ref, table_ref, v_ref):
    all_rows = sum(SUM_ROWS)
    highs, lows = [], []
    for i, ions in enumerate(owners):
        slots = ions[3].shape[1]
        basis_x, basis_y, high, low = owner_tables(ions)
        store_rows(basis_x, basis_y, ions[3], v_ref.at[:, i * slots : (i + 1) * slots])
        highs.append(high)
        lows.append(low)
    width = sum(high.shape[1] for high in highs)
    both = lax.dot_general(v_ref[:, 0:width], jnp.concatenate(highs, axis=1), NT, preferred_element_type=F32)
    rest = lax.dot_general(v_ref[0:all_rows, 0:width], jnp.concatenate(lows, axis=1), NT, preferred_element_type=F32)
    total = (both[:all_rows] + both[all_rows:]) + rest
    at = 0
    for part in range(2):
        count, begin = SUM_ROWS[part], PART_AT[part]
        for half in range(2):
            rows = slice(begin + half * count, begin + (half + 1) * count)
            value = total[at : at + count, 128 * half : 128 * half + 128]
            table_ref[rows] = value if base_ref is None else base_ref[rows] + value
        at += count


def add_arrivals(block_rows, rows, half, cap, place, pack, targets, table_ref):
    block = half + 128
    slots = 2 * half
    send = jnp.concatenate([block_rows[p : p + 1, half:block] for p in range(slots // 128)], axis=1)
    step = lax.broadcasted_iota(jnp.int32, (16, slots), 0).astype(F32)
    one, none = jnp.ones((16, slots), BF16), jnp.zeros((16, slots), BF16)
    hots = []
    for target in targets:
        rank = send - (target * cap).astype(F32)
        valid = jnp.logical_and(rank >= 0.0, rank < float(cap))
        key = jnp.broadcast_to(jnp.where(valid, rank + place, -1.0), (16, slots)).astype(BF16)
        hots += [jnp.where(key == (step + 16.0 * i).astype(BF16), one, none) for i in range(4)]
    values = jnp.concatenate(rows + [jnp.zeros((4, slots), F32)], axis=0)
    found = lax.dot_general(split_three(values), jnp.concatenate(hots, axis=0), NT, preferred_element_type=F32)
    row = ARRIVE_AT + 8 * pack
    if not isinstance(row, int):
        row = pl.multiple_of(row, 8)
    table_ref[pl.ds(row, 8)] += (found[0:8] + found[8:16]) + found[16:24]


def split_three(value):
    high = value.astype(BF16).astype(F32)
    rest = value - high
    mid = rest.astype(BF16).astype(F32)
    return jnp.concatenate([high, mid, rest - mid], axis=0).astype(BF16)


def count_kernel(rows, width, waves_hbm, out_ref, waves_ref, stack_ref, sem):
    copy = pltpu.make_async_copy(waves_hbm, waves_ref, sem)
    copy.start()
    copy.wait()
    for row in range(rows):
        for comp in range(3):
            stack_ref[row : row + 1, comp * width : (comp + 1) * width] = waves_ref[
                comp : comp + 1, row * width : (row + 1) * width
            ].astype(F32)
    counts = count_waves(stack_ref, rows, width)
    for row in range(0, COUNT_ROWS, 8):
        out_ref[:, 16 * row : 16 * row + 128] = counts[row : row + 8]


def sums_kernel(plan, *refs):
    refs = list(refs)
    base_ref = refs.pop(0) if plan["has_base"] else None
    ion_refs = [refs.pop(0) for _ in plan["chunks"]]
    table_ref = refs.pop(0)
    v_ref = refs.pop(0)
    half, cap, row_count = plan["half"], plan["cap"], plan["row_count"]
    block = half + 128
    per_pack = 64 // cap
    device = lax.axis_index("blk") * row_count + lax.axis_index("row")
    targets = (device, device ^ row_count)
    kept = slice(ARRIVE_AT, table_ref.shape[0])
    table_ref[kept] = jnp.zeros_like(table_ref[kept]) if base_ref is None else base_ref[kept]

    for ions_ref, (owners, first_owner) in zip(ion_refs, plan["chunks"]):
        if owners <= 4 and per_pack == 1:
            for owner in range(0, owners, 2):
                group = []
                for i in range(owner, min(owner + 2, owners)):
                    block_rows = ions_ref[:, i * block : (i + 1) * block]
                    group.append(owner_rows(block_rows, half))
                    add_arrivals(block_rows, group[-1], half, cap, 0.0, first_owner + i, targets, table_ref)
                add_owners(group, base_ref, table_ref, v_ref)
                base_ref = table_ref
        else:
            if base_ref is not table_ref:
                sums = slice(0, ARRIVE_AT)
                table_ref[sums] = jnp.zeros_like(table_ref[sums]) if base_ref is None else base_ref[sums]
                base_ref = table_ref

            def step(owner, carry, ions_ref=ions_ref, first_owner=first_owner):
                begin = pl.multiple_of(owner * block, 128)
                index = first_owner + owner
                place = (lax.rem(index, per_pack) * cap).astype(F32)
                block_rows = ions_ref[:, pl.ds(begin, block)]
                ions = owner_rows(block_rows, half)
                add_arrivals(block_rows, ions, half, cap, place, index // per_pack, targets, table_ref)
                add_owners([ions], table_ref, table_ref, v_ref)
                return carry

            lax.fori_loop(0, owners, step, 0)


SLOPE_X, BASIS_Y, SLOPE_Y, BASIS_ROWS = 24, 48, 80, 112


def store_bases(ions, basis_ref, z_ref):
    count = ions.shape[1]
    basis_x = first_basis(ions[0:1])
    basis_y = second_basis(ions[1:2])
    parts = basis_x + first_slopes(basis_x) + basis_y + second_slopes(basis_y)
    for i, part in enumerate(parts):
        basis_ref[8 * i : 8 * i + 8] = part
    plain = third_basis(ions[2:3])
    harm = lax.broadcasted_iota(jnp.int32, (HARM, count), 0).astype(F32) + 1.0
    slope = jnp.concatenate([-harm * plain[HARM:], harm * plain[:HARM]], axis=0)
    for i, table in enumerate((plain, slope)):
        high, low = split_two(table)
        z_ref[:, i * count : (i + 1) * count] = jnp.concatenate(
            [high, low, high, jnp.zeros((256 - 6 * HARM, count), BF16)], axis=0
        )


def own_kernel(half, cap, row_count, bits, data_ref, recv_ref, basis_ref, z_ref, hot_ref, gain_ref):
    store_bases(jnp.concatenate([data_ref[0:4, 0:half], data_ref[4:8, 0:half]], axis=1), basis_ref, z_ref)
    atoms_dev = recv_ref.shape[0]
    device = lax.axis_index("blk") * row_count + lax.axis_index("row")
    key = key_of_rows(recv_ref[...].reshape(1, atoms_dev), device, cap, row_count, bits)
    spot = lax.broadcasted_iota(jnp.int32, hot_ref.shape, 0)
    hot_ref[...] = jnp.where(spot == key, 1.0, 0.0).astype(BF16)
    gain_ref[...] = dense_weights()


def swap(parts):
    return [parts[1], parts[0], pltpu.roll(parts[2], 4, 0)]


def store_coefs(part, core, gain_ref, count_refs, coef_ref):
    lane = lax.broadcasted_iota(jnp.int32, (8, 128), 1)
    is_cos = lane < HARM
    is_wave = lane < 2 * HARM

    def gains(row):
        at = COUNT_AT[part] + row
        half = 2 * at // COUNT_ROWS
        lanes = slice(16 * at - 8 * COUNT_ROWS * half, 16 * at - 8 * COUNT_ROWS * half + 128)
        tile = jnp.where(core == half, count_refs[0][:, lanes], count_refs[1][:, lanes]) * gain_ref[at : at + 8]
        back, far = pltpu.roll(tile, 88, 1), pltpu.roll(tile, 48, 1)
        pairs = ((tile, pltpu.roll(tile, HARM, 1)), (back, tile), (far, back))
        return [jnp.where(is_cos, a, jnp.where(is_wave, b, 0.0)) for a, b in pairs]

    order = ORDERS[part]
    pairs = {}
    for i, name in enumerate(order):
        gain = gains(8 * i)
        other = swap(gain)
        pairs[name] = [a + b for a, b in zip(gain, other)], [a - b for a, b in zip(gain, other)]
    for i, (harmonic, sine) in enumerate(order):
        both, odd = pairs[(harmonic, sine)]
        both_o, odd_o = pairs.get((harmonic, 1 - sine), (None, None))
        for x in range(3):
            row = FORCE_AT[part] + BASIS * i + 8 * x
            if both_o is None:
                coefs = (both[x], odd[x])
            else:
                coefs = (both[x] + both_o[x], odd[x] + odd_o[x], both[x] - both_o[x], odd[x] - odd_o[x])
            for kind, coef in enumerate(coefs):
                coef_ref[kind, row : row + 8] = coef
    tails = [gains(COUNT_LEN[part] - 16 + 8 * sine)[0] for sine in range(2)]
    for sine in range(2):
        row = FORCE_AT[part] + BASIS * len(order) + 8 * sine
        coef_ref[0, row : row + 8] = tails[sine] + tails[1 - sine]
        coef_ref[2, row : row + 8] = tails[sine] - tails[1 - sine]


def coef_kernel(gain_ref, count_ref, other_count_ref, coef_ref):
    core = lax.axis_index("blk") % 2
    for part in range(2):
        store_coefs(part, core, gain_ref, (count_ref, other_count_ref), coef_ref)


def weighted_sums(part, mine_ref, other_ref, coef_ref, w_ref):
    lane = lax.broadcasted_iota(jnp.int32, (8, 128), 1)
    is_cos = lane < HARM
    is_wave = lane < 2 * HARM
    count = SUM_ROWS[part]

    def both(row):
        row = PART_AT[part] + row
        return mine_ref[row : row + 8] + other_ref[row : row + 8]

    def blocks(row):
        near, far = both(row), both(count + row)
        middle = jnp.where(lane < 48, pltpu.roll(near, 48, 1), pltpu.roll(far, 48, 1))
        return [jnp.where(is_wave, value, 0.0) for value in (near, middle, pltpu.roll(far, 96, 1))]

    def turn(sums):
        return jnp.where(is_cos, pltpu.roll(sums, 88, 1), -pltpu.roll(sums, HARM, 1))

    def harmonics_of(stem):
        found = {}
        for harmonic, _ in STEMS[part]:
            if harmonic == 0:
                plain, cos_1, sin_1 = stem[(0, 0)]
                found.update({(0, 0): plain, (1, 0): cos_1, (1, 1): sin_1})
                continue
            cos, sin = stem[(harmonic, 0)], stem[(harmonic, 1)]
            found[(harmonic, 0)], found[(harmonic, 1)] = cos[0], sin[0]
            found[(harmonic - 1, 0)] = cos[1] + sin[2]
            found[(harmonic - 1, 1)] = sin[1] - cos[2]
            found[(harmonic + 1, 0)] = cos[1] - sin[2]
            found[(harmonic + 1, 1)] = sin[1] + cos[2]
        return found

    def store(row, value):
        high, low = split_two(value)
        high = high.astype(F32)
        low = low.astype(F32)
        turned = pltpu.roll(high, 2 * HARM, 1)
        row = FORCE_AT[part] + row
        w_ref[row : row + 8, 0:128] = jnp.where(is_wave, high, turned)
        w_ref[row : row + 8, 128:256] = jnp.where(lane < 32, turned, pltpu.roll(low, 32, 1))

    by_block = [
        harmonics_of({stem: blocks(BASIS * i + 8 * x) for i, stem in enumerate(STEMS[part])}) for x in range(3)
    ]
    order = ORDERS[part]
    groups = {}
    for name in order:
        sums = [by_block[x][name] for x in range(3)]
        turned = [turn(value) for value in sums]
        groups[name] = swap(sums), turned, swap(turned)
    for i, (harmonic, sine) in enumerate(order):
        turned_s = groups[(harmonic, sine)][2]
        for x in range(3):
            row = BASIS * i + 8 * x
            coefs = [coef_ref[kind, FORCE_AT[part] + row : FORCE_AT[part] + row + 8] for kind in range(4)]
            value = coefs[0] * by_block[x][(harmonic, sine)] - coefs[1] * turned_s[x]
            if harmonic:
                sums_os, turned_o, _ = groups[(harmonic, 1 - sine)]
                value = value - coefs[2] * turned_o[x] - coefs[3] * sums_os[x]
            store(row, value)
    tail = blocks(BASIS * len(STEMS[part]))
    found = harmonics_of({(h, sine): [b[h % 8 + sine : h % 8 + sine + 1] for b in tail] for h, sine in STEMS[part]})
    index = lax.broadcasted_iota(jnp.int32, (8, 128), 0)
    kinds = []
    for sine in range(2):
        rows = jnp.zeros((8, 128), F32)
        for harmonic, kind in order:
            if kind == sine:
                rows = jnp.where(index == harmonic % 8, found[(harmonic, kind)], rows)
        kinds.append((rows, turn(rows)))
    at = BASIS * len(order)
    for sine in range(2):
        row = FORCE_AT[part] + at + 8 * sine
        store(at + 8 * sine, coef_ref[0, row : row + 8] * kinds[sine][0] - coef_ref[2, row : row + 8] * kinds[1 - sine][1])
    if at + 16 < FORCE_ROWS[part]:
        fill = FORCE_ROWS[part] - at - 16
        w_ref[FORCE_AT[part] + at + 16 : FORCE_AT[part] + FORCE_ROWS[part]] = jnp.zeros((fill, 256), F32)


def pull(weights, basis_ref, z_ref, count, begin, tile):
    lanes = slice(begin, begin + tile)
    plain = jnp.dot(weights, z_ref[:, begin : begin + tile], preferred_element_type=F32)
    sloped = jnp.dot(weights, z_ref[:, count + begin : count + begin + tile], preferred_element_type=F32)
    zero = jnp.zeros((8, tile), F32)
    even, slope, third = [zero] * 3, [zero] * 3, [zero] * 3
    sum_y = sum_z = zero
    for part in range(2):
        for place, (harmonic, sine) in enumerate(ORDERS[part]):
            at = 16 * (harmonic // 8) + 8 * sine + harmonic % 8
            basis = basis_ref[BASIS_Y + at : BASIS_Y + at + 1, lanes]
            basis_slope = basis_ref[SLOPE_Y + at : SLOPE_Y + at + 1, lanes]
            for i in range(3):
                row = FORCE_AT[part] + BASIS * place + 8 * i
                plain_rows, sloped_rows = plain[row : row + 8], sloped[row : row + 8]
                if harmonic == 0:
                    even[i] = even[i] + plain_rows
                    third[i] = third[i] + sloped_rows
                else:
                    even[i] = even[i] + basis * plain_rows
                    slope[i] = slope[i] + basis_slope * plain_rows
                    third[i] = third[i] + basis * sloped_rows
        for sine in range(2):
            row = FORCE_AT[part] + BASIS * len(ORDERS[part]) + 8 * sine
            at = 16 * part + 8 * sine
            sum_y = sum_y + basis_ref[SLOPE_Y + at : SLOPE_Y + at + 8, lanes] * plain[row : row + 8]
            sum_z = sum_z + basis_ref[BASIS_Y + at : BASIS_Y + at + 8, lanes] * sloped[row : row + 8]
    sum_x = zero
    for i in range(3):
        rows_x = basis_ref[8 * i : 8 * i + 8, lanes]
        sum_x = sum_x + basis_ref[SLOPE_X + 8 * i : SLOPE_X + 8 * i + 8, lanes] * even[i]
        sum_y = sum_y + rows_x * slope[i]
        sum_z = sum_z + rows_x * third[i]
    return [jnp.sum(value, axis=0, keepdims=True) for value in (sum_x, sum_y, sum_z)]


TILE = 256


def force_kernel(
    force_scale, half, mine_ref, other_ref, data_ref, basis_ref, z_ref, hot_ref, coef_ref,
    slot_ref, atom_ref, w_ref, atom_basis_ref, atom_z_ref,
):
    packs = hot_ref.shape[0] // 128
    lane = lax.broadcasted_iota(jnp.int32, (8, 128), 1)
    starts = [ARRIVE_AT + 8 * p for p in range(packs)]
    pool = jnp.concatenate([jnp.where(lane < 64, mine_ref[r : r + 8], other_ref[r : r + 8]) for r in starts], axis=1)
    found = jnp.dot(split_three(pool), hot_ref[...], preferred_element_type=F32)
    routed = ((found[0:8] + found[8:16]) + found[16:24])[0:4]
    for part in range(2):
        weighted_sums(part, mine_ref, other_ref, coef_ref, w_ref)
    weights = w_ref[...].astype(BF16)
    store_bases(routed, atom_basis_ref, atom_z_ref)
    charge = jnp.concatenate([data_ref[3:4, 0:half], data_ref[7:8, 0:half]], axis=1)
    jobs = ((basis_ref, z_ref, charge, slot_ref), (atom_basis_ref, atom_z_ref, routed[3:4], atom_ref))
    for rows_ref, table_ref, charges, out_ref in jobs:
        count = out_ref.shape[1]
        for begin in range(0, count, TILE):
            lanes = slice(begin, begin + TILE)
            gain = (-DOUBLE_PI * force_scale) * charges[:, lanes]
            gains = (gain, gain, gain / BOX_Z)
            found = pull(weights, rows_ref, table_ref, count, begin, TILE)
            out_ref[:, lanes] = jnp.concatenate([gains[i] * found[i] for i in range(3)], axis=0)


def params():
    return pltpu.CompilerParams(vmem_limit_bytes=VMEM_BYTES)


def stay(value):
    return pltpu.with_memory_space_constraint(value, pltpu.HBM)


def whole(count):
    return [pl.BlockSpec(memory_space=pltpu.VMEM)] * count


def body(coords, charges, counts, send_slot, recv_index, wave_ints):
    slots = charges.shape[0]
    half = slots // 2
    block = half + 128
    atoms_dev = recv_index.shape[0]
    devices = lax.axis_size(("blk", "row"))
    blk_count = lax.axis_size("blk")
    row_count = lax.axis_size("row")
    k_local = wave_ints.shape[1]
    cap = 2 * atoms_dev // devices
    packs = max(1, devices // 2 * cap // 64)
    per_pack = 64 // cap
    wave_rows, wave_width = wave_shape(k_local)
    force_scale = FORCE_GAIN / math.sqrt(float(atoms_dev * devices * blk_count * k_local))
    table_shape = jax.ShapeDtypeStruct((ARRIVE_AT + 8 * packs, 128), F32)
    count_shape = jax.ShapeDtypeStruct((8, 16 * COUNT_ROWS), F32)

    with jax.named_scope("payload"):
        own_ions = pl.pallas_call(
            prep_kernel,
            out_shape=jax.ShapeDtypeStruct((8, block), F32),
            in_specs=[pl.BlockSpec(memory_space=pltpu.HBM)] * 4,
            out_specs=whole(1)[0],
            scratch_shapes=[
                pltpu.VMEM(coords.shape, F32),
                pltpu.VMEM(charges.shape, F32),
                pltpu.SMEM(counts.shape, jnp.int32),
                pltpu.VMEM(send_slot.shape, jnp.int32),
                pltpu.SemaphoreType.DMA((4,)),
            ],
            compiler_params=params(),
        )(stay(coords), stay(charges), counts, stay(send_slot))

    def flip(value, blk_bit, row_bit):
        if not row_bit:
            return lax.ppermute(value, "blk", [(i, i ^ blk_bit) for i in range(blk_count)])
        if not blk_bit:
            return lax.ppermute(value, "row", [(i, i ^ row_bit) for i in range(row_count)])
        distance = row_count * blk_bit + row_bit
        return lax.ppermute(value, ("blk", "row"), [(i, i ^ distance) for i in range(devices)])

    def joined(values):
        return values[0] if len(values) == 1 else jnp.concatenate(values, axis=1)

    def accumulate(table, chunks, cost=1):
        plan = {
            "has_base": table is not None,
            "chunks": [chunk[1:] for chunk in chunks],
            "half": half,
            "cap": cap,
            "row_count": row_count,
        }
        args = [table] * plan["has_base"] + [chunk[0] for chunk in chunks]
        flops = int(cost * 2 * sum(chunk[1] for chunk in chunks) * slots * 256 * 720)
        with jax.named_scope("structure_sums"):
            return pl.pallas_call(
                functools.partial(sums_kernel, plan),
                out_shape=table_shape,
                in_specs=whole(len(args)),
                out_specs=whole(1)[0],
                scratch_shapes=[pltpu.VMEM((2 * sum(SUM_ROWS), 2 * slots), BF16)],
                compiler_params=params(),
                cost_estimate=pl.CostEstimate(flops=flops, bytes_accessed=1 << 20, transcendentals=0),
            )(*args)

    steps = []
    bit = row_count // 2
    while bit >= 2:
        steps.append((0, bit))
        bit //= 2
    bit = 4
    while bit < blk_count:
        steps.append((bit, 0))
        bit *= 2
    bits = [row_count * blk_bit + row_bit for blk_bit, row_bit in steps] + [2 * row_count, 1]
    table, counted = None, None
    ions, held, chunks = [own_ions], 1, [(own_ions, 1, 0)]
    for blk_bit, row_bit in steps:
        with jax.named_scope("exchange_ions"):
            got = flip(joined(ions), blk_bit, row_bit)
        if blk_bit:
            with jax.named_scope("exchange_counts"):
                counted = counted + flip(counted, blk_bit, 0)
        if counted is None:
            with jax.named_scope("counts"):
                counted = pl.pallas_call(
                    functools.partial(count_kernel, wave_rows, wave_width),
                    out_shape=count_shape,
                    in_specs=[pl.BlockSpec(memory_space=pltpu.HBM)],
                    out_specs=whole(1)[0],
                    scratch_shapes=[
                        pltpu.VMEM(wave_ints.shape, jnp.int32),
                        pltpu.VMEM((wave_rows, 3 * wave_width), F32),
                        pltpu.SemaphoreType.DMA,
                    ],
                    compiler_params=params(),
                    cost_estimate=pl.CostEstimate(
                        flops=2 * k_local * COUNT_ROWS * 128, bytes_accessed=1 << 20, transcendentals=0
                    ),
                )(stay(wave_ints))
            got, counted = lax.optimization_barrier((got, counted))
        else:
            table, chunks = accumulate(table, chunks), []
            got, table = lax.optimization_barrier((got, table))
        chunks = chunks + [(got, held, held)]
        ions = ions + [got]
        held *= 2
    low = lax.axis_index("blk") % 2 == 0
    halves = counted[:, : 8 * COUNT_ROWS], counted[:, 8 * COUNT_ROWS :]
    with jax.named_scope("exchange_counts"):
        near = flip(jnp.where(low, halves[1], halves[0]), 1, 0)
        counted = jnp.where(low, halves[0], halves[1]) + near
    with jax.named_scope("exchange_ions"):
        sent = joined(ions)
        corner = flip(sent, 2, 1)
        along = flip(sent, 0, 1)
        across = flip(jnp.concatenate([sent, counted], axis=1), 2, 0)
    table = accumulate(table, chunks, cost=8)
    table = accumulate(table, [(corner, held, 3 * held)], cost=0.3)
    table = accumulate(table, [(along, held, 2 * held)], cost=0.3)
    with jax.named_scope("exchange_core"):
        counted = counted + across[:, held * block :]
        other_counted = flip(counted, 1, 0)
    across, table, counted = lax.optimization_barrier((across, table, counted))
    table = accumulate(table, [(across, held, held)], cost=1)
    with jax.named_scope("exchange_core"):
        other = flip(table, 1, 0)
    own_ions, recv_index, table = lax.optimization_barrier((own_ions, recv_index, table))
    with jax.named_scope("own_ions"):
        basis, table_z, hot, gain = pl.pallas_call(
            functools.partial(own_kernel, half, cap, row_count, bits),
            out_shape=(
                jax.ShapeDtypeStruct((BASIS_ROWS, slots), F32),
                jax.ShapeDtypeStruct((256, 2 * slots), BF16),
                jax.ShapeDtypeStruct((128 * packs, atoms_dev), BF16),
                jax.ShapeDtypeStruct((COUNT_ROWS, 128), F32),
            ),
            in_specs=whole(2),
            out_specs=tuple(whole(4)),
            compiler_params=params(),
            cost_estimate=pl.CostEstimate(flops=1<<33, bytes_accessed=1 << 20, transcendentals=0),
        )(own_ions, recv_index)
    with jax.named_scope("coefficients"):
        coefs = pl.pallas_call(
            coef_kernel,
            out_shape=jax.ShapeDtypeStruct((4, sum(FORCE_ROWS), 128), F32),
            in_specs=whole(3),
            out_specs=whole(1)[0],
            compiler_params=params(),
            cost_estimate=pl.CostEstimate(flops=1<<33, bytes_accessed=1 << 20, transcendentals=0),
        )(gain, counted, other_counted)
    with jax.named_scope("forces"):
        return pl.pallas_call(
            functools.partial(force_kernel, force_scale, half),
            out_shape=(
                jax.ShapeDtypeStruct((3, slots), F32),
                jax.ShapeDtypeStruct((3, atoms_dev), F32),
            ),
            in_specs=whole(7),
            out_specs=tuple(whole(2)),
            scratch_shapes=[
                pltpu.VMEM((sum(FORCE_ROWS), 256), F32),
                pltpu.VMEM((BASIS_ROWS, atoms_dev), F32),
                pltpu.VMEM((256, 2 * atoms_dev), BF16),
            ],
            compiler_params=params(),
        )(table, other, own_ions, basis, table_z, hot, coefs)


def solution(mesh):
    placed = (
        P(None, ("groups", "blk", "row")),
        P(("groups", "blk", "row")),
        P(("groups", "blk", "row")),
        P(("groups", "blk", "row")),
        P(("groups", "blk", "row")),
        P(None, "blk"),
    )
    return jax.shard_map(
        body,
        mesh=mesh,
        in_specs=placed,
        out_specs=(P(None, ("groups", "blk", "row")), P(None, ("groups", "blk", "row"))),
        check_vma=False,
    )
```

```python
import functools
import math

import jax
import jax.numpy as jnp
from jax import lax
from jax.experimental import pallas as pl
from jax.experimental.pallas import tpu as pltpu
from jax.sharding import PartitionSpec as P

DOUBLE_PI = 2.0 * math.pi
EWALD_BETA = 30.0
BOX_Z = 3.0
FORCE_GAIN = 400.0
SIN_POLY = (6.283185, -41.34159, 81.599945, -76.61447, 41.342884, -12.471244)
COS_POLY = (1.0, -19.739204, 64.93912, -85.45014, 60.16763, -25.9676, 6.5286584)

BASIS = 24
HARM = 40
STEMS = (((0, 0), (3, 0), (3, 1), (6, 0), (6, 1)), ((9, 0), (9, 1), (12, 0), (12, 1)))
SUM_ROWS = (144, 112)
ORDERS = (
    tuple((k, 0) for k in range(8)) + tuple((k, 1) for k in range(1, 8)),
    tuple((k, 0) for k in range(8, 13)) + tuple((k, 1) for k in range(8, 13)),
)
COUNT_ROWS = 240
COUNT_AT = (0, 136)
COUNT_LEN = (136, 96)
FORCE_ROWS = (384, 256)
FORCE_AT = (0, 384)
PART_AT = (0, 2 * SUM_ROWS[0])
ARRIVE_AT = PART_AT[1] + 2 * SUM_ROWS[1]
F32 = jnp.float32
BF16 = jnp.bfloat16
NT = (((1,), (1,)), ((), ()))
VMEM_BYTES = 40 * 1024 * 1024


def horner(coefs, v):
    total = jnp.full_like(v, coefs[-1])
    for coef in coefs[-2::-1]:
        total = total * v + coef
    return total


def harmonics(pos, first):
    harm = lax.broadcasted_iota(jnp.int32, (8, pos.shape[1]), 0).astype(F32) + float(first)
    turns = harm * pos
    turns = turns - jnp.floor(turns + 0.5)
    square = turns * turns
    return horner(COS_POLY, square), turns * horner(SIN_POLY, square)


def advance(first, by):
    cos_a, sin_a = first
    cos_b, sin_b = by
    return cos_a * cos_b - sin_a * sin_b, sin_a * cos_b + cos_a * sin_b


def row_of(pair, row):
    return pair[0][row : row + 1], pair[1][row : row + 1]


def merge_last(cos_part, sin_part):
    low = lax.broadcasted_iota(jnp.int32, cos_part.shape, 0) < 4
    return jnp.where(low, cos_part, pltpu.roll(sin_part, 4, 0))


def first_basis(pos):
    first = harmonics(pos, 1)
    second = advance(first, row_of(first, 7))
    return [first[0], first[1], merge_last(*second)]


def first_slopes(basis):
    row = lax.broadcasted_iota(jnp.int32, basis[0].shape, 0)
    harm = row.astype(F32) + 1.0
    low = row < 4
    factor = jnp.where(low, -(harm + 8.0), harm + 4.0)
    return [-harm * basis[1], harm * basis[0], factor * pltpu.roll(basis[2], 4, 0)]


def second_basis(pos):
    first = harmonics(pos, 0)
    fourth = row_of(first, 4)
    second = advance(first, advance(fourth, fourth))
    return [first[0], first[1], second[0], second[1]]


def second_slopes(basis):
    harm = lax.broadcasted_iota(jnp.int32, basis[0].shape, 0).astype(F32)
    high = harm + 8.0
    return [-harm * basis[1], harm * basis[0], -high * basis[3], high * basis[2]]


def second_row(basis, harmonic, sine):
    return basis[2 * (harmonic // 8) + sine][harmonic % 8 : harmonic % 8 + 1]


def third_basis(pos):
    first = harmonics(pos, 1)
    second = advance(first, row_of(first, 7))
    third = advance(first, row_of(second, 7))
    fourth = advance(second, row_of(second, 7))
    fifth = advance(first, row_of(fourth, 7))
    parts = (first, second, third, fourth, fifth)
    return jnp.concatenate([p[0] for p in parts] + [p[1] for p in parts], axis=0)


def split_two(value):
    high = value.astype(BF16)
    return high, (value - high.astype(F32)).astype(BF16)


def key_of_rows(recv, device, cap, row_count, bits):
    per_pack = 64 // cap
    source = (recv // cap) ^ device
    order = jnp.zeros_like(source)
    for place, distance in enumerate(bits):
        order = order | jnp.where((source & distance) != 0, 1 << place, 0)
    far = jnp.where((source & row_count) != 0, 64, 0)
    return (order // per_pack) * 128 + far + (order % per_pack) * cap + recv % cap


def prep_kernel(
    coords_hbm, charges_hbm, counts_hbm, send_hbm, out_ref, coords_ref, charges_ref, counts_ref, send_ref, sems
):
    copies = [
        pltpu.make_async_copy(source, target, sems.at[i])
        for i, (source, target) in enumerate(
            (
                (counts_hbm, counts_ref),
                (send_hbm, send_ref),
                (charges_hbm, charges_ref),
                (coords_hbm, coords_ref),
            )
        )
    ]
    for copy in copies:
        copy.start()
    slots = charges_ref.shape[0]
    half = slots // 2
    out_ref[:, 0 : half + 128] = jnp.zeros((8, half + 128), F32)
    for copy in copies:
        copy.wait()
    live = lax.broadcasted_iota(jnp.int32, (1, slots), 1) < counts_ref[0]
    charge = jnp.where(live, charges_ref[...].reshape(1, slots), 0.0)
    send = jnp.where(live, send_ref[...].reshape(1, slots), -1).astype(F32)
    for part in range(2):
        lanes = slice(part * half, (part + 1) * half)
        out_ref[4 * part : 4 * part + 3, 0:half] = coords_ref[:, lanes]
        out_ref[4 * part + 3 : 4 * part + 4, 0:half] = charge[:, lanes]
    for piece in range(slots // 128):
        out_ref[piece : piece + 1, half : half + 128] = send[:, piece * 128 : (piece + 1) * 128]


def wave_shape(k_local):
    rows = 8
    while k_local % (rows * 128):
        rows //= 2
    return rows, k_local // rows


def basis_row(index):
    size = jnp.abs(index)
    sign = jnp.where(index < 0.0, 1.0, 0.0)
    row = jnp.where(size <= 8.0, size - 1.0 + 8.0 * sign, size + 7.0 + 4.0 * sign)
    return jnp.where(size == 0.0, float(BASIS), row)


def basis_size(row):
    low = jnp.where(row < 8, row, row - 8) + 1
    high = jnp.where(row < 20, row - 16, row - 20) + 9
    return jnp.where(row < 16, low, jnp.where(row < BASIS, high, 0))


def dense_weights():
    row = lax.broadcasted_iota(jnp.int32, (COUNT_ROWS, 128), 0)
    lane = lax.broadcasted_iota(jnp.int32, (COUNT_ROWS, 128), 1)
    early = row < COUNT_AT[1]
    own = jnp.where(early, row, row - COUNT_AT[1])
    paired = own < jnp.where(early, COUNT_LEN[0] - 16, COUNT_LEN[1] - 16)
    group = own // 8
    size_y = jnp.where(early, jnp.where(group < 8, group, group - 7), 8 + jnp.where(group < 5, group, group - 5))
    size_y = jnp.where(paired, size_y, jnp.where(early, own % 8, 8 + own % 8))
    part = jnp.where(lane < HARM, 0, jnp.where(lane < 2 * HARM, 1, 2))
    size_x = jnp.where(paired, basis_size(own % 8 + 8 * part), 0)
    phys_x = DOUBLE_PI * size_x.astype(F32)
    phys_y = DOUBLE_PI * size_y.astype(F32)
    phys_z = DOUBLE_PI * (lane - HARM * part + 1).astype(F32) / BOX_Z
    k_squared = phys_x * phys_x + phys_y * phys_y + phys_z * phys_z
    return jnp.exp(-k_squared / (4.0 * EWALD_BETA * EWALD_BETA)) / k_squared


def count_waves(waves, rows, width):
    wave_h = waves[0:rows, 0:width]
    wave_k = waves[0:rows, width : 2 * width]
    wave_l = waves[0:rows, 2 * width : 3 * width]
    flip = jnp.where(wave_l < 0.0, -1.0, 1.0)
    row_x = basis_row(wave_h * flip)
    wave_k = wave_k * flip
    size_y = jnp.abs(wave_k)
    sine = jnp.where(wave_k < 0.0, 1.0, 0.0)
    const = row_x == float(BASIS)
    part = jnp.where(row_x >= 16.0, 2.0, jnp.where(row_x >= 8.0, 1.0, 0.0))
    part = jnp.where(const, 0.0, part)
    late = size_y >= 8.0
    group = jnp.where(late, size_y - 8.0 + 5.0 * sine, size_y + 7.0 * sine)
    paired_id = 8.0 * group + (row_x - 8.0 * part) + jnp.where(late, float(COUNT_AT[1]), 0.0)
    tail = jnp.where(late, size_y - 8.0 + float(COUNT_AT[1] + COUNT_LEN[1] - 16), size_y + float(COUNT_LEN[0] - 16))
    row_id = jnp.where(const, tail + 8.0 * sine, paired_id)
    lane_id = wave_l * flip + (HARM * part - 1.0)
    step = lax.broadcasted_iota(jnp.int32, (16, width), 0).astype(F32)
    steps = [(step + 16.0 * i).astype(BF16) for i in range(COUNT_ROWS // 16)]
    one = jnp.ones((16, width), BF16)
    none = jnp.zeros((16, width), BF16)
    total = None
    for piece in range(rows):
        rows_at = jnp.broadcast_to(row_id[piece : piece + 1], (16, width)).astype(BF16)
        lanes_at = jnp.broadcast_to(lane_id[piece : piece + 1], (16, width)).astype(BF16)
        row_hot = jnp.concatenate([jnp.where(rows_at == at, one, none) for at in steps], axis=0)
        lane_hot = jnp.concatenate([jnp.where(lanes_at == at, one, none) for at in steps[:8]], axis=0)
        found = lax.dot_general(row_hot, lane_hot, NT, preferred_element_type=F32)
        total = found if total is None else total + found
    return total


def owner_rows(block_rows, half):
    return [
        jnp.concatenate([block_rows[i : i + 1, 0:half], block_rows[i + 4 : i + 5, 0:half]], axis=1) for i in range(4)
    ]


def owner_tables(rows):
    pos_x, pos_y, pos_z, charge = rows
    basis_x = jnp.concatenate([charge * part for part in first_basis(pos_x)], axis=0)
    basis_y = second_basis(pos_y)
    third = third_basis(pos_z)
    lanes = jnp.concatenate([third, third * basis_y[0][1:2], third * basis_y[1][1:2]], axis=0)
    high, low = split_two(lanes)
    gap = jnp.zeros((256 - 6 * HARM, third.shape[1]), BF16)
    high = jnp.concatenate([high, gap], axis=0)
    low = jnp.concatenate([low, gap], axis=0)
    return basis_x, basis_y, high, low


def stem_rows(part, basis_y):
    return [second_row(basis_y, harmonic, sine) for harmonic, sine in STEMS[part]]


def store_rows(basis_x, basis_y, charge, v_ref):
    all_rows = sum(SUM_ROWS)
    slots = charge.shape[1]
    at = 0
    for part in range(2):
        stems = stem_rows(part, basis_y)
        rows = [stem * basis_x for stem in stems] + [charge * rows for rows in basis_y[2 * part : 2 * part + 2]]
        fill = SUM_ROWS[part] - BASIS * len(stems) - 16
        if fill:
            rows.append(jnp.zeros((fill, slots), F32))
        rows = jnp.concatenate(rows, axis=0)
        for begin in range(0, SUM_ROWS[part], 16):
            high, low = split_two(rows[begin : begin + 16])
            v_ref[at : at + 16] = high
            v_ref[all_rows + at : all_rows + at + 16] = low
            at += 16


def add_owners(owners, base_ref, table_ref, v_ref):
    all_rows = sum(SUM_ROWS)
    highs, lows = [], []
    for i, ions in enumerate(owners):
        slots = ions[3].shape[1]
        basis_x, basis_y, high, low = owner_tables(ions)
        store_rows(basis_x, basis_y, ions[3], v_ref.at[:, i * slots : (i + 1) * slots])
        highs.append(high)
        lows.append(low)
    width = sum(high.shape[1] for high in highs)
    both = lax.dot_general(v_ref[:, 0:width], jnp.concatenate(highs, axis=1), NT, preferred_element_type=F32)
    rest = lax.dot_general(v_ref[0:all_rows, 0:width], jnp.concatenate(lows, axis=1), NT, preferred_element_type=F32)
    total = (both[:all_rows] + both[all_rows:]) + rest
    at = 0
    for part in range(2):
        count, begin = SUM_ROWS[part], PART_AT[part]
        for half in range(2):
            rows = slice(begin + half * count, begin + (half + 1) * count)
            value = total[at : at + count, 128 * half : 128 * half + 128]
            table_ref[rows] = value if base_ref is None else base_ref[rows] + value
        at += count


def add_arrivals(block_rows, rows, half, cap, place, pack, targets, table_ref):
    block = half + 128
    slots = 2 * half
    send = jnp.concatenate([block_rows[p : p + 1, half:block] for p in range(slots // 128)], axis=1)
    step = lax.broadcasted_iota(jnp.int32, (16, slots), 0).astype(F32)
    one, none = jnp.ones((16, slots), BF16), jnp.zeros((16, slots), BF16)
    hots = []
    for target in targets:
        rank = send - (target * cap).astype(F32)
        valid = jnp.logical_and(rank >= 0.0, rank < float(cap))
        key = jnp.broadcast_to(jnp.where(valid, rank + place, -1.0), (16, slots)).astype(BF16)
        hots += [jnp.where(key == (step + 16.0 * i).astype(BF16), one, none) for i in range(4)]
    values = jnp.concatenate(rows + [jnp.zeros((4, slots), F32)], axis=0)
    found = lax.dot_general(split_three(values), jnp.concatenate(hots, axis=0), NT, preferred_element_type=F32)
    row = ARRIVE_AT + 8 * pack
    if not isinstance(row, int):
        row = pl.multiple_of(row, 8)
    table_ref[pl.ds(row, 8)] += (found[0:8] + found[8:16]) + found[16:24]


def split_three(value):
    high = value.astype(BF16).astype(F32)
    rest = value - high
    mid = rest.astype(BF16).astype(F32)
    return jnp.concatenate([high, mid, rest - mid], axis=0).astype(BF16)


def count_kernel(rows, width, waves_hbm, out_ref, waves_ref, stack_ref, sems):
    share = rows * width // COPIES
    copies = [
        pltpu.make_async_copy(
            waves_hbm.at[:, pl.ds(share * i, share)], waves_ref.at[:, pl.ds(share * i, share)], sems.at[i]
        )
        for i in range(COPIES)
    ]
    for copy in copies:
        copy.start()
    for copy in copies:
        copy.wait()
    for row in range(rows):
        for comp in range(3):
            stack_ref[row : row + 1, comp * width : (comp + 1) * width] = waves_ref[
                comp : comp + 1, row * width : (row + 1) * width
            ].astype(F32)
    counts = count_waves(stack_ref, rows, width)
    for row in range(0, COUNT_ROWS, 8):
        out_ref[:, 16 * row : 16 * row + 128] = counts[row : row + 8]


def sums_kernel(plan, *refs):
    refs = list(refs)
    base_ref = refs.pop(0) if plan["has_base"] else None
    ion_refs = [refs.pop(0) for _ in plan["chunks"]]
    table_ref = refs.pop(0)
    v_ref = refs.pop(0)
    half, cap, row_count = plan["half"], plan["cap"], plan["row_count"]
    block = half + 128
    per_pack = 64 // cap
    device = lax.axis_index("blk") * row_count + lax.axis_index("row")
    targets = (device, device ^ row_count)
    kept = slice(ARRIVE_AT, table_ref.shape[0])
    table_ref[kept] = jnp.zeros_like(table_ref[kept]) if base_ref is None else base_ref[kept]

    for ions_ref, (owners, first_owner) in zip(ion_refs, plan["chunks"]):
        if owners <= 4 and per_pack == 1:
            for owner in range(0, owners, 2):
                group = []
                for i in range(owner, min(owner + 2, owners)):
                    block_rows = ions_ref[:, i * block : (i + 1) * block]
                    group.append(owner_rows(block_rows, half))
                    add_arrivals(block_rows, group[-1], half, cap, 0.0, first_owner + i, targets, table_ref)
                add_owners(group, base_ref, table_ref, v_ref)
                base_ref = table_ref
        else:
            if base_ref is not table_ref:
                sums = slice(0, ARRIVE_AT)
                table_ref[sums] = jnp.zeros_like(table_ref[sums]) if base_ref is None else base_ref[sums]
                base_ref = table_ref

            def step(owner, carry, ions_ref=ions_ref, first_owner=first_owner):
                begin = pl.multiple_of(owner * block, 128)
                index = first_owner + owner
                place = (lax.rem(index, per_pack) * cap).astype(F32)
                block_rows = ions_ref[:, pl.ds(begin, block)]
                ions = owner_rows(block_rows, half)
                add_arrivals(block_rows, ions, half, cap, place, index // per_pack, targets, table_ref)
                add_owners([ions], table_ref, table_ref, v_ref)
                return carry

            lax.fori_loop(0, owners, step, 0)


SLOPE_X, BASIS_Y, SLOPE_Y, BASIS_ROWS = 24, 48, 80, 112


def store_bases(ions, basis_ref, z_ref):
    count = ions.shape[1]
    basis_x = first_basis(ions[0:1])
    basis_y = second_basis(ions[1:2])
    parts = basis_x + first_slopes(basis_x) + basis_y + second_slopes(basis_y)
    for i, part in enumerate(parts):
        basis_ref[8 * i : 8 * i + 8] = part
    plain = third_basis(ions[2:3])
    harm = lax.broadcasted_iota(jnp.int32, (HARM, count), 0).astype(F32) + 1.0
    slope = jnp.concatenate([-harm * plain[HARM:], harm * plain[:HARM]], axis=0)
    for i, table in enumerate((plain, slope)):
        high, low = split_two(table)
        z_ref[:, i * count : (i + 1) * count] = jnp.concatenate(
            [high, low, high, jnp.zeros((256 - 6 * HARM, count), BF16)], axis=0
        )


def own_kernel(half, cap, row_count, bits, data_ref, recv_ref, basis_ref, z_ref, hot_ref, gain_ref):
    store_bases(jnp.concatenate([data_ref[0:4, 0:half], data_ref[4:8, 0:half]], axis=1), basis_ref, z_ref)
    atoms_dev = recv_ref.shape[0]
    device = lax.axis_index("blk") * row_count + lax.axis_index("row")
    key = key_of_rows(recv_ref[...].reshape(1, atoms_dev), device, cap, row_count, bits)
    spot = lax.broadcasted_iota(jnp.int32, hot_ref.shape, 0)
    hot_ref[...] = jnp.where(spot == key, 1.0, 0.0).astype(BF16)
    gain_ref[...] = dense_weights()


def swap(parts):
    return [parts[1], parts[0], pltpu.roll(parts[2], 4, 0)]


def store_coefs(part, gain_ref, count_refs, coef_ref):
    lane = lax.broadcasted_iota(jnp.int32, (8, 128), 1)
    is_cos = lane < HARM
    is_wave = lane < 2 * HARM

    def gains(row):
        at = COUNT_AT[part] + row
        lanes = slice(16 * at, 16 * at + 128)
        tile = (count_refs[0][:, lanes] + count_refs[1][:, lanes]) * gain_ref[at : at + 8]
        back, far = pltpu.roll(tile, 88, 1), pltpu.roll(tile, 48, 1)
        pairs = ((tile, pltpu.roll(tile, HARM, 1)), (back, tile), (far, back))
        return [jnp.where(is_cos, a, jnp.where(is_wave, b, 0.0)) for a, b in pairs]

    order = ORDERS[part]
    pairs = {}
    for i, name in enumerate(order):
        gain = gains(8 * i)
        other = swap(gain)
        pairs[name] = [a + b for a, b in zip(gain, other)], [a - b for a, b in zip(gain, other)]
    for i, (harmonic, sine) in enumerate(order):
        both, odd = pairs[(harmonic, sine)]
        both_o, odd_o = pairs.get((harmonic, 1 - sine), (None, None))
        for x in range(3):
            row = FORCE_AT[part] + BASIS * i + 8 * x
            if both_o is None:
                coefs = (both[x], odd[x])
            else:
                coefs = (both[x] + both_o[x], odd[x] + odd_o[x], both[x] - both_o[x], odd[x] - odd_o[x])
            for kind, coef in enumerate(coefs):
                coef_ref[kind, row : row + 8] = coef
    tails = [gains(COUNT_LEN[part] - 16 + 8 * sine)[0] for sine in range(2)]
    for sine in range(2):
        row = FORCE_AT[part] + BASIS * len(order) + 8 * sine
        coef_ref[0, row : row + 8] = tails[sine] + tails[1 - sine]
        coef_ref[2, row : row + 8] = tails[sine] - tails[1 - sine]


def coef_kernel(gain_ref, count_ref, other_count_ref, coef_ref):
    for part in range(2):
        store_coefs(part, gain_ref, (count_ref, other_count_ref), coef_ref)


def weighted_sums(part, mine_ref, other_ref, coef_ref, w_ref):
    lane = lax.broadcasted_iota(jnp.int32, (8, 128), 1)
    is_cos = lane < HARM
    is_wave = lane < 2 * HARM
    count = SUM_ROWS[part]

    def both(row):
        row = PART_AT[part] + row
        return mine_ref[row : row + 8] + other_ref[row : row + 8]

    def blocks(row):
        near, far = both(row), both(count + row)
        middle = jnp.where(lane < 48, pltpu.roll(near, 48, 1), pltpu.roll(far, 48, 1))
        return [jnp.where(is_wave, value, 0.0) for value in (near, middle, pltpu.roll(far, 96, 1))]

    def turn(sums):
        return jnp.where(is_cos, pltpu.roll(sums, 88, 1), -pltpu.roll(sums, HARM, 1))

    def harmonics_of(stem):
        found = {}
        for harmonic, _ in STEMS[part]:
            if harmonic == 0:
                plain, cos_1, sin_1 = stem[(0, 0)]
                found.update({(0, 0): plain, (1, 0): cos_1, (1, 1): sin_1})
                continue
            cos, sin = stem[(harmonic, 0)], stem[(harmonic, 1)]
            found[(harmonic, 0)], found[(harmonic, 1)] = cos[0], sin[0]
            found[(harmonic - 1, 0)] = cos[1] + sin[2]
            found[(harmonic - 1, 1)] = sin[1] - cos[2]
            found[(harmonic + 1, 0)] = cos[1] - sin[2]
            found[(harmonic + 1, 1)] = sin[1] + cos[2]
        return found

    def store(row, value):
        high, low = split_two(value)
        high = high.astype(F32)
        low = low.astype(F32)
        turned = pltpu.roll(high, 2 * HARM, 1)
        row = FORCE_AT[part] + row
        w_ref[row : row + 8, 0:128] = jnp.where(is_wave, high, turned)
        w_ref[row : row + 8, 128:256] = jnp.where(lane < 32, turned, pltpu.roll(low, 32, 1))

    by_block = [
        harmonics_of({stem: blocks(BASIS * i + 8 * x) for i, stem in enumerate(STEMS[part])}) for x in range(3)
    ]
    order = ORDERS[part]
    groups = {}
    for name in order:
        sums = [by_block[x][name] for x in range(3)]
        turned = [turn(value) for value in sums]
        groups[name] = swap(sums), turned, swap(turned)
    for i, (harmonic, sine) in enumerate(order):
        turned_s = groups[(harmonic, sine)][2]
        for x in range(3):
            row = BASIS * i + 8 * x
            coefs = [coef_ref[kind, FORCE_AT[part] + row : FORCE_AT[part] + row + 8] for kind in range(4)]
            value = coefs[0] * by_block[x][(harmonic, sine)] - coefs[1] * turned_s[x]
            if harmonic:
                sums_os, turned_o, _ = groups[(harmonic, 1 - sine)]
                value = value - coefs[2] * turned_o[x] - coefs[3] * sums_os[x]
            store(row, value)
    tails = [blocks(BASIS * len(STEMS[part]) + 8 * sine) for sine in range(2)]
    found = harmonics_of({(h, sine): [b[h % 8 : h % 8 + 1] for b in tails[sine]] for h, sine in STEMS[part]})
    index = lax.broadcasted_iota(jnp.int32, (8, 128), 0)
    kinds = []
    for sine in range(2):
        rows = jnp.zeros((8, 128), F32)
        for harmonic, kind in order:
            if kind == sine:
                rows = jnp.where(index == harmonic % 8, found[(harmonic, kind)], rows)
        kinds.append((rows, turn(rows)))
    at = BASIS * len(order)
    for sine in range(2):
        row = FORCE_AT[part] + at + 8 * sine
        store(at + 8 * sine, coef_ref[0, row : row + 8] * kinds[sine][0] - coef_ref[2, row : row + 8] * kinds[1 - sine][1])
    if at + 16 < FORCE_ROWS[part]:
        fill = FORCE_ROWS[part] - at - 16
        w_ref[FORCE_AT[part] + at + 16 : FORCE_AT[part] + FORCE_ROWS[part]] = jnp.zeros((fill, 256), F32)


def pull(weights, basis_ref, z_ref, count, begin, tile):
    lanes = slice(begin, begin + tile)
    plain = jnp.dot(weights, z_ref[:, begin : begin + tile], preferred_element_type=F32)
    sloped = jnp.dot(weights, z_ref[:, count + begin : count + begin + tile], preferred_element_type=F32)
    zero = jnp.zeros((8, tile), F32)
    even, slope, third = [zero] * 3, [zero] * 3, [zero] * 3
    sum_y = sum_z = zero
    for part in range(2):
        for place, (harmonic, sine) in enumerate(ORDERS[part]):
            at = 16 * (harmonic // 8) + 8 * sine + harmonic % 8
            basis = basis_ref[BASIS_Y + at : BASIS_Y + at + 1, lanes]
            basis_slope = basis_ref[SLOPE_Y + at : SLOPE_Y + at + 1, lanes]
            for i in range(3):
                row = FORCE_AT[part] + BASIS * place + 8 * i
                plain_rows, sloped_rows = plain[row : row + 8], sloped[row : row + 8]
                if harmonic == 0:
                    even[i] = even[i] + plain_rows
                    third[i] = third[i] + sloped_rows
                else:
                    even[i] = even[i] + basis * plain_rows
                    slope[i] = slope[i] + basis_slope * plain_rows
                    third[i] = third[i] + basis * sloped_rows
        for sine in range(2):
            row = FORCE_AT[part] + BASIS * len(ORDERS[part]) + 8 * sine
            at = 16 * part + 8 * sine
            sum_y = sum_y + basis_ref[SLOPE_Y + at : SLOPE_Y + at + 8, lanes] * plain[row : row + 8]
            sum_z = sum_z + basis_ref[BASIS_Y + at : BASIS_Y + at + 8, lanes] * sloped[row : row + 8]
    sum_x = zero
    for i in range(3):
        rows_x = basis_ref[8 * i : 8 * i + 8, lanes]
        sum_x = sum_x + basis_ref[SLOPE_X + 8 * i : SLOPE_X + 8 * i + 8, lanes] * even[i]
        sum_y = sum_y + rows_x * slope[i]
        sum_z = sum_z + rows_x * third[i]
    return [jnp.sum(value, axis=0, keepdims=True) for value in (sum_x, sum_y, sum_z)]


TILE = 256
COPIES = 4


def force_kernel(
    force_scale, half, mine_ref, other_ref, data_ref, basis_ref, z_ref, hot_ref, coef_ref,
    slot_ref, atom_ref, w_ref, atom_basis_ref, atom_z_ref,
):
    packs = hot_ref.shape[0] // 128
    lane = lax.broadcasted_iota(jnp.int32, (8, 128), 1)
    starts = [ARRIVE_AT + 8 * p for p in range(packs)]
    pool = jnp.concatenate([jnp.where(lane < 64, mine_ref[r : r + 8], other_ref[r : r + 8]) for r in starts], axis=1)
    found = jnp.dot(split_three(pool), hot_ref[...], preferred_element_type=F32)
    routed = ((found[0:8] + found[8:16]) + found[16:24])[0:4]
    for part in range(2):
        weighted_sums(part, mine_ref, other_ref, coef_ref, w_ref)
    weights = w_ref[...].astype(BF16)
    store_bases(routed, atom_basis_ref, atom_z_ref)
    charge = jnp.concatenate([data_ref[3:4, 0:half], data_ref[7:8, 0:half]], axis=1)
    jobs = ((basis_ref, z_ref, charge, slot_ref), (atom_basis_ref, atom_z_ref, routed[3:4], atom_ref))
    for rows_ref, table_ref, charges, out_ref in jobs:
        count = out_ref.shape[1]
        for begin in range(0, count, TILE):
            lanes = slice(begin, begin + TILE)
            gain = (-DOUBLE_PI * force_scale) * charges[:, lanes]
            gains = (gain, gain, gain / BOX_Z)
            found = pull(weights, rows_ref, table_ref, count, begin, TILE)
            out_ref[:, lanes] = jnp.concatenate([gains[i] * found[i] for i in range(3)], axis=0)


def params():
    return pltpu.CompilerParams(vmem_limit_bytes=VMEM_BYTES)


def stay(value):
    return pltpu.with_memory_space_constraint(value, pltpu.HBM)


def whole(count):
    return [pl.BlockSpec(memory_space=pltpu.VMEM)] * count


def body(coords, charges, counts, send_slot, recv_index, wave_ints):
    slots = charges.shape[0]
    half = slots // 2
    block = half + 128
    atoms_dev = recv_index.shape[0]
    devices = lax.axis_size(("blk", "row"))
    blk_count = lax.axis_size("blk")
    row_count = lax.axis_size("row")
    k_local = wave_ints.shape[1]
    cap = 2 * atoms_dev // devices
    packs = max(1, devices // 2 * cap // 64)
    per_pack = 64 // cap
    wave_rows, wave_width = wave_shape(k_local)
    force_scale = FORCE_GAIN / math.sqrt(float(atoms_dev * devices * blk_count * k_local))
    table_shape = jax.ShapeDtypeStruct((ARRIVE_AT + 8 * packs, 128), F32)
    count_shape = jax.ShapeDtypeStruct((8, 16 * COUNT_ROWS), F32)

    with jax.named_scope("payload"):
        own_ions = pl.pallas_call(
            prep_kernel,
            out_shape=jax.ShapeDtypeStruct((8, block), F32),
            in_specs=[pl.BlockSpec(memory_space=pltpu.HBM)] * 4,
            out_specs=whole(1)[0],
            scratch_shapes=[
                pltpu.VMEM(coords.shape, F32),
                pltpu.VMEM(charges.shape, F32),
                pltpu.SMEM(counts.shape, jnp.int32),
                pltpu.VMEM(send_slot.shape, jnp.int32),
                pltpu.SemaphoreType.DMA((4,)),
            ],
            compiler_params=params(),
        )(stay(coords), stay(charges), counts, stay(send_slot))

    def flip(value, blk_bit, row_bit):
        if not row_bit:
            return lax.ppermute(value, "blk", [(i, i ^ blk_bit) for i in range(blk_count)])
        if not blk_bit:
            return lax.ppermute(value, "row", [(i, i ^ row_bit) for i in range(row_count)])
        distance = row_count * blk_bit + row_bit
        return lax.ppermute(value, ("blk", "row"), [(i, i ^ distance) for i in range(devices)])

    def joined(values):
        return values[0] if len(values) == 1 else jnp.concatenate(values, axis=1)

    def accumulate(table, chunks, cost=1):
        plan = {
            "has_base": table is not None,
            "chunks": [chunk[1:] for chunk in chunks],
            "half": half,
            "cap": cap,
            "row_count": row_count,
        }
        args = [table] * plan["has_base"] + [chunk[0] for chunk in chunks]
        flops = int(cost * 2 * sum(chunk[1] for chunk in chunks) * slots * 256 * 720)
        with jax.named_scope("structure_sums"):
            return pl.pallas_call(
                functools.partial(sums_kernel, plan),
                out_shape=table_shape,
                in_specs=whole(len(args)),
                out_specs=whole(1)[0],
                scratch_shapes=[pltpu.VMEM((2 * sum(SUM_ROWS), 2 * slots), BF16)],
                compiler_params=params(),
                cost_estimate=pl.CostEstimate(flops=flops, bytes_accessed=1 << 20, transcendentals=0),
            )(*args)

    steps = []
    bit = row_count // 2
    while bit >= 2:
        steps.append((0, bit))
        bit //= 2
    bit = 4
    while bit < blk_count:
        steps.append((bit, 0))
        bit *= 2
    bits = [row_count * blk_bit + row_bit for blk_bit, row_bit in steps] + [2 * row_count, 1]
    table, counted = None, None
    ions, held, chunks = [own_ions], 1, [(own_ions, 1, 0)]
    for blk_bit, row_bit in steps:
        with jax.named_scope("exchange_ions"):
            got = flip(joined(ions), blk_bit, row_bit)
        if blk_bit:
            with jax.named_scope("exchange_counts"):
                counted = counted + flip(counted, blk_bit, 0)
        if counted is None:
            with jax.named_scope("counts"):
                counted = pl.pallas_call(
                    functools.partial(count_kernel, wave_rows, wave_width),
                    out_shape=count_shape,
                    in_specs=[pl.BlockSpec(memory_space=pltpu.HBM)],
                    out_specs=whole(1)[0],
                    scratch_shapes=[
                        pltpu.VMEM(wave_ints.shape, jnp.int32),
                        pltpu.VMEM((wave_rows, 3 * wave_width), F32),
                        pltpu.SemaphoreType.DMA((COPIES,)),
                    ],
                    compiler_params=params(),
                    cost_estimate=pl.CostEstimate(
                        flops=2 * k_local * COUNT_ROWS * 128, bytes_accessed=1 << 20, transcendentals=0
                    ),
                )(stay(wave_ints))
            got, counted = lax.optimization_barrier((got, counted))
        else:
            table, chunks = accumulate(table, chunks), []
            got, table = lax.optimization_barrier((got, table))
        chunks = chunks + [(got, held, held)]
        ions = ions + [got]
        held *= 2
    with jax.named_scope("exchange_ions"):
        sent = joined(ions)
        across = flip(jnp.concatenate([sent, counted], axis=1), 2, 0)
        along = flip(sent, 0, 1)
        corner = flip(sent, 2, 1)
    table = accumulate(table, chunks)
    own_ions, recv_index, table = lax.optimization_barrier((own_ions, recv_index, table))
    with jax.named_scope("own_ions"):
        basis, table_z, hot, gain = pl.pallas_call(
            functools.partial(own_kernel, half, cap, row_count, bits),
            out_shape=(
                jax.ShapeDtypeStruct((BASIS_ROWS, slots), F32),
                jax.ShapeDtypeStruct((256, 2 * slots), BF16),
                jax.ShapeDtypeStruct((128 * packs, atoms_dev), BF16),
                jax.ShapeDtypeStruct((COUNT_ROWS, 128), F32),
            ),
            in_specs=whole(2),
            out_specs=tuple(whole(4)),
            compiler_params=params(),
            cost_estimate=pl.CostEstimate(flops=1<<22, bytes_accessed=1 << 20, transcendentals=0),
        )(own_ions, recv_index)
    along, table, basis, table_z, hot, gain = lax.optimization_barrier((along, table, basis, table_z, hot, gain))
    table = accumulate(table, [(along, held, 2 * held)], cost=0.05)
    table = accumulate(table, [(across, held, held)], cost=0.05)
    with jax.named_scope("exchange_core"):
        counted = counted + across[:, held * block :]
        other_counted = flip(counted, 1, 0)
    corner, table, counted = lax.optimization_barrier((corner, table, counted))
    table = accumulate(table, [(corner, held, 3 * held)], cost=16)
    with jax.named_scope("exchange_core"):
        other = flip(table, 1, 0)
    with jax.named_scope("coefficients"):
        coefs = pl.pallas_call(
            coef_kernel,
            out_shape=jax.ShapeDtypeStruct((4, sum(FORCE_ROWS), 128), F32),
            in_specs=whole(3),
            out_specs=whole(1)[0],
            compiler_params=params(),
            cost_estimate=pl.CostEstimate(flops=1<<33, bytes_accessed=1 << 20, transcendentals=0),
        )(gain, counted, other_counted)
    with jax.named_scope("forces"):
        return pl.pallas_call(
            functools.partial(force_kernel, force_scale, half),
            out_shape=(
                jax.ShapeDtypeStruct((3, slots), F32),
                jax.ShapeDtypeStruct((3, atoms_dev), F32),
            ),
            in_specs=whole(7),
            out_specs=tuple(whole(2)),
            scratch_shapes=[
                pltpu.VMEM((sum(FORCE_ROWS), 256), F32),
                pltpu.VMEM((BASIS_ROWS, atoms_dev), F32),
                pltpu.VMEM((256, 2 * atoms_dev), BF16),
            ],
            compiler_params=params(),
        )(table, other, own_ions, basis, table_z, hot, coefs)


def solution(mesh):
    placed = (
        P(None, ("groups", "blk", "row")),
        P(("groups", "blk", "row")),
        P(("groups", "blk", "row")),
        P(("groups", "blk", "row")),
        P(("groups", "blk", "row")),
        P(None, "blk"),
    )
    return jax.shard_map(
        body,
        mesh=mesh,
        in_specs=placed,
        out_specs=(P(None, ("groups", "blk", "row")), P(None, ("groups", "blk", "row"))),
        check_vma=False,
    )
```
